32 devices in a mesh: fine: 16 (over z, y, x), coarse: 2 (over core).
Axes of the slice: x: 2, y: 2, z: 4, core: 2. Of those that a mesh axis runs over, the one named last changes fastest.
Arguments:
- load_cases: bfloat16 [32, 16, 1024], P(('fine', 'coarse')), may hold values from -6 to 6
- dual_ops: bfloat16 [32, 1024, 1024], P(('fine', 'coarse')), as said below
- coarse_basis: bfloat16 [32, 48, 1024], P(('fine', 'coarse')), may hold values from -0.4375 to 0.4375
- factor_blocks: float32 [32, 4, 48, 48], P(('fine', 'coarse')), may hold values from -0.4375 to 0.4375
- pattern: int32 [32, 4], P(('fine', 'coarse')), may hold values from 0 to 31
- partners: int32 [32, 6], P(('fine', 'coarse')), may hold values from 0 to 15, as said below
- row_counts: int32 [32, 8], P(('fine', 'coarse')), may hold values from 0 to 128, as said below
Outputs:
- multipliers: float32 [32, 16, 1024], P(('fine', 'coarse'))
- residual: float32 [32, 16, 1024], P(('fine', 'coarse'))
The draws below stay inside these ranges and needn't reach their ends.
Inputs may be any that keep to these rules, and one draw needn't show every extreme that they name: Each layer gives each in-layer block index b its own odd distance d_b, the distances being 1, 3, up to 11 in some order: the subdomain at an even in-layer index i faces (i + d_b) modulo the number of in-layer indices, one at an odd index faces (i - d_b) modulo that number. So the partner of a subdomain's partner is itself, and a subdomain's 6 partners are distinct and differ from itself. `row_counts`: facing blocks have equal counts; blocks 6 of the first layer and 7 of the last layer are 0. `dual_ops`: each subdomain's matrix is symmetric positive definite.
All inputs are finite; a program needn't handle non-finite values.
Results may differ from the reference program's by a relative error of at most 0.0041.
Values may be sent and summed in bfloat16 or wider, within the bound.
No kernel may reach another device: no remote copies, remote signals or barrier semaphores. Data moves between devices by JAX's collectives and lax.ppermute only.
A program may use at most 64 MiB of HBM per device.

```python
import math
import jax
import jax.numpy as jnp
from jax import lax

BLOCK = 128
PLANES = 6
M = 1024
MODES = 48
NP = 4
LOADS = 16
ITERS = 2
SUBS = 32
N_FINE = 16
N_COARSE = 2


def pair_table(key):
    base_key = jax.random.fold_in(key, 11)

    def one_layer(layer_key):
        order = jax.random.permutation(jax.random.fold_in(layer_key, 1), PLANES).astype(jnp.int32)
        distance = 2 * order + 1
        teams = jnp.arange(N_FINE, dtype=jnp.int32)
        even_side = teams % 2 == 0
        mates = jnp.where(even_side[:, None], teams[:, None] + distance[None, :], teams[:, None] - distance[None, :])
        return (mates % N_FINE).astype(jnp.int32)
    layer_keys = jax.vmap(lambda index: jax.random.fold_in(base_key, index))(jnp.arange(N_COARSE, dtype=jnp.int32))
    tables = jax.vmap(one_layer)(layer_keys)
    return jnp.transpose(tables, (1, 0, 2)).reshape(SUBS, PLANES)


def draw_partners(key, part):
    return pair_table(key)


def draw_row_counts(key, part):
    partner_tab = pair_table(key)
    subdomain = jnp.arange(SUBS, dtype=jnp.int32)
    layer_index = subdomain % N_COARSE
    partner_sub = partner_tab * N_COARSE + layer_index[:, None]
    base_values = jax.random.randint(jax.random.fold_in(key, 12), (SUBS, PLANES), 0, BLOCK + 1)
    mate_values = base_values[partner_sub, jnp.arange(PLANES, dtype=jnp.int32)[None, :]]
    in_plane = (base_values + mate_values) % (BLOCK + 1)
    in_plane = in_plane.at[0, 0].set(BLOCK)
    in_plane = in_plane.at[partner_sub[0, 0], 0].set(BLOCK)
    upward = jax.random.randint(jax.random.fold_in(key, 13), (SUBS,), 1, BLOCK + 1)
    upward = upward.at[0].set(BLOCK)
    upward = jnp.where(layer_index == N_COARSE - 1, 0, upward)
    downward = jnp.concatenate([jnp.zeros((1,), upward.dtype), upward[:-1]])
    return jnp.concatenate([in_plane, downward[:, None], upward[:, None]], axis=1).astype(jnp.int32)


def draw_dual_ops(key, part):
    spread = 0.7 * math.sqrt(3.0 / (2.0 * M))

    def one_matrix(index):
        sub_key = jax.random.fold_in(key, index)
        diagonal = jax.random.uniform(jax.random.fold_in(sub_key, 1), (M,), jnp.float32, 2.0, 4.0)
        noise = jax.random.uniform(jax.random.fold_in(sub_key, 2), (M, M), jnp.float32, -spread, spread)
        return (jnp.diag(diagonal) + noise + noise.T).astype(jnp.bfloat16)
    return lax.map(one_matrix, jnp.arange(SUBS, dtype=jnp.int32))


def with_ends(values, stream_key, low, top_value):
    spot = [jax.random.randint(jax.random.fold_in(stream_key, axis), (), 0, length) for axis, length in enumerate(values.shape)]
    main_axis = values.shape.index(max(values.shape))
    beside = spot[:main_axis] + [(spot[main_axis] + 1) % values.shape[main_axis]] + spot[main_axis + 1:]
    return values.at[tuple(spot)].set(low).at[tuple(beside)].set(top_value)


def level_of(rng, extent, pieces, low, top_value):
    loudness = 1.0
    for position, parts in pieces:
        draws = jax.random.uniform(jax.random.fold_in(jax.random.fold_in(rng, 6), position), (parts,), jnp.float32, low / len(pieces), top_value / len(pieces))
        loudness = loudness * jnp.repeat(jnp.exp(draws), extent[position] // parts).reshape((-1,) + (1,) * (len(extent) - 1 - position))
    return loudness


def gaussian(rng, extent, scale, reach, shards=(), kind=jnp.bfloat16):
    factor_of = level_of(rng, extent, shards, -0.22, 0.18) if shards else 1.0
    values = jax.random.normal(rng, extent, jnp.float32) * scale * factor_of
    return jnp.minimum(jnp.maximum(values, -reach), reach).astype(kind)


def setup_inputs(seed: int = 0) -> dict:
    arg_keys = jax.random.split(jax.random.key(seed), 8)
    return {
        "load_cases": gaussian(arg_keys[0], (SUBS, LOADS, M), 1.0, 6.0, ((0, 32),)),
        "dual_ops": draw_dual_ops(jax.random.fold_in(arg_keys[7], 71), 0),
        "coarse_basis": gaussian(arg_keys[2], (SUBS, MODES, M), (4 * MODES) ** -0.5, 0.4375, ((0, 32),)),
        "factor_blocks": gaussian(arg_keys[3], (SUBS, NP, MODES, MODES), (MODES * NP) ** -0.5, 0.4375, ((0, 32),), jnp.float32),
        "pattern": with_ends(jax.random.randint(arg_keys[4], (SUBS, NP), 0, SUBS), jax.random.fold_in(arg_keys[4], 1), 0, SUBS - 1).astype(jnp.int32),
        "partners": draw_partners(jax.random.fold_in(arg_keys[7], 71), 0),
        "row_counts": draw_row_counts(jax.random.fold_in(arg_keys[7], 71), 0),
    }


def make_signs(partners, row_counts):
    subdomain = jnp.arange(SUBS, dtype=jnp.int32)
    fine_index = subdomain // N_COARSE
    plane_signs = jnp.where(fine_index[:, None] < partners, 1.0, -1.0)
    layer_signs = jnp.broadcast_to(jnp.array([-1.0, 1.0], jnp.float32), (SUBS, 2))
    block_signs = jnp.concatenate([plane_signs, layer_signs], axis=1).astype(jnp.float32)
    signs = jnp.repeat(block_signs, BLOCK, axis=1)
    live = (jnp.arange(BLOCK, dtype=jnp.int32)[None, None, :] < row_counts[:, :, None]).astype(jnp.float32)
    return signs[:, None, :], live.reshape(SUBS, 1, M)


def assemble(values, partners, live):
    blocked = values.astype(jnp.float32).reshape(SUBS, LOADS, PLANES + 2, BLOCK)
    subdomain = jnp.arange(SUBS, dtype=jnp.int32)
    layer_index = subdomain % N_COARSE
    partner_sub = partners * N_COARSE + layer_index[:, None]
    plane_index = jnp.arange(PLANES, dtype=jnp.int32)[None, :]
    facing = blocked[partner_sub, :, plane_index, :]
    facing = jnp.transpose(facing, (0, 2, 1, 3))
    lower = jnp.roll(blocked[:, :, PLANES + 1, :], 1, axis=0)
    lower = jnp.where((layer_index == 0)[:, None, None], 0.0, lower)
    upper = jnp.roll(blocked[:, :, PLANES, :], -1, axis=0)
    upper = jnp.where((layer_index == N_COARSE - 1)[:, None, None], 0.0, upper)
    opposite = jnp.concatenate([facing, lower[:, :, None, :], upper[:, :, None, :]], axis=2)
    return live * (blocked + opposite).reshape(SUBS, LOADS, M)


def reference(load_cases, dual_ops, coarse_basis, factor_blocks, pattern, partners, row_counts):
    signs, live = make_signs(partners, row_counts)
    basis_full = coarse_basis.astype(jnp.float32)
    residual = assemble((signs * load_cases.astype(jnp.float32)).astype(jnp.bfloat16), partners, live)
    multipliers = jnp.zeros((SUBS, LOADS, M), jnp.float32)
    for iteration in range(ITERS):
        restricted = jnp.einsum('slm,sqm->slq', signs * residual, basis_full, precision=lax.Precision.HIGHEST)
        picked = restricted[pattern]
        coarse_sol = jnp.einsum('spla,spab->slb', picked, factor_blocks, precision=lax.Precision.HIGHEST)
        coarse_half = lax.optimization_barrier(coarse_sol.astype(jnp.bfloat16))
        spread_back = jnp.einsum('sla,sam->slm', coarse_half.astype(jnp.float32), basis_full, precision=lax.Precision.HIGHEST)
        correction = (signs * spread_back).astype(jnp.bfloat16)
        direction = residual + assemble(correction, partners, live)
        scaled = (signs * direction).astype(jnp.bfloat16)

        def apply_one(pair):
            return jnp.dot(pair[0], pair[1], preferred_element_type=jnp.float32)

        product = lax.map(apply_one, (scaled, dual_ops))
        applied = (signs * product).astype(jnp.bfloat16)
        image = assemble(applied, partners, live)
        gamma = jnp.sum(residual * direction, axis=(0, 2))
        delta = jnp.sum(direction * image, axis=(0, 2))
        step_size = (gamma / delta)[None, :, None]
        multipliers = multipliers + step_size * direction
        residual = residual - step_size * image
    return multipliers, residual
```

```python
import jax
import jax.numpy as jnp
from jax import lax
from jax.sharding import PartitionSpec as P

PLANES = 6
ITERS = 2
AXES = ("fine", "coarse")
HIGHEST = lax.Precision.HIGHEST


def body(load_cases, dual_ops, coarse_basis, factor_blocks, pattern, partners, row_counts):
    cases, width = load_cases.shape[1:]
    blocks = PLANES + 2
    block_rows = width // blocks
    modes = coarse_basis.shape[1]
    terms = factor_blocks.shape[1]
    fine_count = lax.axis_size("fine")
    coarse_count = lax.axis_size("coarse")
    subs = fine_count * coarse_count
    fine_index = lax.axis_index("fine")
    coarse_index = lax.axis_index("coarse")
    me = fine_index * coarse_count + coarse_index

    partner_row = partners[0]
    below = jnp.where(coarse_index > 0, me - 1, -1)
    above = jnp.where(coarse_index < coarse_count - 1, me + 1, -1)
    facing = jnp.concatenate([partner_row * coarse_count + coarse_index, jnp.stack([below, above])])
    everyone = jnp.arange(subs, dtype=jnp.int32)
    chosen = facing[:, None] == everyone[None, :]
    selector = chosen.astype(jnp.bfloat16)

    plane_signs = jnp.where(fine_index < partner_row, 1.0, -1.0).astype(jnp.float32)
    block_signs = jnp.concatenate([plane_signs, jnp.array([-1.0, 1.0], jnp.float32)])
    signs = jnp.repeat(block_signs, block_rows)[None, :]
    live = (
        (jnp.arange(block_rows, dtype=jnp.int32)[None, :] < row_counts[0][:, None])
        .astype(jnp.float32)
        .reshape(1, width)
    )
    basis = coarse_basis[0]

    def by_block(values):
        return jnp.transpose(values.reshape(values.shape[0], blocks, block_rows), (1, 0, 2))

    def exchange(per_block):
        rows = per_block.shape[1]
        flat = per_block.reshape(blocks, rows * block_rows)
        out = jnp.dot(selector.T, flat, preferred_element_type=jnp.float32).astype(jnp.bfloat16)
        out = out.reshape(subs, rows, block_rows)
        arrived = lax.all_to_all(out, AXES, 0, 0, tiled=True).reshape(subs, rows * block_rows)
        back = jnp.dot(selector, arrived, preferred_element_type=jnp.float32).astype(jnp.bfloat16)
        return back.reshape(blocks, rows, block_rows)

    def to_rows(per_block):
        return jnp.transpose(per_block, (1, 0, 2)).reshape(per_block.shape[1], width)

    def gather(values):
        copies = jnp.broadcast_to(values[None], (subs,) + values.shape)
        return lax.all_to_all(copies, AXES, 0, 0, tiled=True)

    flat_factors = factor_blocks[0].reshape(-1, block_rows)
    pattern_rows = jnp.zeros((8, block_rows), jnp.float32)
    pattern_rows = pattern_rows.at[0, :terms].set(pattern[0].astype(jnp.float32))
    packed = jnp.concatenate([flat_factors, pattern_rows], axis=0)
    packed_all = lax.all_gather(packed, AXES, axis=0, tiled=False)
    who = jnp.concatenate([me[None], jnp.maximum(facing, 0)])
    packed_near = packed_all[who]
    factor_rows = flat_factors.shape[0]
    near_factors = packed_near[:, :factor_rows].reshape(blocks + 1, terms * modes, modes)
    near_pattern = packed_near[:, factor_rows, :terms].astype(jnp.int32)

    loads = load_cases[0]
    received = exchange(jnp.concatenate([by_block(loads), by_block(basis)], axis=1))
    facing_basis = received[:, cases:]
    near_basis = jnp.concatenate([basis[None, :, :block_rows], facing_basis], axis=0)[1:]
    residual = live * (loads.astype(jnp.float32) - to_rows(received[:, :cases]).astype(jnp.float32))

    def restrict(values):
        return lax.dot_general(
            values, basis.astype(jnp.float32), (((1,), (1,)), ((), ())), precision=HIGHEST
        )

    def coarse_direction(residual, restricted):
        picked = jnp.transpose(restricted[near_pattern], (0, 2, 1, 3))
        picked = picked.reshape(blocks + 1, cases, terms * modes)
        solved = jnp.einsum("jlk,jkb->jlb", picked, near_factors, precision=HIGHEST)
        solved = solved.astype(jnp.bfloat16)
        mine = jnp.dot(solved[0], basis, preferred_element_type=jnp.float32).astype(jnp.bfloat16)
        theirs = jnp.einsum(
            "jla,jam->jlm", solved[1:], near_basis, preferred_element_type=jnp.float32
        ).astype(jnp.bfloat16)
        return residual + live * (mine.astype(jnp.float32) - to_rows(theirs).astype(jnp.float32))

    def apply_dual(direction):
        return jnp.dot(
            direction.astype(jnp.bfloat16), dual_ops[0], preferred_element_type=jnp.float32
        ).astype(jnp.bfloat16)

    def image_of(applied):
        other = to_rows(exchange(by_block(applied)))
        return live * (applied.astype(jnp.float32) - other.astype(jnp.float32))

    def partial_sums(residual, direction, applied):
        gamma = jnp.sum(residual * direction, axis=1)
        delta = 2.0 * jnp.sum(direction * applied.astype(jnp.float32), axis=1)
        return jnp.stack([gamma, delta], axis=1)

    multipliers = jnp.zeros_like(residual)
    restricted = gather(restrict(residual))
    for iteration in range(ITERS):
        direction = coarse_direction(residual, restricted)
        applied = apply_dual(direction)
        sums = partial_sums(residual, direction, applied)
        image = image_of(applied)
        if iteration + 1 < ITERS:
            message = jnp.concatenate([restrict(image), sums], axis=1)
        else:
            message = sums
        collected = gather(message)
        totals = jnp.sum(collected[:, :, -2:], axis=0)
        step = (totals[:, 0] / totals[:, 1])[:, None]
        multipliers = multipliers + step * direction
        residual = residual - step * image
        if iteration + 1 < ITERS:
            restricted = restricted - step[None] * collected[:, :, :modes]
    return ((signs * multipliers)[None], (signs * residual)[None])


def solution(mesh):
    rows = P(AXES, None, None)
    return jax.shard_map(
        body,
        mesh=mesh,
        in_specs=(rows, rows, rows, P(AXES, None, None, None), P(AXES, None), P(AXES, None), P(AXES, None)),
        out_specs=(rows, rows),
        check_vma=False,
    )
```

```python
import functools

import jax
import jax.numpy as jnp
from jax import lax
from jax.experimental import pallas as pl
from jax.experimental.pallas import tpu as pltpu
from jax.sharding import PartitionSpec as P

PLANES = 6
AXES = ("fine", "coarse")
LANES = 128
HALF = 64
BF16 = jnp.bfloat16
F32 = jnp.float32
GAMMA = 48
DELTA = 49


def lane_ids(rows):
    return lax.broadcasted_iota(jnp.int32, (rows, LANES), 1)


def dot(a, b):
    return lax.dot_general(a, b, (((1,), (0,)), ((), ())), preferred_element_type=F32)


def facing_subs(sizes, partners_ref):
    fine_count, coarse_count = sizes
    fine = lax.axis_index("fine")
    coarse = lax.axis_index("coarse")
    me = fine * coarse_count + coarse
    subs = [partners_ref[0, b] * coarse_count + coarse for b in range(PLANES)]
    subs.append(jnp.where(coarse > 0, me - 1, me))
    subs.append(jnp.where(coarse < coarse_count - 1, me + 1, me))
    return subs


def slot_of(sizes, partner):
    fine_count = sizes[0]
    fine = lax.axis_index("fine")
    ahead = jnp.where(fine % 2 == 0, partner - fine, fine - partner)
    ahead = jnp.where(ahead < 0, ahead + fine_count, ahead)
    return (ahead - 1) // 2


def live_mask(counts_ref, block):
    return (lane_ids(1) < counts_ref[0, block]).astype(F32)


def post_blocks(out_ref, targets, rows):
    cases = rows.shape[0]
    for block, target in enumerate(targets):
        out_ref[target, :cases, :] = rows[:, block * LANES : (block + 1) * LANES]


def send_kernel(sizes, partners_ref, loads_ref, out_ref):
    out_ref[...] = jnp.zeros_like(out_ref)
    post_blocks(out_ref, facing_subs(sizes, partners_ref), loads_ref[0])


def pack_kernel(sizes, partners_ref, pattern_ref, factors_ref, basis_ref, *outs):
    terms, modes = factors_ref.shape[1:3]
    gap = jnp.zeros((modes, HALF - modes), F32)
    parts = []
    for term in range(terms):
        whole = factors_ref[0, term]
        high = whole.astype(BF16).astype(F32)
        parts.append(jnp.concatenate([high, gap, whole - high, gap], axis=1))
    factors = jnp.concatenate(parts, axis=0).astype(BF16)
    row = lax.broadcasted_iota(jnp.int32, (16, LANES), 0)
    ids = jnp.zeros((16, LANES), F32)
    for term in range(terms):
        sub = pattern_ref[0, term]
        ids = jnp.where(row == term, (sub // 16).astype(F32), ids)
        ids = jnp.where(row == 8 + term, (sub % 16).astype(F32), ids)
    ids = ids.astype(BF16)
    slots = [slot_of(sizes, partners_ref[0, b]) for b in range(PLANES)]
    wanted = []
    for slot in range(PLANES):
        wanted.append(sum(jnp.where(slots[b] == slot, b, 0) for b in range(PLANES)))
    if len(outs) == PLANES + 1:
        wanted.append(jnp.where(lax.axis_index("coarse") == 0, PLANES + 1, PLANES))
    else:
        wanted += [PLANES, PLANES + 1]
    depth = terms * modes
    for out_ref, block in zip(outs, wanted):
        out_ref[:depth, :] = factors
        start = block * LANES
        if not isinstance(start, int):
            start = pl.multiple_of(start, LANES)
        out_ref[depth : depth + modes, :] = basis_ref[0, :, pl.ds(start, LANES)]
        out_ref[depth + modes :, :] = ids


def difference(sizes, partners_ref, counts_ref, mine, arrived_ref):
    targets = facing_subs(sizes, partners_ref)
    cases = mine.shape[0]
    result, ours, theirs = [], [], []
    for block, target in enumerate(targets):
        mask = live_mask(counts_ref, block)
        left = mine[:, block * LANES : (block + 1) * LANES].astype(F32) * mask
        right = arrived_ref[target, :cases, :].astype(F32) * mask
        result.append(left - right)
        ours.append(left.astype(BF16))
        theirs.append(right.astype(BF16))
    return result, ours, theirs


def restrict_kernel(sizes, partners_ref, counts_ref, mine_ref, arrived_ref, basis_ref, sums_ref, out_ref, message_ref):
    modes = basis_ref.shape[1]
    mine = mine_ref[...].reshape(mine_ref.shape[-2:])
    cases = mine.shape[0]
    result, ours, theirs = difference(sizes, partners_ref, counts_ref, mine, arrived_ref)
    for block, values in enumerate(result):
        out_ref[:, block * LANES : (block + 1) * LANES] = values
    both = jnp.concatenate([jnp.concatenate(ours, axis=1), jnp.concatenate(theirs, axis=1)], axis=0)
    basis = basis_ref[0]
    gap = jnp.zeros((HALF - modes, basis.shape[1]), BF16)
    twice = jnp.concatenate([basis, gap, basis, gap], axis=0)
    coefficients = lax.dot_general(both, twice, (((1,), (1,)), ((), ())), preferred_element_type=F32)
    coefficients = coefficients[:cases] - coefficients[cases:]
    half = cases // 2
    message = jnp.where(lane_ids(half) < HALF, coefficients[:half], coefficients[half:])
    if sums_ref is not None:
        message = message + sums_ref[...]
    message_ref[...] = jnp.broadcast_to(message[None], message_ref.shape)


def solve(coeffs, near, terms, modes):
    half = 8
    depth = terms * modes
    high = coeffs.astype(BF16)
    low = (coeffs - high.astype(F32)).astype(BF16)
    table = jnp.concatenate([high, low], axis=1)
    chunks = coeffs.shape[0] // LANES
    lanes = lane_ids(half).astype(F32)
    step = lax.broadcasted_iota(jnp.int32, (half, LANES), 0).astype(F32)
    picks = []
    for packed in near:
        ids = packed[depth + modes :, :].astype(F32)
        ids = (ids[:8] * 16.0 + ids[8:]) * float(half)
        for term in range(terms):
            target = ids[term : term + 1] + step
            picks.append(
                jnp.concatenate([(target == lanes + float(LANES * c)).astype(F32) for c in range(chunks)], axis=1)
            )
    picks = jnp.concatenate(picks, axis=0).astype(BF16)
    picked = dot(picks, table)
    left = lane_ids(half) < HALF
    gap = jnp.zeros((HALF - modes, LANES), BF16)
    solutions = []
    for index, packed in enumerate(near):
        sides = []
        for part in range(2):
            columns = []
            for pair in range(0, terms, 2):
                first, second = [
                    picked[(index * terms + term) * half : (index * terms + term + 1) * half, part * LANES : (part + 1) * LANES]
                    for term in (pair, pair + 1)
                ]
                top = jnp.where(left, first, pltpu.roll(second, HALF, 1))
                bottom = jnp.where(left, pltpu.roll(first, HALF, 1), second)
                columns.append(jnp.concatenate([top, bottom], axis=0))
            sides.append(jnp.concatenate(columns, axis=1))
        rows = jnp.concatenate(sides, axis=0).astype(BF16)
        factors = []
        for term in range(terms):
            factors += [packed[term * modes : (term + 1) * modes, :], gap]
        product = dot(rows, jnp.concatenate(factors, axis=0))
        product = product[: 2 * half] + product[2 * half :]
        product = product + pltpu.roll(product, HALF, 1)
        solutions.append(product[:, :modes].astype(BF16))
    return solutions


def advance(sizes, dims, partners_ref, counts_ref, coeffs, residual, near_refs, basis_ref, dual_ref, theirs_ref,
            direction_ref, applied_ref):
    terms, modes = dims
    depth = terms * modes
    near = [ref[...] for ref in near_refs]
    solutions = solve(coeffs, near, terms, modes)
    mine = dot(solutions[0], basis_ref[0]).astype(BF16).astype(F32)
    for index, packed in enumerate(near[1:]):
        theirs_ref[index] = dot(solutions[index + 1], packed[depth : depth + modes, :]).astype(BF16).astype(F32)
    pieces = []
    for block in range(PLANES + 2):
        if block < PLANES:
            place = slot_of(sizes, partners_ref[0, block])
        else:
            place = min(block, len(near) - 2)
        span = slice(block * LANES, (block + 1) * LANES)
        pieces.append(residual[:, span] + live_mask(counts_ref, block) * (mine[:, span] - theirs_ref[place]))
    direction = jnp.concatenate(pieces, axis=1)
    direction_ref[...] = direction
    applied = dot(direction.astype(BF16), dual_ref[0]).astype(BF16)
    applied_ref[...] = applied
    gamma = jnp.sum(residual * direction, axis=1, keepdims=True)
    delta = 2.0 * jnp.sum(direction * applied.astype(F32), axis=1, keepdims=True)
    half = gamma.shape[0] // 2
    lanes = lane_ids(half)
    sums = jnp.zeros((half, LANES), F32)
    for lane, values in ((GAMMA, gamma), (DELTA, delta)):
        sums = jnp.where(lanes == lane, values[:half], sums)
        sums = jnp.where(lanes == HALF + lane, values[half:], sums)
    return applied, sums


def first_kernel(sizes, dims, count, partners_ref, counts_ref, coeffs_ref, residual_ref, basis_ref, dual_ref, *refs):
    near_refs = refs[:count]
    message_ref, direction_ref, applied_ref, sums_ref, theirs_ref = refs[count:]
    applied, sums = advance(
        sizes, dims, partners_ref, counts_ref, coeffs_ref[...], residual_ref[...], near_refs, basis_ref, dual_ref,
        theirs_ref, direction_ref, applied_ref,
    )
    message_ref[...] = jnp.zeros_like(message_ref)
    post_blocks(message_ref, facing_subs(sizes, partners_ref), applied)
    sums_ref[...] = sums


def steps_from(totals):
    low = totals[:, GAMMA : GAMMA + 1] / totals[:, DELTA : DELTA + 1]
    high = totals[:, HALF + GAMMA : HALF + GAMMA + 1] / totals[:, HALF + DELTA : HALF + DELTA + 1]
    return low, high


def second_kernel(sizes, dims, count, partners_ref, counts_ref, coeffs_ref, change_ref, residual_ref, image_ref,
                  before_ref, basis_ref, dual_ref, *refs):
    near_refs = refs[:count]
    message_ref, residual_out, multipliers_out, direction_ref, applied_ref, theirs_ref = refs[count:]
    half = residual_ref.shape[0] // 2
    change = change_ref[...].reshape(-1, half, LANES)
    low, high = steps_from(jnp.sum(change, axis=0))
    step = jnp.concatenate([low, high], axis=0)
    packed_step = jnp.where(lane_ids(half) < HALF, low, high)
    coeffs = coeffs_ref[...] - (change * packed_step[None]).reshape(coeffs_ref.shape)
    residual = residual_ref[...] - step * image_ref[...]
    residual_out[...] = residual
    multipliers_out[...] = step * before_ref[...]
    applied, sums = advance(
        sizes, dims, partners_ref, counts_ref, coeffs, residual, near_refs, basis_ref, dual_ref, theirs_ref,
        direction_ref, applied_ref,
    )
    top = sums.astype(BF16).astype(F32)
    middle = (sums - top).astype(BF16).astype(F32)
    bottom = sums - top - middle
    coded = (top + pltpu.roll(middle, 2, 1) + pltpu.roll(bottom, 4, 1)).astype(BF16)
    cases = applied.shape[0]
    message_ref[:, :cases, :] = jnp.zeros((message_ref.shape[0], cases, LANES), BF16)
    message_ref[:, cases:, :] = jnp.broadcast_to(coded[None], (message_ref.shape[0], half, LANES))
    post_blocks(message_ref, facing_subs(sizes, partners_ref), applied)


def last_kernel(sizes, partners_ref, counts_ref, arrived_ref, applied_ref, residual_ref, multipliers_ref, direction_ref,
                multipliers_out, residual_out):
    cases = applied_ref.shape[0]
    totals = jnp.sum(arrived_ref[:, cases:, :].astype(F32), axis=0)
    totals = totals + pltpu.roll(totals, LANES - 2, 1) + pltpu.roll(totals, LANES - 4, 1)
    step = jnp.concatenate(steps_from(totals), axis=0)
    image, _, _ = difference(sizes, partners_ref, counts_ref, applied_ref[...], arrived_ref)
    fine = lax.axis_index("fine")
    for block in range(PLANES + 2):
        span = slice(block * LANES, (block + 1) * LANES)
        if block < PLANES:
            sign = jnp.where(fine < partners_ref[0, block], 1.0, -1.0).astype(F32)
        else:
            sign = -1.0 if block == PLANES else 1.0
        multipliers_out[0, :, span] = sign * (multipliers_ref[:, span] + step * direction_ref[:, span])
        residual_out[0, :, span] = sign * (residual_ref[:, span] - step * image[block])


SMEM = pl.BlockSpec(memory_space=pltpu.SMEM)
VMEM = pl.BlockSpec(memory_space=pltpu.VMEM)


def call(kernel, name, scalars, arrays, outs, scratch=()):
    return pl.pallas_call(
        kernel,
        name=name,
        out_shape=[jax.ShapeDtypeStruct(shape, dtype) for shape, dtype in outs],
        in_specs=[SMEM] * len(scalars) + [VMEM] * len(arrays),
        out_specs=[VMEM] * len(outs),
        scratch_shapes=list(scratch),
        compiler_params=pltpu.CompilerParams(vmem_limit_bytes=40 * 1024 * 1024),
    )(*scalars, *arrays)


def body(load_cases, dual_ops, coarse_basis, factor_blocks, pattern, partners, row_counts):
    cases, width = load_cases.shape[1:]
    terms, modes = factor_blocks.shape[1:3]
    fine_count = lax.axis_size("fine")
    coarse_count = lax.axis_size("coarse")
    subs = fine_count * coarse_count
    sizes = (fine_count, coarse_count)
    dims = (terms, modes)
    half = cases // 2

    def swap_all(message):
        return lax.all_to_all(message, AXES, 0, 0, tiled=True)

    [message] = call(
        functools.partial(send_kernel, sizes), "send_loads", (partners,), (load_cases,), [((subs, cases, LANES), BF16)]
    )
    arrived = swap_all(message)

    layers = 1 if coarse_count == 2 else 2
    packed = call(
        functools.partial(pack_kernel, sizes),
        "pack_factors",
        (partners, pattern),
        (factor_blocks, coarse_basis),
        [((terms * modes + modes + 16, LANES), BF16)] * (PLANES + layers),
    )
    near = [packed[-1]]
    for slot in range(PLANES):
        distance = 2 * slot + 1
        pairs = [(i, (i + distance if i % 2 == 0 else i - distance) % fine_count) for i in range(fine_count)]
        near.append(lax.ppermute(packed[slot], "fine", pairs))
    if layers == 1:
        near.append(lax.ppermute(packed[PLANES], "coarse", [(0, 1), (1, 0)]))
    else:
        up = [(i, i + 1) for i in range(coarse_count - 1)]
        near.append(lax.ppermute(packed[PLANES + 1], "coarse", up))
        near.append(lax.ppermute(packed[PLANES], "coarse", [(j, i) for i, j in up]))
    count = len(near)

    scalars = (partners, row_counts)
    rows = ((cases, width), F32)
    half_rows = ((cases, width), BF16)
    coded = ((subs, half, LANES), F32)
    theirs = [pltpu.VMEM((count - 1, cases, LANES), F32)]

    def restrict_first(partners_ref, counts_ref, mine_ref, arrived_ref, basis_ref, out_ref, message_ref):
        restrict_kernel(
            sizes, partners_ref, counts_ref, mine_ref, arrived_ref, basis_ref, None, out_ref, message_ref
        )

    residual, message = call(
        restrict_first, "restrict_residual", scalars, (load_cases, arrived, coarse_basis), [rows, coded]
    )
    coeffs = swap_all(message).reshape(subs * half, LANES)

    message, direction, applied, sums = call(
        functools.partial(first_kernel, sizes, dims, count),
        "first_direction",
        scalars,
        (coeffs, residual, coarse_basis, dual_ops, *near),
        [((subs, cases, LANES), BF16), rows, half_rows, ((half, LANES), F32)],
        theirs,
    )
    arrived = swap_all(message)
    image, message = call(
        functools.partial(restrict_kernel, sizes),
        "restrict_image",
        scalars,
        (applied, arrived, coarse_basis, sums),
        [rows, coded],
    )
    change = swap_all(message).reshape(subs * half, LANES)

    message, residual, multipliers, direction, applied = call(
        functools.partial(second_kernel, sizes, dims, count),
        "second_direction",
        scalars,
        (coeffs, change, residual, image, direction, coarse_basis, dual_ops, *near),
        [((subs, cases + half, LANES), BF16), rows, rows, rows, half_rows],
        theirs,
    )
    arrived = swap_all(message)
    out = ((1, cases, width), F32)
    multipliers, residual = call(
        functools.partial(last_kernel, sizes),
        "finish",
        scalars,
        (arrived, applied, residual, multipliers, direction),
        [out, out],
    )
    return multipliers, residual


def solution(mesh):
    rows = P(AXES, None, None)
    return jax.shard_map(
        body,
        mesh=mesh,
        in_specs=(rows, rows, rows, P(AXES, None, None, None), P(AXES, None), P(AXES, None), P(AXES, None)),
        out_specs=(rows, rows),
        check_vma=False,
    )
```

```python
import functools

import jax
import jax.numpy as jnp
from jax import lax
from jax.experimental import pallas as pl
from jax.experimental.pallas import tpu as pltpu
from jax.sharding import PartitionSpec as P

PLANES = 6
AXES = ("fine", "coarse")
LANES = 128
HALF = 64
BF16 = jnp.bfloat16
F32 = jnp.float32
GAMMA = 48
DELTA = 49


def lane_ids(rows):
    return lax.broadcasted_iota(jnp.int32, (rows, LANES), 1)


def dot(a, b):
    return lax.dot_general(a, b, (((1,), (0,)), ((), ())), preferred_element_type=F32)


def facing_subs(sizes, partners_ref):
    fine_count, coarse_count = sizes
    fine = lax.axis_index("fine")
    coarse = lax.axis_index("coarse")
    me = fine * coarse_count + coarse
    subs = [partners_ref[0, b] * coarse_count + coarse for b in range(PLANES)]
    subs.append(jnp.where(coarse > 0, me - 1, me))
    subs.append(jnp.where(coarse < coarse_count - 1, me + 1, me))
    return subs


def slot_of(sizes, partner):
    fine_count = sizes[0]
    fine = lax.axis_index("fine")
    ahead = jnp.where(fine % 2 == 0, partner - fine, fine - partner)
    ahead = jnp.where(ahead < 0, ahead + fine_count, ahead)
    return (ahead - 1) // 2


def live_mask(counts_ref, block):
    return (lane_ids(1) < counts_ref[0, block]).astype(F32)


def post_blocks(out_ref, targets, rows):
    cases = rows.shape[0]
    for block, target in enumerate(targets):
        out_ref[target, :cases, :] = rows[:, block * LANES : (block + 1) * LANES]


def post_split(sizes, partners_ref, rows, plane_ref, layer_refs):
    plane_ref[...] = jnp.zeros_like(plane_ref)
    post_blocks(plane_ref, [partners_ref[0, b] for b in range(PLANES)], rows)
    lower = rows[:, PLANES * LANES : (PLANES + 1) * LANES]
    upper = rows[:, (PLANES + 1) * LANES :]
    if len(layer_refs) == 1:
        bottom = lax.axis_index("coarse") == 0
        layer_refs[0][...] = jnp.where(bottom, upper.astype(F32), lower.astype(F32)).astype(rows.dtype)
    else:
        layer_refs[0][...] = lower
        layer_refs[1][...] = upper


def fetch(pairs, sems):
    copies = [pltpu.make_async_copy(source, target, sems.at[i]) for i, (source, target) in enumerate(pairs)]
    for copy in copies:
        copy.start()
    return copies


def send_kernel(sizes, partners_ref, counts_ref, pattern_ref, loads_ref, partners_out, counts_out, pattern_out,
                loads_out, plane_ref, *refs):
    layer_refs, partners_smem, sems = refs[:-2], refs[-2], refs[-1]
    copies = fetch(
        [(partners_ref, partners_smem), (loads_ref, loads_out), (partners_ref, partners_out), (counts_ref, counts_out),
         (pattern_ref, pattern_out)],
        sems,
    )
    copies[0].wait()
    copies[1].wait()
    post_split(sizes, partners_smem, loads_out[0], plane_ref, layer_refs)
    for copy in copies[2:]:
        copy.wait()


def pack_kernel(sizes, slots_here, partners_ref, pattern_ref, factors_hbm, basis_hbm, dual_hbm, basis_out, dual_out, *refs):
    outs, factors_ref, sems = refs[:-2], refs[-2], refs[-1]
    copies = fetch([(factors_hbm, factors_ref), (basis_hbm, basis_out), (dual_hbm, dual_out)], sems)
    copies[0].wait()
    terms, modes = factors_ref.shape[1:3]
    gap = jnp.zeros((modes, HALF - modes), F32)
    parts = []
    for term in range(terms):
        whole = factors_ref[0, term]
        high = whole.astype(BF16).astype(F32)
        parts.append(jnp.concatenate([high, gap, whole - high, gap], axis=1))
    factors = jnp.concatenate(parts, axis=0).astype(BF16)
    row = lax.broadcasted_iota(jnp.int32, (16, LANES), 0)
    ids = jnp.zeros((16, LANES), F32)
    for term in range(terms):
        sub = pattern_ref[0, term]
        ids = jnp.where(row == term, (sub // 16).astype(F32), ids)
        ids = jnp.where(row == 8 + term, (sub % 16).astype(F32), ids)
    ids = ids.astype(BF16)
    copies[1].wait()
    depth = terms * modes
    for out_ref in outs:
        out_ref[:depth, :] = factors
        out_ref[depth + modes :, :] = ids
    layers = len(outs) - slots_here
    put_bases(sizes, partners_ref, basis_out, outs[:slots_here], 0, (depth, depth + modes))
    if layers == 1:
        wanted = [jnp.where(lax.axis_index("coarse") == 0, PLANES + 1, PLANES)]
    else:
        wanted = [PLANES, PLANES + 1]
    for out_ref, block in zip(outs[slots_here:], wanted):
        out_ref[depth : depth + modes, :] = block_of(basis_out, block)
    copies[2].wait()


def block_of(basis_ref, block):
    start = block * LANES
    if not isinstance(start, int):
        start = pl.multiple_of(start, LANES)
    return basis_ref[0, :, pl.ds(start, LANES)]


def put_bases(sizes, partners_ref, basis_ref, outs, first, span):
    slots = [slot_of(sizes, partners_ref[0, b]) for b in range(PLANES)]
    for index, out_ref in enumerate(outs):
        block = sum(jnp.where(slots[b] == first + index, b, 0) for b in range(PLANES))
        out_ref[span[0] : span[1], :] = block_of(basis_ref, block)


def repack_kernel(sizes, first, span, partners_ref, packed_ref, basis_ref, after_ref, *outs):
    for out_ref in outs:
        out_ref[...] = packed_ref[...]
    put_bases(sizes, partners_ref, basis_ref, outs, first, span)


def facing_split(partners_ref, plane_ref, layer_refs):
    blocks = [plane_ref[partners_ref[0, b]] for b in range(PLANES)]
    return blocks + [layer_refs[0][...], layer_refs[-1][...]]


def difference(counts_ref, mine, facing):
    result, ours, theirs = [], [], []
    for block, other in enumerate(facing):
        mask = live_mask(counts_ref, block)
        left = mine[:, block * LANES : (block + 1) * LANES].astype(F32) * mask
        right = other.astype(F32) * mask
        result.append(left - right)
        ours.append(left.astype(BF16))
        theirs.append(right.astype(BF16))
    return result, ours, theirs


def restrict_kernel(layers, partners_ref, counts_ref, mine_ref, basis_ref, sums_ref, plane_ref, *refs):
    layer_refs, (out_ref, message_ref) = refs[:layers], refs[-2:]
    modes = basis_ref.shape[1]
    mine = mine_ref[...].reshape(mine_ref.shape[-2:])
    cases = mine.shape[0]
    facing = facing_split(partners_ref, plane_ref, layer_refs)
    result, ours, theirs = difference(counts_ref, mine, facing)
    for block, values in enumerate(result):
        out_ref[:, block * LANES : (block + 1) * LANES] = values
    both = jnp.concatenate([jnp.concatenate(ours, axis=1), jnp.concatenate(theirs, axis=1)], axis=0)
    basis = basis_ref[0]
    gap = jnp.zeros((HALF - modes, basis.shape[1]), BF16)
    twice = jnp.concatenate([basis, gap, basis, gap], axis=0)
    coefficients = lax.dot_general(both, twice, (((1,), (1,)), ((), ())), preferred_element_type=F32)
    coefficients = coefficients[:cases] - coefficients[cases:]
    half = cases // 2
    message = jnp.where(lane_ids(half) < HALF, coefficients[:half], coefficients[half:])
    if sums_ref is not None:
        message = message + sums_ref[...]
    message_ref[...] = jnp.broadcast_to(message[None], message_ref.shape)


def solve(coeffs, near, terms, modes):
    half = 8
    depth = terms * modes
    high = coeffs.astype(BF16)
    low = (coeffs - high.astype(F32)).astype(BF16)
    table = jnp.concatenate([high, low], axis=1)
    chunks = coeffs.shape[0] // LANES
    lanes = lane_ids(half).astype(F32)
    step = lax.broadcasted_iota(jnp.int32, (half, LANES), 0).astype(F32)
    picks = []
    for packed in near:
        ids = packed[depth + modes :, :].astype(F32)
        ids = (ids[:8] * 16.0 + ids[8:]) * float(half)
        for term in range(terms):
            target = ids[term : term + 1] + step
            picks.append(
                jnp.concatenate([(target == lanes + float(LANES * c)).astype(F32) for c in range(chunks)], axis=1)
            )
    picks = jnp.concatenate(picks, axis=0).astype(BF16)
    picked = dot(picks, table)
    left = lane_ids(half) < HALF
    gap = jnp.zeros((HALF - modes, LANES), BF16)
    solutions = []
    for index, packed in enumerate(near):
        sides = []
        for part in range(2):
            columns = []
            for pair in range(0, terms, 2):
                first, second = [
                    picked[(index * terms + term) * half : (index * terms + term + 1) * half, part * LANES : (part + 1) * LANES]
                    for term in (pair, pair + 1)
                ]
                top = jnp.where(left, first, pltpu.roll(second, HALF, 1))
                bottom = jnp.where(left, pltpu.roll(first, HALF, 1), second)
                columns.append(jnp.concatenate([top, bottom], axis=0))
            sides.append(jnp.concatenate(columns, axis=1))
        rows = jnp.concatenate(sides, axis=0).astype(BF16)
        factors = []
        for term in range(terms):
            factors += [packed[term * modes : (term + 1) * modes, :], gap]
        product = dot(rows, jnp.concatenate(factors, axis=0))
        product = product[: 2 * half] + product[2 * half :]
        product = product + pltpu.roll(product, HALF, 1)
        solutions.append(product[:, :modes].astype(BF16))
    return solutions


def advance(sizes, dims, partners_ref, counts_ref, coeffs, residual, near_refs, basis_ref, dual_ref, theirs_ref,
            direction_ref, applied_ref):
    terms, modes = dims
    depth = terms * modes
    near = [ref[...] for ref in near_refs]
    solutions = solve(coeffs, near, terms, modes)
    mine = dot(solutions[0], basis_ref[0]).astype(BF16).astype(F32)
    for index, packed in enumerate(near[1:]):
        theirs_ref[index] = dot(solutions[index + 1], packed[depth : depth + modes, :]).astype(BF16).astype(F32)
    pieces = []
    for block in range(PLANES + 2):
        if block < PLANES:
            place = slot_of(sizes, partners_ref[0, block])
        else:
            place = min(block, len(near) - 2)
        span = slice(block * LANES, (block + 1) * LANES)
        pieces.append(residual[:, span] + live_mask(counts_ref, block) * (mine[:, span] - theirs_ref[place]))
    direction = jnp.concatenate(pieces, axis=1)
    direction_ref[...] = direction
    applied = dot(direction.astype(BF16), dual_ref[0]).astype(BF16)
    applied_ref[...] = applied
    gamma = jnp.sum(residual * direction, axis=1, keepdims=True)
    delta = 2.0 * jnp.sum(direction * applied.astype(F32), axis=1, keepdims=True)
    half = gamma.shape[0] // 2
    lanes = lane_ids(half)
    sums = jnp.zeros((half, LANES), F32)
    for lane, values in ((GAMMA, gamma), (DELTA, delta)):
        sums = jnp.where(lanes == lane, values[:half], sums)
        sums = jnp.where(lanes == HALF + lane, values[half:], sums)
    return applied, sums


def first_kernel(sizes, dims, count, partners_ref, counts_ref, coeffs_ref, residual_ref, basis_ref, dual_ref, *refs):
    near_refs = refs[:count]
    direction_ref, applied_ref, sums_ref, plane_ref = refs[count : count + 4]
    layer_refs, theirs_ref = refs[count + 4 : -1], refs[-1]
    applied, sums = advance(
        sizes, dims, partners_ref, counts_ref, coeffs_ref[...], residual_ref[...], near_refs, basis_ref, dual_ref,
        theirs_ref, direction_ref, applied_ref,
    )
    post_split(sizes, partners_ref, applied, plane_ref, layer_refs)
    sums_ref[...] = sums


def steps_from(totals):
    low = totals[:, GAMMA : GAMMA + 1] / totals[:, DELTA : DELTA + 1]
    high = totals[:, HALF + GAMMA : HALF + GAMMA + 1] / totals[:, HALF + DELTA : HALF + DELTA + 1]
    return low, high


def second_kernel(sizes, dims, count, partners_ref, counts_ref, coeffs_ref, change_ref, residual_ref, image_ref,
                  before_ref, basis_ref, dual_ref, *refs):
    near_refs = refs[:count]
    message_ref, residual_out, multipliers_out, direction_ref, applied_ref, theirs_ref = refs[count:]
    half = residual_ref.shape[0] // 2
    change = change_ref[...].reshape(-1, half, LANES)
    low, high = steps_from(jnp.sum(change, axis=0))
    step = jnp.concatenate([low, high], axis=0)
    packed_step = jnp.where(lane_ids(half) < HALF, low, high)
    coeffs = coeffs_ref[...] - (change * packed_step[None]).reshape(coeffs_ref.shape)
    residual = residual_ref[...] - step * image_ref[...]
    residual_out[...] = residual
    multipliers_out[...] = step * before_ref[...]
    applied, sums = advance(
        sizes, dims, partners_ref, counts_ref, coeffs, residual, near_refs, basis_ref, dual_ref, theirs_ref,
        direction_ref, applied_ref,
    )
    top = sums.astype(BF16).astype(F32)
    middle = (sums - top).astype(BF16).astype(F32)
    bottom = sums - top - middle
    coded = (top + pltpu.roll(middle, 2, 1) + pltpu.roll(bottom, 4, 1)).astype(BF16)
    cases = applied.shape[0]
    message_ref[:, :cases, :] = jnp.zeros((message_ref.shape[0], cases, LANES), BF16)
    message_ref[:, cases:, :] = jnp.broadcast_to(coded[None], (message_ref.shape[0], half, LANES))
    post_blocks(message_ref, facing_subs(sizes, partners_ref), applied)


def last_kernel(sizes, partners_ref, counts_ref, arrived_ref, applied_ref, residual_ref, multipliers_ref, direction_ref,
                multipliers_out, residual_out):
    cases = applied_ref.shape[0]
    totals = jnp.sum(arrived_ref[:, cases:, :].astype(F32), axis=0)
    totals = totals + pltpu.roll(totals, LANES - 2, 1) + pltpu.roll(totals, LANES - 4, 1)
    step = jnp.concatenate(steps_from(totals), axis=0)
    facing = [arrived_ref[target, :cases, :] for target in facing_subs(sizes, partners_ref)]
    image, _, _ = difference(counts_ref, applied_ref[...], facing)
    fine = lax.axis_index("fine")
    for block in range(PLANES + 2):
        span = slice(block * LANES, (block + 1) * LANES)
        if block < PLANES:
            sign = jnp.where(fine < partners_ref[0, block], 1.0, -1.0).astype(F32)
        else:
            sign = -1.0 if block == PLANES else 1.0
        multipliers_out[0, :, span] = sign * (multipliers_ref[:, span] + step * direction_ref[:, span])
        residual_out[0, :, span] = sign * (residual_ref[:, span] - step * image[block])


SMEM = pl.BlockSpec(memory_space=pltpu.SMEM)
VMEM = pl.BlockSpec(memory_space=pltpu.VMEM)


HBM = pl.BlockSpec(memory_space=pl.ANY)


def call(kernel, name, scalars, arrays, outs, scratch=(), far=()):
    return pl.pallas_call(
        kernel,
        name=name,
        out_shape=[jax.ShapeDtypeStruct(shape, dtype) for shape, dtype in outs],
        in_specs=[SMEM] * len(scalars) + [VMEM] * len(arrays) + [HBM] * len(far),
        out_specs=[VMEM] * len(outs),
        scratch_shapes=list(scratch),
        compiler_params=pltpu.CompilerParams(vmem_limit_bytes=40 * 1024 * 1024),
    )(*scalars, *arrays, *far)


def body(load_cases, dual_ops, coarse_basis, factor_blocks, pattern, partners, row_counts):
    cases, width = load_cases.shape[1:]
    terms, modes = factor_blocks.shape[1:3]
    fine_count = lax.axis_size("fine")
    coarse_count = lax.axis_size("coarse")
    subs = fine_count * coarse_count
    sizes = (fine_count, coarse_count)
    dims = (terms, modes)
    half = cases // 2
    layers = 1 if coarse_count == 2 else 2
    split = 3

    def swap_all(message):
        return lax.all_to_all(message, AXES, 0, 0, tiled=True)

    def swap_layers(messages):
        if layers == 1:
            return [lax.ppermute(messages[0], "coarse", [(0, 1), (1, 0)])]
        up = [(i, i + 1) for i in range(coarse_count - 1)]
        return [lax.ppermute(messages[1], "coarse", up), lax.ppermute(messages[0], "coarse", [(j, i) for i, j in up])]

    def swap_blocks(plane, layer):
        return [lax.all_to_all(plane, "fine", 0, 0, tiled=True)] + swap_layers(layer)

    def swap_slot(packed, slot):
        distance = 2 * slot + 1
        pairs = [(i, (i + distance if i % 2 == 0 else i - distance) % fine_count) for i in range(fine_count)]
        return lax.ppermute(packed, "fine", pairs)

    rows = ((cases, width), F32)
    half_rows = ((cases, width), BF16)
    coded = ((subs, half, LANES), F32)
    blocks = [((fine_count, cases, LANES), BF16)] + [((cases, LANES), BF16)] * layers
    dma = pltpu.SemaphoreType.DMA

    partners, row_counts, pattern, loads, plane, *layer = call(
        functools.partial(send_kernel, sizes),
        "send_loads",
        (),
        (),
        [(partners.shape, jnp.int32), (row_counts.shape, jnp.int32), (pattern.shape, jnp.int32), (load_cases.shape, BF16)]
        + blocks,
        [pltpu.SMEM(partners.shape, jnp.int32), dma((5,))],
        (partners, row_counts, pattern, load_cases),
    )
    arrived = swap_blocks(plane, layer)

    depth = terms * modes
    packed_shape = ((depth + modes + 16, LANES), BF16)
    basis, dual, *packed = call(
        functools.partial(pack_kernel, sizes, split),
        "pack_factors",
        (partners, pattern),
        (),
        [(coarse_basis.shape, BF16), (dual_ops.shape, BF16)] + [packed_shape] * (split + layers),
        [pltpu.VMEM(factor_blocks.shape, F32), dma((3,))],
        (factor_blocks, coarse_basis, dual_ops),
    )
    near = [packed[split]] + [swap_slot(packed[slot], slot) for slot in range(split)]
    near_layers = swap_layers(packed[split:])

    scalars = (partners, row_counts)

    def restrict_first(partners_ref, counts_ref, mine_ref, basis_ref, plane_ref, *refs):
        restrict_kernel(layers, partners_ref, counts_ref, mine_ref, basis_ref, None, plane_ref, *refs)

    residual, message = call(
        restrict_first, "restrict_residual", scalars, (loads, basis, *arrived), [rows, coded], (),
        (*near[1:], *near_layers),
    )
    coeffs = swap_all(message).reshape(subs * half, LANES)

    packed = call(
        functools.partial(repack_kernel, sizes, split, (depth, depth + modes)),
        "pack_factors_again",
        (partners,),
        (packed[split], basis),
        [packed_shape] * (PLANES - split),
        (),
        (residual,),
    )
    near += [swap_slot(packed[slot - split], slot) for slot in range(split, PLANES)] + near_layers
    count = len(near)
    theirs = [pltpu.VMEM((count - 1, cases, LANES), F32)]

    direction, applied, sums, plane, *layer = call(
        functools.partial(first_kernel, sizes, dims, count),
        "first_direction",
        scalars,
        (coeffs, residual, basis, dual, *near),
        [rows, half_rows, ((half, LANES), F32)] + blocks,
        theirs,
    )
    arrived = swap_blocks(plane, layer)
    image, message = call(
        functools.partial(restrict_kernel, layers),
        "restrict_image",
        scalars,
        (applied, basis, sums, *arrived),
        [rows, coded],
    )
    change = swap_all(message).reshape(subs * half, LANES)

    message, residual, multipliers, direction, applied = call(
        functools.partial(second_kernel, sizes, dims, count),
        "second_direction",
        scalars,
        (coeffs, change, residual, image, direction, basis, dual, *near),
        [((subs, cases + half, LANES), BF16), rows, rows, rows, half_rows],
        theirs,
    )
    arrived = swap_all(message)
    out = ((1, cases, width), F32)
    multipliers, residual = call(
        functools.partial(last_kernel, sizes),
        "finish",
        scalars,
        (arrived, applied, residual, multipliers, direction),
        [out, out],
    )
    return multipliers, residual


def solution(mesh):
    rows = P(AXES, None, None)
    return jax.shard_map(
        body,
        mesh=mesh,
        in_specs=(rows, rows, rows, P(AXES, None, None, None), P(AXES, None), P(AXES, None), P(AXES, None)),
        out_specs=(rows, rows),
        check_vma=False,
    )
```

```python
import functools

import jax
import jax.numpy as jnp
from jax import lax
from jax.experimental import pallas as pl
from jax.experimental.pallas import tpu as pltpu
from jax.sharding import PartitionSpec as P

PLANES = 6
AXES = ("fine", "coarse")
LANES = 128
HALF = 64
BF16 = jnp.bfloat16
F32 = jnp.float32
GAMMA = 48
DELTA = 49


def lane_ids(rows):
    return lax.broadcasted_iota(jnp.int32, (rows, LANES), 1)


def dot(a, b):
    return lax.dot_general(a, b, (((1,), (0,)), ((), ())), preferred_element_type=F32)


def facing_subs(sizes, partners_ref):
    fine_count, coarse_count = sizes
    fine = lax.axis_index("fine")
    coarse = lax.axis_index("coarse")
    me = fine * coarse_count + coarse
    subs = [partners_ref[0, b] * coarse_count + coarse for b in range(PLANES)]
    subs.append(jnp.where(coarse > 0, me - 1, me))
    subs.append(jnp.where(coarse < coarse_count - 1, me + 1, me))
    return subs


def slot_of(sizes, partner):
    fine_count = sizes[0]
    fine = lax.axis_index("fine")
    ahead = jnp.where(fine % 2 == 0, partner - fine, fine - partner)
    ahead = jnp.where(ahead < 0, ahead + fine_count, ahead)
    return (ahead - 1) // 2


def live_mask(counts_ref, block):
    return (lane_ids(1) < counts_ref[0, block]).astype(F32)


def post_blocks(out_ref, targets, rows):
    cases = rows.shape[0]
    for block, target in enumerate(targets):
        out_ref[target, :cases, :] = rows[:, block * LANES : (block + 1) * LANES]


def fetch(pairs, sems):
    copies = [pltpu.make_async_copy(source, target, sems.at[i]) for i, (source, target) in enumerate(pairs)]
    for copy in copies:
        copy.start()
    return copies


def pack_kernel(sizes, layers, partners_ref, counts_ref, pattern_ref, loads_ref, basis_ref, factors_ref,
                partners_out, counts_out, loads_out, basis_out, *refs):
    outs, partners_smem, pattern_smem, factors_vmem, sems = refs[:-4], *refs[-4:]
    copies = fetch(
        [(partners_ref, partners_smem), (pattern_ref, pattern_smem), (loads_ref, loads_out), (basis_ref, basis_out),
         (factors_ref, factors_vmem), (partners_ref, partners_out), (counts_ref, counts_out)],
        sems,
    )
    for copy in copies:
        copy.wait()
    terms, modes = factors_vmem.shape[1:3]
    gap = jnp.zeros((modes, HALF - modes), F32)
    parts = []
    for term in range(terms):
        whole = factors_vmem[0, term]
        high = whole.astype(BF16).astype(F32)
        parts.append(jnp.concatenate([high, gap, whole - high, gap], axis=1))
    factors = jnp.concatenate(parts, axis=0).astype(BF16)
    row = lax.broadcasted_iota(jnp.int32, (16, LANES), 0)
    ids = jnp.zeros((16, LANES), F32)
    for term in range(terms):
        sub = pattern_smem[0, term]
        ids = jnp.where(row == term, (sub // 16).astype(F32), ids)
        ids = jnp.where(row == 8 + term, (sub % 16).astype(F32), ids)
    ids = ids.astype(BF16)
    slots = [slot_of(sizes, partners_smem[0, b]) for b in range(PLANES)]
    wanted = []
    for slot in range(PLANES):
        wanted.append(sum(jnp.where(slots[b] == slot, b, 0) for b in range(PLANES)))
    if layers == 1:
        wanted.append(jnp.where(lax.axis_index("coarse") == 0, PLANES + 1, PLANES))
    else:
        wanted += [PLANES, PLANES + 1]
    places = layout_of(terms, modes)
    for out_ref, block in zip(outs, wanted):
        out_ref[places["factors"], :] = factors
        out_ref[places["ids"], :] = ids
        start = block * LANES
        if not isinstance(start, int):
            start = pl.multiple_of(start, LANES)
        out_ref[places["basis"], :] = basis_out[0, :, pl.ds(start, LANES)]
        out_ref[places["loads"], :] = loads_out[0, :, pl.ds(start, LANES)]


def layout_of(terms, modes):
    sizes = (("factors", terms * modes), ("basis", modes), ("ids", 16), ("loads", 16))
    places, start = {}, 0
    for name, rows in sizes:
        places[name] = slice(start, start + rows)
        start += rows
    return places


def dual_kernel(dual_ref, after_ref, out_ref, sems):
    for copy in fetch([(dual_ref, out_ref)], sems):
        copy.wait()


def difference(counts_ref, mine, facing):
    result, ours, theirs = [], [], []
    for block, other in enumerate(facing):
        mask = live_mask(counts_ref, block)
        left = mine[:, block * LANES : (block + 1) * LANES].astype(F32) * mask
        right = other.astype(F32) * mask
        result.append(left - right)
        ours.append(left.astype(BF16))
        theirs.append(right.astype(BF16))
    return result, ours, theirs


def first_restrict_kernel(sizes, dims, layers, partners_ref, counts_ref, loads_ref, basis_ref, *refs):
    near_refs, (out_ref, message_ref, scratch_ref) = refs[: PLANES + layers], refs[-3:]
    span = layout_of(*dims)["loads"]
    for slot in range(PLANES):
        scratch_ref[slot] = near_refs[slot][span, :]
    facing = [scratch_ref[slot_of(sizes, partners_ref[0, b])] for b in range(PLANES)]
    facing += [near_refs[PLANES][span, :], near_refs[-1][span, :]]
    restrict(counts_ref, loads_ref[0], facing, basis_ref, None, out_ref, message_ref)


def restrict_kernel(sizes, partners_ref, counts_ref, mine_ref, basis_ref, sums_ref, arrived_ref, out_ref, message_ref):
    facing = [arrived_ref[target] for target in facing_subs(sizes, partners_ref)]
    restrict(counts_ref, mine_ref[...], facing, basis_ref, sums_ref, out_ref, message_ref)


def restrict(counts_ref, mine, facing, basis_ref, sums_ref, out_ref, message_ref):
    modes = basis_ref.shape[1]
    cases = mine.shape[0]
    result, ours, theirs = difference(counts_ref, mine, facing)
    for block, values in enumerate(result):
        out_ref[:, block * LANES : (block + 1) * LANES] = values
    both = jnp.concatenate([jnp.concatenate(ours, axis=1), jnp.concatenate(theirs, axis=1)], axis=0)
    basis = basis_ref[0]
    gap = jnp.zeros((HALF - modes, basis.shape[1]), BF16)
    twice = jnp.concatenate([basis, gap, basis, gap], axis=0)
    coefficients = lax.dot_general(both, twice, (((1,), (1,)), ((), ())), preferred_element_type=F32)
    coefficients = coefficients[:cases] - coefficients[cases:]
    half = cases // 2
    message = jnp.where(lane_ids(half) < HALF, coefficients[:half], coefficients[half:])
    if sums_ref is not None:
        message = message + sums_ref[...]
    message_ref[...] = jnp.broadcast_to(message[None], message_ref.shape)


def solve(coeffs, near, terms, modes):
    half = 8
    places = layout_of(terms, modes)
    high = coeffs.astype(BF16)
    low = (coeffs - high.astype(F32)).astype(BF16)
    table = jnp.concatenate([high, low], axis=1)
    chunks = coeffs.shape[0] // LANES
    lanes = lane_ids(half).astype(F32)
    step = lax.broadcasted_iota(jnp.int32, (half, LANES), 0).astype(F32)
    picks = []
    for packed in near:
        ids = packed[places["ids"], :].astype(F32)
        ids = (ids[:8] * 16.0 + ids[8:]) * float(half)
        for term in range(terms):
            target = ids[term : term + 1] + step
            picks.append(
                jnp.concatenate([(target == lanes + float(LANES * c)).astype(F32) for c in range(chunks)], axis=1)
            )
    picks = jnp.concatenate(picks, axis=0).astype(BF16)
    picked = dot(picks, table)
    left = lane_ids(half) < HALF
    gap = jnp.zeros((HALF - modes, LANES), BF16)
    solutions = []
    for index, packed in enumerate(near):
        sides = []
        for part in range(2):
            columns = []
            for pair in range(0, terms, 2):
                first, second = [
                    picked[(index * terms + term) * half : (index * terms + term + 1) * half, part * LANES : (part + 1) * LANES]
                    for term in (pair, pair + 1)
                ]
                top = jnp.where(left, first, pltpu.roll(second, HALF, 1))
                bottom = jnp.where(left, pltpu.roll(first, HALF, 1), second)
                columns.append(jnp.concatenate([top, bottom], axis=0))
            sides.append(jnp.concatenate(columns, axis=1))
        rows = jnp.concatenate(sides, axis=0).astype(BF16)
        factors = []
        for term in range(terms):
            factors += [packed[term * modes : (term + 1) * modes, :], gap]
        product = dot(rows, jnp.concatenate(factors, axis=0))
        product = product[: 2 * half] + product[2 * half :]
        product = product + pltpu.roll(product, HALF, 1)
        solutions.append(product[:, :modes].astype(BF16))
    return solutions


def advance(sizes, dims, partners_ref, counts_ref, coeffs, residual, near_refs, basis_ref, dual_ref, theirs_ref,
            direction_ref, applied_ref):
    terms, modes = dims
    span = layout_of(terms, modes)["basis"]
    near = [ref[...] for ref in near_refs]
    solutions = solve(coeffs, near, terms, modes)
    mine = dot(solutions[0], basis_ref[0]).astype(BF16).astype(F32)
    for index, packed in enumerate(near[1:]):
        theirs_ref[index] = dot(solutions[index + 1], packed[span, :]).astype(BF16).astype(F32)
    pieces = []
    for block in range(PLANES + 2):
        if block < PLANES:
            place = slot_of(sizes, partners_ref[0, block])
        else:
            place = min(block, len(near) - 2)
        here = slice(block * LANES, (block + 1) * LANES)
        pieces.append(residual[:, here] + live_mask(counts_ref, block) * (mine[:, here] - theirs_ref[place]))
    direction = jnp.concatenate(pieces, axis=1)
    direction_ref[...] = direction
    applied = dot(direction.astype(BF16), dual_ref[0]).astype(BF16)
    applied_ref[...] = applied
    gamma = jnp.sum(residual * direction, axis=1, keepdims=True)
    delta = 2.0 * jnp.sum(direction * applied.astype(F32), axis=1, keepdims=True)
    half = gamma.shape[0] // 2
    lanes = lane_ids(half)
    sums = jnp.zeros((half, LANES), F32)
    for lane, values in ((GAMMA, gamma), (DELTA, delta)):
        sums = jnp.where(lanes == lane, values[:half], sums)
        sums = jnp.where(lanes == HALF + lane, values[half:], sums)
    return applied, sums


def first_kernel(sizes, dims, count, partners_ref, counts_ref, coeffs_ref, residual_ref, basis_ref, dual_ref, *refs):
    near_refs = refs[:count]
    message_ref, direction_ref, applied_ref, sums_ref, theirs_ref = refs[count:]
    applied, sums = advance(
        sizes, dims, partners_ref, counts_ref, coeffs_ref[...], residual_ref[...], near_refs, basis_ref, dual_ref,
        theirs_ref, direction_ref, applied_ref,
    )
    message_ref[...] = jnp.zeros_like(message_ref)
    post_blocks(message_ref, facing_subs(sizes, partners_ref), applied)
    sums_ref[...] = sums


def steps_from(totals):
    low = totals[:, GAMMA : GAMMA + 1] / totals[:, DELTA : DELTA + 1]
    high = totals[:, HALF + GAMMA : HALF + GAMMA + 1] / totals[:, HALF + DELTA : HALF + DELTA + 1]
    return low, high


def second_kernel(sizes, dims, count, partners_ref, counts_ref, coeffs_ref, change_ref, residual_ref, image_ref,
                  before_ref, basis_ref, dual_ref, *refs):
    near_refs = refs[:count]
    message_ref, residual_out, multipliers_out, direction_ref, applied_ref, theirs_ref = refs[count:]
    half = residual_ref.shape[0] // 2
    change = change_ref[...].reshape(-1, half, LANES)
    low, high = steps_from(jnp.sum(change, axis=0))
    step = jnp.concatenate([low, high], axis=0)
    packed_step = jnp.where(lane_ids(half) < HALF, low, high)
    coeffs = coeffs_ref[...] - (change * packed_step[None]).reshape(coeffs_ref.shape)
    residual = residual_ref[...] - step * image_ref[...]
    residual_out[...] = residual
    multipliers_out[...] = step * before_ref[...]
    applied, sums = advance(
        sizes, dims, partners_ref, counts_ref, coeffs, residual, near_refs, basis_ref, dual_ref, theirs_ref,
        direction_ref, applied_ref,
    )
    top = sums.astype(BF16).astype(F32)
    middle = (sums - top).astype(BF16).astype(F32)
    bottom = sums - top - middle
    coded = (top + pltpu.roll(middle, 2, 1) + pltpu.roll(bottom, 4, 1)).astype(BF16)
    cases = applied.shape[0]
    message_ref[:, :cases, :] = jnp.zeros((message_ref.shape[0], cases, LANES), BF16)
    message_ref[:, cases:, :] = jnp.broadcast_to(coded[None], (message_ref.shape[0], half, LANES))
    post_blocks(message_ref, facing_subs(sizes, partners_ref), applied)


def last_kernel(sizes, partners_ref, counts_ref, arrived_ref, applied_ref, residual_ref, multipliers_ref, direction_ref,
                multipliers_out, residual_out):
    cases = applied_ref.shape[0]
    totals = jnp.sum(arrived_ref[:, cases:, :].astype(F32), axis=0)
    totals = totals + pltpu.roll(totals, LANES - 2, 1) + pltpu.roll(totals, LANES - 4, 1)
    step = jnp.concatenate(steps_from(totals), axis=0)
    facing = [arrived_ref[target, :cases, :] for target in facing_subs(sizes, partners_ref)]
    image, _, _ = difference(counts_ref, applied_ref[...], facing)
    fine = lax.axis_index("fine")
    for block in range(PLANES + 2):
        span = slice(block * LANES, (block + 1) * LANES)
        if block < PLANES:
            sign = jnp.where(fine < partners_ref[0, block], 1.0, -1.0).astype(F32)
        else:
            sign = -1.0 if block == PLANES else 1.0
        multipliers_out[0, :, span] = sign * (multipliers_ref[:, span] + step * direction_ref[:, span])
        residual_out[0, :, span] = sign * (residual_ref[:, span] - step * image[block])


SMEM = pl.BlockSpec(memory_space=pltpu.SMEM)
VMEM = pl.BlockSpec(memory_space=pltpu.VMEM)


HBM = pl.BlockSpec(memory_space=pltpu.HBM)
ANY = pl.BlockSpec(memory_space=pl.ANY)


def call(kernel, name, scalars, arrays, outs, scratch=(), far=(), after=()):
    return pl.pallas_call(
        kernel,
        name=name,
        out_shape=[jax.ShapeDtypeStruct(shape, dtype) for shape, dtype in outs],
        in_specs=[SMEM] * len(scalars) + [VMEM] * len(arrays) + [HBM] * len(far) + [ANY] * len(after),
        out_specs=[VMEM] * len(outs),
        scratch_shapes=list(scratch),
        compiler_params=pltpu.CompilerParams(vmem_limit_bytes=40 * 1024 * 1024),
    )(*scalars, *arrays, *far, *after)


def body(load_cases, dual_ops, coarse_basis, factor_blocks, pattern, partners, row_counts):
    cases, width = load_cases.shape[1:]
    terms, modes = factor_blocks.shape[1:3]
    fine_count = lax.axis_size("fine")
    coarse_count = lax.axis_size("coarse")
    subs = fine_count * coarse_count
    sizes = (fine_count, coarse_count)
    dims = (terms, modes)
    half = cases // 2
    layers = 1 if coarse_count == 2 else 2

    def swap_all(message):
        return lax.all_to_all(message, AXES, 0, 0, tiled=True)

    def swap_layers(messages):
        if layers == 1:
            return [lax.ppermute(messages[0], "coarse", [(0, 1), (1, 0)])]
        up = [(i, i + 1) for i in range(coarse_count - 1)]
        return [lax.ppermute(messages[1], "coarse", up), lax.ppermute(messages[0], "coarse", [(j, i) for i, j in up])]

    def swap_slot(packed, slot):
        distance = 2 * slot + 1
        pairs = [(i, (i + distance if i % 2 == 0 else i - distance) % fine_count) for i in range(fine_count)]
        return lax.ppermute(packed, "fine", pairs)

    rows = ((cases, width), F32)
    half_rows = ((cases, width), BF16)
    coded = ((subs, half, LANES), F32)
    dma = pltpu.SemaphoreType.DMA

    message_rows = layout_of(terms, modes)["loads"].stop
    partners, row_counts, loads, basis, *packed = call(
        functools.partial(pack_kernel, sizes, layers),
        "pack_setup",
        (),
        (),
        [(partners.shape, jnp.int32), (row_counts.shape, jnp.int32), (load_cases.shape, BF16), (coarse_basis.shape, BF16)]
        + [((message_rows, LANES), BF16)] * (PLANES + layers),
        [pltpu.SMEM(partners.shape, jnp.int32), pltpu.SMEM(pattern.shape, jnp.int32),
         pltpu.VMEM(factor_blocks.shape, F32), dma((7,))],
        (partners, row_counts, pattern, load_cases, coarse_basis, factor_blocks),
    )
    received = [swap_slot(packed[slot], slot) for slot in range(PLANES)] + swap_layers(packed[PLANES:])
    near = [packed[-1]] + received
    count = len(near)
    theirs = [pltpu.VMEM((count - 1, cases, LANES), F32)]

    scalars = (partners, row_counts)
    residual, message = call(
        functools.partial(first_restrict_kernel, sizes, dims, layers),
        "restrict_residual",
        scalars,
        (loads, basis, *received),
        [rows, coded],
        [pltpu.VMEM((PLANES, cases, LANES), BF16)],
    )
    coeffs = swap_all(message).reshape(subs * half, LANES)
    [dual] = call(dual_kernel, "fetch_dual", (), (), [(dual_ops.shape, BF16)], [dma((1,))], (dual_ops,), (residual,))

    message, direction, applied, sums = call(
        functools.partial(first_kernel, sizes, dims, count),
        "first_direction",
        scalars,
        (coeffs, residual, basis, dual, *near),
        [((subs, cases, LANES), BF16), rows, half_rows, ((half, LANES), F32)],
        theirs,
    )
    arrived = swap_all(message)
    image, message = call(
        functools.partial(restrict_kernel, sizes),
        "restrict_image",
        scalars,
        (applied, basis, sums, arrived),
        [rows, coded],
    )
    change = swap_all(message).reshape(subs * half, LANES)

    message, residual, multipliers, direction, applied = call(
        functools.partial(second_kernel, sizes, dims, count),
        "second_direction",
        scalars,
        (coeffs, change, residual, image, direction, basis, dual, *near),
        [((subs, cases + half, LANES), BF16), rows, rows, rows, half_rows],
        theirs,
    )
    arrived = swap_all(message)
    out = ((1, cases, width), F32)
    multipliers, residual = call(
        functools.partial(last_kernel, sizes),
        "finish",
        scalars,
        (arrived, applied, residual, multipliers, direction),
        [out, out],
    )
    return multipliers, residual


def solution(mesh):
    rows = P(AXES, None, None)
    return jax.shard_map(
        body,
        mesh=mesh,
        in_specs=(rows, rows, rows, P(AXES, None, None, None), P(AXES, None), P(AXES, None), P(AXES, None)),
        out_specs=(rows, rows),
        check_vma=False,
    )
```

```python
import functools

import jax
import jax.numpy as jnp
from jax import lax
from jax.experimental import pallas as pl
from jax.experimental.pallas import tpu as pltpu
from jax.sharding import PartitionSpec as P

PLANES = 6
AXES = ("fine", "coarse")
LANES = 128
HALF = 64
BF16 = jnp.bfloat16
F32 = jnp.float32
GAMMA = 48
DELTA = 49


def lane_ids(rows):
    return lax.broadcasted_iota(jnp.int32, (rows, LANES), 1)


def dot(a, b):
    return lax.dot_general(a, b, (((1,), (0,)), ((), ())), preferred_element_type=F32)


def wanted_blocks(sizes, layers, meta_ref):
    slots = [slot_of(sizes, meta_ref[0, b]) for b in range(PLANES)]
    blocks = []
    for slot in range(PLANES):
        blocks.append(sum(jnp.where(slots[b] == slot, b, 0) for b in range(PLANES)))
    if layers == 1:
        return blocks + [jnp.where(lax.axis_index("coarse") == 0, PLANES + 1, PLANES)]
    return blocks + [PLANES, PLANES + 1]


def lanes_of(block):
    start = block * LANES
    return pl.ds(start if isinstance(start, int) else pl.multiple_of(start, LANES), LANES)


def facing_subs(sizes, partners_ref):
    fine_count, coarse_count = sizes
    fine = lax.axis_index("fine")
    coarse = lax.axis_index("coarse")
    me = fine * coarse_count + coarse
    subs = [partners_ref[0, b] * coarse_count + coarse for b in range(PLANES)]
    subs.append(jnp.where(coarse > 0, me - 1, me))
    subs.append(jnp.where(coarse < coarse_count - 1, me + 1, me))
    return subs


def slot_of(sizes, partner):
    fine_count = sizes[0]
    fine = lax.axis_index("fine")
    ahead = jnp.where(fine % 2 == 0, partner - fine, fine - partner)
    ahead = jnp.where(ahead < 0, ahead + fine_count, ahead)
    return (ahead - 1) // 2


def live_mask(counts_ref, block):
    return (lane_ids(1) < counts_ref[0, PLANES + block]).astype(F32)


def post_blocks(out_ref, targets, rows):
    cases = rows.shape[0]
    for block, target in enumerate(targets):
        out_ref[target, :cases, :] = rows[:, block * LANES : (block + 1) * LANES]


def fetch(pairs, sems):
    copies = [pltpu.make_async_copy(source, target, sems.at[i]) for i, (source, target) in enumerate(pairs)]
    for copy in copies:
        copy.start()
    return copies


def pack_kernel(sizes, layers, cases, meta_ref, rows_ref, factors_ref, *outs):
    terms, modes = factors_ref.shape[1:3]
    gap = jnp.zeros((modes, HALF - modes), F32)
    parts = []
    for term in range(terms):
        whole = factors_ref[0, term]
        high = whole.astype(BF16).astype(F32)
        parts.append(jnp.concatenate([high, gap, whole - high, gap], axis=1))
    factors = jnp.concatenate(parts, axis=0).astype(BF16)
    row = lax.broadcasted_iota(jnp.int32, (16, LANES), 0)
    ids = jnp.zeros((16, LANES), F32)
    for term in range(terms):
        sub = meta_ref[0, 2 * PLANES + 2 + term]
        ids = jnp.where(row == term, (sub // 16).astype(F32), ids)
        ids = jnp.where(row == 8 + term, (sub % 16).astype(F32), ids)
    ids = ids.astype(BF16)
    places = layout_of(terms, modes)
    for out_ref, block in zip(outs, wanted_blocks(sizes, layers, meta_ref)):
        out_ref[places["factors"], :] = factors
        out_ref[places["ids"], :] = ids
        out_ref[places["loads"], :] = rows_ref[:cases, lanes_of(block)]
        out_ref[places["basis"], :] = rows_ref[cases:, lanes_of(block)]


def layout_of(terms, modes):
    sizes = (("factors", terms * modes), ("basis", modes), ("ids", 16), ("loads", 16))
    places, start = {}, 0
    for name, rows in sizes:
        places[name] = slice(start, start + rows)
        start += rows
    return places


def dual_kernel(dual_ref, after_ref, out_ref, sems):
    for copy in fetch([(dual_ref, out_ref)], sems):
        copy.wait()


def difference(counts_ref, mine, facing):
    result, ours, theirs = [], [], []
    for block, other in enumerate(facing):
        mask = live_mask(counts_ref, block)
        left = mine[:, block * LANES : (block + 1) * LANES].astype(F32) * mask
        right = other.astype(F32) * mask
        result.append(left - right)
        ours.append(left.astype(BF16))
        theirs.append(right.astype(BF16))
    return result, ours, theirs


def restrict_kernel(sizes, layers, span, cases, own_loads, meta_ref, rows_ref, *refs):
    near_refs, refs = refs[: PLANES + layers], refs[PLANES + layers :]
    out_ref, message_ref, scratch_ref = refs[-3:]
    for slot in range(PLANES):
        scratch_ref[slot] = near_refs[slot][span, :]
    facing = [scratch_ref[slot_of(sizes, meta_ref[0, b])] for b in range(PLANES)]
    facing += [near_refs[PLANES][span, :], near_refs[-1][span, :]]
    mine = rows_ref[:cases, :] if own_loads else refs[0][...]
    basis = rows_ref[cases:, :]
    modes = basis.shape[0]
    result, ours, theirs = difference(meta_ref, mine, facing)
    for block, values in enumerate(result):
        out_ref[:, block * LANES : (block + 1) * LANES] = values
    both = jnp.concatenate([jnp.concatenate(ours, axis=1), jnp.concatenate(theirs, axis=1)], axis=0)
    gap = jnp.zeros((HALF - modes, basis.shape[1]), BF16)
    twice = jnp.concatenate([basis, gap, basis, gap], axis=0)
    coefficients = lax.dot_general(both, twice, (((1,), (1,)), ((), ())), preferred_element_type=F32)
    coefficients = coefficients[:cases] - coefficients[cases:]
    half = cases // 2
    message = jnp.where(lane_ids(half) < HALF, coefficients[:half], coefficients[half:])
    if not own_loads:
        message = message + refs[1][...]
    message_ref[...] = jnp.broadcast_to(message[None], message_ref.shape)


def solve(coeffs, near, terms, modes):
    half = 8
    places = layout_of(terms, modes)
    high = coeffs.astype(BF16)
    low = (coeffs - high.astype(F32)).astype(BF16)
    table = jnp.concatenate([high, low], axis=1)
    chunks = coeffs.shape[0] // LANES
    lanes = lane_ids(half).astype(F32)
    step = lax.broadcasted_iota(jnp.int32, (half, LANES), 0).astype(F32)
    picks = []
    for packed in near:
        ids = packed[places["ids"], :].astype(F32)
        ids = (ids[:8] * 16.0 + ids[8:]) * float(half)
        for term in range(terms):
            target = ids[term : term + 1] + step
            picks.append(
                jnp.concatenate([(target == lanes + float(LANES * c)).astype(F32) for c in range(chunks)], axis=1)
            )
    picks = jnp.concatenate(picks, axis=0).astype(BF16)
    picked = dot(picks, table)
    left = lane_ids(half) < HALF
    gap = jnp.zeros((HALF - modes, LANES), BF16)
    solutions = []
    for index, packed in enumerate(near):
        sides = []
        for part in range(2):
            columns = []
            for pair in range(0, terms, 2):
                first, second = [
                    picked[(index * terms + term) * half : (index * terms + term + 1) * half, part * LANES : (part + 1) * LANES]
                    for term in (pair, pair + 1)
                ]
                top = jnp.where(left, first, pltpu.roll(second, HALF, 1))
                bottom = jnp.where(left, pltpu.roll(first, HALF, 1), second)
                columns.append(jnp.concatenate([top, bottom], axis=0))
            sides.append(jnp.concatenate(columns, axis=1))
        rows = jnp.concatenate(sides, axis=0).astype(BF16)
        factors = []
        for term in range(terms):
            factors += [packed[term * modes : (term + 1) * modes, :], gap]
        product = dot(rows, jnp.concatenate(factors, axis=0))
        product = product[: 2 * half] + product[2 * half :]
        product = product + pltpu.roll(product, HALF, 1)
        solutions.append(product[:, :modes].astype(BF16))
    return solutions


def advance(sizes, dims, meta_ref, coeffs, residual, near_refs, rows_ref, dual_ref, theirs_ref, direction_ref,
            applied_ref):
    terms, modes = dims
    span = layout_of(terms, modes)["basis"]
    near = [ref[...] for ref in near_refs]
    solutions = solve(coeffs, near, terms, modes)
    mine = dot(solutions[0], rows_ref[residual.shape[0] :, :]).astype(BF16).astype(F32)
    for index, packed in enumerate(near[1:]):
        theirs_ref[index] = dot(solutions[index + 1], packed[span, :]).astype(BF16).astype(F32)
    pieces = []
    for block in range(PLANES + 2):
        if block < PLANES:
            place = slot_of(sizes, meta_ref[0, block])
        else:
            place = min(block, len(near) - 2)
        here = slice(block * LANES, (block + 1) * LANES)
        pieces.append(residual[:, here] + live_mask(meta_ref, block) * (mine[:, here] - theirs_ref[place]))
    direction = jnp.concatenate(pieces, axis=1)
    direction_ref[...] = direction
    applied = dot(direction.astype(BF16), dual_ref[0]).astype(BF16)
    applied_ref[...] = applied
    gamma = jnp.sum(residual * direction, axis=1, keepdims=True)
    delta = 2.0 * jnp.sum(direction * applied.astype(F32), axis=1, keepdims=True)
    half = gamma.shape[0] // 2
    lanes = lane_ids(half)
    sums = jnp.zeros((half, LANES), F32)
    for lane, values in ((GAMMA, gamma), (DELTA, delta)):
        sums = jnp.where(lanes == lane, values[:half], sums)
        sums = jnp.where(lanes == HALF + lane, values[half:], sums)
    return applied, sums


def first_kernel(sizes, dims, layers, count, meta_ref, coeffs_ref, residual_ref, rows_ref, dual_ref, *refs):
    near_refs = refs[:count]
    direction_ref, applied_ref, sums_ref = refs[count : count + 3]
    message_refs, theirs_ref = refs[count + 3 : -1], refs[-1]
    _, sums = advance(
        sizes, dims, meta_ref, coeffs_ref[...], residual_ref[...], near_refs, rows_ref, dual_ref, theirs_ref,
        direction_ref, applied_ref,
    )
    for message_ref, block in zip(message_refs, wanted_blocks(sizes, layers, meta_ref)):
        message_ref[...] = applied_ref[:, lanes_of(block)]
    sums_ref[...] = sums


def steps_from(totals):
    low = totals[:, GAMMA : GAMMA + 1] / totals[:, DELTA : DELTA + 1]
    high = totals[:, HALF + GAMMA : HALF + GAMMA + 1] / totals[:, HALF + DELTA : HALF + DELTA + 1]
    return low, high


def second_kernel(sizes, dims, count, meta_ref, coeffs_ref, change_ref, residual_ref, image_ref, before_ref, rows_ref,
                  dual_ref, *refs):
    near_refs = refs[:count]
    message_ref, residual_out, multipliers_out, direction_ref, applied_ref, theirs_ref = refs[count:]
    half = residual_ref.shape[0] // 2
    change = change_ref[...].reshape(-1, half, LANES)
    low, high = steps_from(jnp.sum(change, axis=0))
    step = jnp.concatenate([low, high], axis=0)
    packed_step = jnp.where(lane_ids(half) < HALF, low, high)
    coeffs = coeffs_ref[...] - (change * packed_step[None]).reshape(coeffs_ref.shape)
    residual = residual_ref[...] - step * image_ref[...]
    residual_out[...] = residual
    multipliers_out[...] = step * before_ref[...]
    applied, sums = advance(
        sizes, dims, meta_ref, coeffs, residual, near_refs, rows_ref, dual_ref, theirs_ref, direction_ref, applied_ref
    )
    top = sums.astype(BF16).astype(F32)
    middle = (sums - top).astype(BF16).astype(F32)
    bottom = sums - top - middle
    coded = (top + pltpu.roll(middle, 2, 1) + pltpu.roll(bottom, 4, 1)).astype(BF16)
    cases = applied.shape[0]
    message_ref[:, :cases, :] = jnp.zeros((message_ref.shape[0], cases, LANES), BF16)
    message_ref[:, cases:, :] = jnp.broadcast_to(coded[None], (message_ref.shape[0], half, LANES))
    post_blocks(message_ref, facing_subs(sizes, meta_ref), applied)


def last_kernel(sizes, meta_ref, arrived_ref, applied_ref, residual_ref, multipliers_ref, direction_ref,
                multipliers_out, residual_out):
    cases = applied_ref.shape[0]
    totals = jnp.sum(arrived_ref[:, cases:, :].astype(F32), axis=0)
    totals = totals + pltpu.roll(totals, LANES - 2, 1) + pltpu.roll(totals, LANES - 4, 1)
    step = jnp.concatenate(steps_from(totals), axis=0)
    facing = [arrived_ref[target, :cases, :] for target in facing_subs(sizes, meta_ref)]
    image, _, _ = difference(meta_ref, applied_ref[...], facing)
    fine = lax.axis_index("fine")
    for block in range(PLANES + 2):
        span = slice(block * LANES, (block + 1) * LANES)
        if block < PLANES:
            sign = jnp.where(fine < meta_ref[0, block], 1.0, -1.0).astype(F32)
        else:
            sign = -1.0 if block == PLANES else 1.0
        multipliers_out[0, :, span] = sign * (multipliers_ref[:, span] + step * direction_ref[:, span])
        residual_out[0, :, span] = sign * (residual_ref[:, span] - step * image[block])


SMEM = pl.BlockSpec(memory_space=pltpu.SMEM)
VMEM = pl.BlockSpec(memory_space=pltpu.VMEM)


HBM = pl.BlockSpec(memory_space=pltpu.HBM)
ANY = pl.BlockSpec(memory_space=pl.ANY)


def call(kernel, name, scalars, arrays, outs, scratch=(), far=(), after=()):
    return pl.pallas_call(
        kernel,
        name=name,
        out_shape=[jax.ShapeDtypeStruct(shape, dtype) for shape, dtype in outs],
        in_specs=[SMEM] * len(scalars) + [VMEM] * len(arrays) + [HBM] * len(far) + [ANY] * len(after),
        out_specs=[VMEM] * len(outs),
        scratch_shapes=list(scratch),
        compiler_params=pltpu.CompilerParams(vmem_limit_bytes=40 * 1024 * 1024),
    )(*scalars, *arrays, *far, *after)


def body(load_cases, dual_ops, coarse_basis, factor_blocks, pattern, partners, row_counts):
    cases, width = load_cases.shape[1:]
    terms, modes = factor_blocks.shape[1:3]
    fine_count = lax.axis_size("fine")
    coarse_count = lax.axis_size("coarse")
    subs = fine_count * coarse_count
    sizes = (fine_count, coarse_count)
    dims = (terms, modes)
    half = cases // 2
    layers = 1 if coarse_count == 2 else 2

    def swap_all(message):
        return lax.all_to_all(message, AXES, 0, 0, tiled=True)

    def swap_slot(message, slot):
        distance = 2 * slot + 1
        pairs = [(i, (i + distance if i % 2 == 0 else i - distance) % fine_count) for i in range(fine_count)]
        return lax.ppermute(message, "fine", pairs)

    def swap_blocks(messages):
        received = [swap_slot(messages[slot], slot) for slot in reversed(range(PLANES))][::-1]
        if layers == 1:
            return received + [lax.ppermute(messages[PLANES], "coarse", [(0, 1), (1, 0)])]
        up = [(i, i + 1) for i in range(coarse_count - 1)]
        lower = lax.ppermute(messages[PLANES + 1], "coarse", up)
        return received + [lower, lax.ppermute(messages[PLANES], "coarse", [(j, i) for i, j in up])]

    full = ((cases, width), F32)
    half_full = ((cases, width), BF16)
    coded = ((subs, half, LANES), F32)
    block = ((cases, LANES), BF16)
    dma = pltpu.SemaphoreType.DMA

    meta = jnp.concatenate([partners, row_counts, pattern], axis=1)
    rows = jnp.concatenate([load_cases[0], coarse_basis[0]], axis=0)
    loads_span = layout_of(terms, modes)["loads"]
    packed = call(
        functools.partial(pack_kernel, sizes, layers, cases),
        "pack_setup",
        (meta,),
        (rows, factor_blocks),
        [((loads_span.stop, LANES), BF16)] * (PLANES + layers),
    )
    received = swap_blocks(packed)
    near = [packed[-1]] + received
    count = len(near)
    theirs = [pltpu.VMEM((count - 1, cases, LANES), F32)]
    landed = [pltpu.VMEM((PLANES, cases, LANES), BF16)]

    residual, message = call(
        functools.partial(restrict_kernel, sizes, layers, loads_span, cases, True),
        "restrict_residual",
        (meta,),
        (rows, *received),
        [full, coded],
        landed,
    )
    coeffs = swap_all(message).reshape(subs * half, LANES)
    [dual] = call(dual_kernel, "fetch_dual", (), (), [(dual_ops.shape, BF16)], [dma((1,))], (dual_ops,), (residual,))

    direction, applied, sums, *messages = call(
        functools.partial(first_kernel, sizes, dims, layers, count),
        "first_direction",
        (meta,),
        (coeffs, residual, rows, dual, *near),
        [full, half_full, ((half, LANES), F32)] + [block] * (PLANES + layers),
        theirs,
    )
    image, message = call(
        functools.partial(restrict_kernel, sizes, layers, slice(0, cases), cases, False),
        "restrict_image",
        (meta,),
        (rows, *swap_blocks(messages), applied, sums),
        [full, coded],
        landed,
    )
    change = swap_all(message).reshape(subs * half, LANES)

    message, residual, multipliers, direction, applied = call(
        functools.partial(second_kernel, sizes, dims, count),
        "second_direction",
        (meta,),
        (coeffs, change, residual, image, direction, rows, dual, *near),
        [((subs, cases + half, LANES), BF16), full, full, full, half_full],
        theirs,
    )
    arrived = swap_all(message)
    out = ((1, cases, width), F32)
    multipliers, residual = call(
        functools.partial(last_kernel, sizes),
        "finish",
        (meta,),
        (arrived, applied, residual, multipliers, direction),
        [out, out],
    )
    return multipliers, residual


def solution(mesh):
    rows = P(AXES, None, None)
    return jax.shard_map(
        body,
        mesh=mesh,
        in_specs=(rows, rows, rows, P(AXES, None, None, None), P(AXES, None), P(AXES, None), P(AXES, None)),
        out_specs=(rows, rows),
        check_vma=False,
    )
```

```python
import functools

import jax
import jax.numpy as jnp
from jax import lax
from jax.experimental import pallas as pl
from jax.experimental.pallas import tpu as pltpu
from jax.sharding import PartitionSpec as P

PLANES = 6
AXES = ("fine", "coarse")
LANES = 128
HALF = 64
BF16 = jnp.bfloat16
F32 = jnp.float32
GAMMA = 48
DELTA = 49


def lane_ids(rows):
    return lax.broadcasted_iota(jnp.int32, (rows, LANES), 1)


def dot(a, b):
    return lax.dot_general(a, b, (((1,), (0,)), ((), ())), preferred_element_type=F32)


def wanted_blocks(sizes, layers, meta_ref):
    slots = [slot_of(sizes, meta_ref[0, b]) for b in range(PLANES)]
    blocks = []
    for slot in range(PLANES):
        blocks.append(sum(jnp.where(slots[b] == slot, b, 0) for b in range(PLANES)))
    if layers == 1:
        return blocks + [jnp.where(lax.axis_index("coarse") == 0, PLANES + 1, PLANES)]
    return blocks + [PLANES, PLANES + 1]


def lanes_of(block):
    start = block * LANES
    return pl.ds(start if isinstance(start, int) else pl.multiple_of(start, LANES), LANES)


def facing_subs(sizes, partners_ref):
    fine_count, coarse_count = sizes
    fine = lax.axis_index("fine")
    coarse = lax.axis_index("coarse")
    me = fine * coarse_count + coarse
    subs = [partners_ref[0, b] * coarse_count + coarse for b in range(PLANES)]
    subs.append(jnp.where(coarse > 0, me - 1, me))
    subs.append(jnp.where(coarse < coarse_count - 1, me + 1, me))
    return subs


def slot_of(sizes, partner):
    fine_count = sizes[0]
    fine = lax.axis_index("fine")
    ahead = jnp.where(fine % 2 == 0, partner - fine, fine - partner)
    ahead = jnp.where(ahead < 0, ahead + fine_count, ahead)
    return PLANES - 1 - (ahead - 1) // 2


def live_mask(counts_ref, block):
    return (lane_ids(1) < counts_ref[0, PLANES + block]).astype(F32)


def post_blocks(out_ref, targets, rows):
    cases = rows.shape[0]
    for block, target in enumerate(targets):
        out_ref[target, :cases, :] = rows[:, block * LANES : (block + 1) * LANES]


def fetch(pairs, sems):
    copies = [pltpu.make_async_copy(source, target, sems.at[i]) for i, (source, target) in enumerate(pairs)]
    for copy in copies:
        copy.start()
    return copies


def pack_kernel(sizes, layers, cases, meta_ref, rows_ref, factors_ref, *outs):
    terms, modes = factors_ref.shape[1:3]
    gap = jnp.zeros((modes, HALF - modes), F32)
    parts = []
    for term in range(terms):
        whole = factors_ref[0, term]
        high = whole.astype(BF16).astype(F32)
        parts.append(jnp.concatenate([high, gap, whole - high, gap], axis=1))
    factors = jnp.concatenate(parts, axis=0).astype(BF16)
    row = lax.broadcasted_iota(jnp.int32, (16, LANES), 0)
    ids = jnp.zeros((16, LANES), F32)
    for term in range(terms):
        sub = meta_ref[0, 2 * PLANES + 2 + term]
        ids = jnp.where(row == term, (sub // 16).astype(F32), ids)
        ids = jnp.where(row == 8 + term, (sub % 16).astype(F32), ids)
    ids = ids.astype(BF16)
    places = layout_of(terms, modes)
    for out_ref, block in zip(outs, wanted_blocks(sizes, layers, meta_ref)):
        out_ref[places["factors"], :] = factors
        out_ref[places["ids"], :] = ids
        out_ref[places["loads"], :] = rows_ref[:cases, lanes_of(block)]
        out_ref[places["basis"], :] = rows_ref[cases:, lanes_of(block)]


def layout_of(terms, modes):
    sizes = (("factors", terms * modes), ("basis", modes), ("ids", 16), ("loads", 16))
    places, start = {}, 0
    for name, rows in sizes:
        places[name] = slice(start, start + rows)
        start += rows
    return places


def dual_kernel(dual_ref, after_ref, out_ref, sems):
    for copy in fetch([(dual_ref, out_ref)], sems):
        copy.wait()


def difference(counts_ref, mine, facing):
    result, ours, theirs = [], [], []
    for block, other in enumerate(facing):
        mask = live_mask(counts_ref, block)
        left = mine[:, block * LANES : (block + 1) * LANES].astype(F32) * mask
        right = other.astype(F32) * mask
        result.append(left - right)
        ours.append(left.astype(BF16))
        theirs.append(right.astype(BF16))
    return result, ours, theirs


def first_restrict_kernel(sizes, dims, layers, meta_ref, rows_ref, *refs):
    near_refs, (_, out_ref, message_ref, scratch_ref) = refs[: PLANES + layers], refs[PLANES + layers :]
    span = layout_of(*dims)["loads"]
    cases = out_ref.shape[0]
    for slot in range(PLANES):
        scratch_ref[slot] = near_refs[slot][span, :]
    facing = [scratch_ref[slot_of(sizes, meta_ref[0, b])] for b in range(PLANES)]
    facing += [near_refs[PLANES][span, :], near_refs[-1][span, :]]
    restrict(meta_ref, rows_ref[:cases, :], facing, rows_ref[cases:, :], None, out_ref, message_ref)


def restrict_kernel(sizes, meta_ref, rows_ref, arrived_ref, applied_ref, sums_ref, out_ref, message_ref):
    facing = [arrived_ref[target] for target in facing_subs(sizes, meta_ref)]
    cases = out_ref.shape[0]
    restrict(meta_ref, applied_ref[...], facing, rows_ref[cases:, :], sums_ref[...], out_ref, message_ref)


def restrict(meta_ref, mine, facing, basis, sums, out_ref, message_ref):
    cases = mine.shape[0]
    modes = basis.shape[0]
    result, ours, theirs = difference(meta_ref, mine, facing)
    for block, values in enumerate(result):
        out_ref[:, block * LANES : (block + 1) * LANES] = values
    both = jnp.concatenate([jnp.concatenate(ours, axis=1), jnp.concatenate(theirs, axis=1)], axis=0)
    gap = jnp.zeros((HALF - modes, basis.shape[1]), BF16)
    twice = jnp.concatenate([basis, gap, basis, gap], axis=0)
    coefficients = lax.dot_general(both, twice, (((1,), (1,)), ((), ())), preferred_element_type=F32)
    coefficients = coefficients[:cases] - coefficients[cases:]
    half = cases // 2
    message = jnp.where(lane_ids(half) < HALF, coefficients[:half], coefficients[half:])
    if sums is not None:
        message = message + sums
    message_ref[...] = jnp.broadcast_to(message[None], message_ref.shape)


def solve(coeffs, near, terms, modes):
    half = 8
    places = layout_of(terms, modes)
    high = coeffs.astype(BF16)
    low = (coeffs - high.astype(F32)).astype(BF16)
    table = jnp.concatenate([high, low], axis=1)
    chunks = coeffs.shape[0] // LANES
    lanes = lane_ids(half).astype(F32)
    step = lax.broadcasted_iota(jnp.int32, (half, LANES), 0).astype(F32)
    picks = []
    for packed in near:
        ids = packed[places["ids"], :].astype(F32)
        ids = (ids[:8] * 16.0 + ids[8:]) * float(half)
        for term in range(terms):
            target = ids[term : term + 1] + step
            picks.append(
                jnp.concatenate([(target == lanes + float(LANES * c)).astype(F32) for c in range(chunks)], axis=1)
            )
    picks = jnp.concatenate(picks, axis=0).astype(BF16)
    picked = dot(picks, table)
    left = lane_ids(half) < HALF
    gap = jnp.zeros((HALF - modes, LANES), BF16)
    solutions = []
    for index, packed in enumerate(near):
        sides = []
        for part in range(2):
            columns = []
            for pair in range(0, terms, 2):
                first, second = [
                    picked[(index * terms + term) * half : (index * terms + term + 1) * half, part * LANES : (part + 1) * LANES]
                    for term in (pair, pair + 1)
                ]
                top = jnp.where(left, first, pltpu.roll(second, HALF, 1))
                bottom = jnp.where(left, pltpu.roll(first, HALF, 1), second)
                columns.append(jnp.concatenate([top, bottom], axis=0))
            sides.append(jnp.concatenate(columns, axis=1))
        rows = jnp.concatenate(sides, axis=0).astype(BF16)
        factors = []
        for term in range(terms):
            factors += [packed[term * modes : (term + 1) * modes, :], gap]
        product = dot(rows, jnp.concatenate(factors, axis=0))
        product = product[: 2 * half] + product[2 * half :]
        product = product + pltpu.roll(product, HALF, 1)
        solutions.append(product[:, :modes].astype(BF16))
    return solutions


def advance(sizes, dims, meta_ref, coeffs, residual, near_refs, rows_ref, dual_ref, theirs_ref, direction_ref,
            applied_ref):
    terms, modes = dims
    span = layout_of(terms, modes)["basis"]
    near = [ref[...] for ref in near_refs]
    solutions = solve(coeffs, near, terms, modes)
    mine = dot(solutions[0], rows_ref[residual.shape[0] :, :]).astype(BF16).astype(F32)
    for index, packed in enumerate(near[1:]):
        theirs_ref[index] = dot(solutions[index + 1], packed[span, :]).astype(BF16).astype(F32)
    pieces = []
    for block in range(PLANES + 2):
        if block < PLANES:
            place = slot_of(sizes, meta_ref[0, block])
        else:
            place = min(block, len(near) - 2)
        here = slice(block * LANES, (block + 1) * LANES)
        pieces.append(residual[:, here] + live_mask(meta_ref, block) * (mine[:, here] - theirs_ref[place]))
    direction = jnp.concatenate(pieces, axis=1)
    direction_ref[...] = direction
    applied = dot(direction.astype(BF16), dual_ref[0]).astype(BF16)
    applied_ref[...] = applied
    gamma = jnp.sum(residual * direction, axis=1, keepdims=True)
    delta = 2.0 * jnp.sum(direction * applied.astype(F32), axis=1, keepdims=True)
    half = gamma.shape[0] // 2
    lanes = lane_ids(half)
    sums = jnp.zeros((half, LANES), F32)
    for lane, values in ((GAMMA, gamma), (DELTA, delta)):
        sums = jnp.where(lanes == lane, values[:half], sums)
        sums = jnp.where(lanes == HALF + lane, values[half:], sums)
    return applied, sums


def first_kernel(sizes, dims, count, meta_ref, coeffs_ref, residual_ref, rows_ref, dual_ref, *refs):
    near_refs = refs[:count]
    message_ref, direction_ref, applied_ref, sums_ref, theirs_ref = refs[count:]
    applied, sums = advance(
        sizes, dims, meta_ref, coeffs_ref[...], residual_ref[...], near_refs, rows_ref, dual_ref, theirs_ref,
        direction_ref, applied_ref,
    )
    message_ref[...] = jnp.zeros_like(message_ref)
    post_blocks(message_ref, facing_subs(sizes, meta_ref), applied)
    sums_ref[...] = sums


def steps_from(totals):
    low = totals[:, GAMMA : GAMMA + 1] / totals[:, DELTA : DELTA + 1]
    high = totals[:, HALF + GAMMA : HALF + GAMMA + 1] / totals[:, HALF + DELTA : HALF + DELTA + 1]
    return low, high


def second_kernel(sizes, dims, count, meta_ref, coeffs_ref, change_ref, residual_ref, image_ref, before_ref, rows_ref,
                  dual_ref, *refs):
    near_refs = refs[:count]
    message_ref, residual_out, multipliers_out, direction_ref, applied_ref, theirs_ref = refs[count:]
    half = residual_ref.shape[0] // 2
    change = change_ref[...].reshape(-1, half, LANES)
    low, high = steps_from(jnp.sum(change, axis=0))
    step = jnp.concatenate([low, high], axis=0)
    packed_step = jnp.where(lane_ids(half) < HALF, low, high)
    coeffs = coeffs_ref[...] - (change * packed_step[None]).reshape(coeffs_ref.shape)
    residual = residual_ref[...] - step * image_ref[...]
    residual_out[...] = residual
    multipliers_out[...] = step * before_ref[...]
    applied, sums = advance(
        sizes, dims, meta_ref, coeffs, residual, near_refs, rows_ref, dual_ref, theirs_ref, direction_ref, applied_ref
    )
    top = sums.astype(BF16).astype(F32)
    middle = (sums - top).astype(BF16).astype(F32)
    bottom = sums - top - middle
    coded = (top + pltpu.roll(middle, 2, 1) + pltpu.roll(bottom, 4, 1)).astype(BF16)
    cases = applied.shape[0]
    message_ref[:, :cases, :] = jnp.zeros((message_ref.shape[0], cases, LANES), BF16)
    message_ref[:, cases:, :] = jnp.broadcast_to(coded[None], (message_ref.shape[0], half, LANES))
    post_blocks(message_ref, facing_subs(sizes, meta_ref), applied)


def last_kernel(sizes, meta_ref, arrived_ref, applied_ref, residual_ref, multipliers_ref, direction_ref,
                multipliers_out, residual_out):
    cases = applied_ref.shape[0]
    totals = jnp.sum(arrived_ref[:, cases:, :].astype(F32), axis=0)
    totals = totals + pltpu.roll(totals, LANES - 2, 1) + pltpu.roll(totals, LANES - 4, 1)
    step = jnp.concatenate(steps_from(totals), axis=0)
    facing = [arrived_ref[target, :cases, :] for target in facing_subs(sizes, meta_ref)]
    image, _, _ = difference(meta_ref, applied_ref[...], facing)
    fine = lax.axis_index("fine")
    for block in range(PLANES + 2):
        span = slice(block * LANES, (block + 1) * LANES)
        if block < PLANES:
            sign = jnp.where(fine < meta_ref[0, block], 1.0, -1.0).astype(F32)
        else:
            sign = -1.0 if block == PLANES else 1.0
        multipliers_out[0, :, span] = sign * (multipliers_ref[:, span] + step * direction_ref[:, span])
        residual_out[0, :, span] = sign * (residual_ref[:, span] - step * image[block])


SMEM = pl.BlockSpec(memory_space=pltpu.SMEM)
VMEM = pl.BlockSpec(memory_space=pltpu.VMEM)


HBM = pl.BlockSpec(memory_space=pltpu.HBM)
ANY = pl.BlockSpec(memory_space=pl.ANY)


def call(kernel, name, scalars, arrays, outs, scratch=(), far=(), after=()):
    return pl.pallas_call(
        kernel,
        name=name,
        out_shape=[jax.ShapeDtypeStruct(shape, dtype) for shape, dtype in outs],
        in_specs=[SMEM] * len(scalars) + [VMEM] * len(arrays) + [HBM] * len(far) + [ANY] * len(after),
        out_specs=[VMEM] * len(outs),
        scratch_shapes=list(scratch),
        compiler_params=pltpu.CompilerParams(vmem_limit_bytes=40 * 1024 * 1024),
    )(*scalars, *arrays, *far, *after)


def body(load_cases, dual_ops, coarse_basis, factor_blocks, pattern, partners, row_counts):
    cases, width = load_cases.shape[1:]
    terms, modes = factor_blocks.shape[1:3]
    fine_count = lax.axis_size("fine")
    coarse_count = lax.axis_size("coarse")
    subs = fine_count * coarse_count
    sizes = (fine_count, coarse_count)
    dims = (terms, modes)
    half = cases // 2
    layers = 1 if coarse_count == 2 else 2

    def swap_all(message):
        return lax.all_to_all(message, AXES, 0, 0, tiled=True)

    def swap_slot(message, slot):
        distance = 2 * (PLANES - slot) - 1
        pairs = [(i, (i + distance if i % 2 == 0 else i - distance) % fine_count) for i in range(fine_count)]
        return lax.ppermute(message, "fine", pairs)

    def swap_blocks(messages):
        received = [swap_slot(messages[slot], slot) for slot in range(PLANES)]
        if layers == 1:
            return received + [lax.ppermute(messages[PLANES], "coarse", [(0, 1), (1, 0)])]
        up = [(i, i + 1) for i in range(coarse_count - 1)]
        lower = lax.ppermute(messages[PLANES + 1], "coarse", up)
        return received + [lower, lax.ppermute(messages[PLANES], "coarse", [(j, i) for i, j in up])]

    full = ((cases, width), F32)
    half_full = ((cases, width), BF16)
    coded = ((subs, half, LANES), F32)
    dma = pltpu.SemaphoreType.DMA

    meta = jnp.concatenate([partners, row_counts, pattern], axis=1)
    rows = jnp.concatenate([load_cases[0], coarse_basis[0]], axis=0)
    loads_span = layout_of(terms, modes)["loads"]
    packed = call(
        functools.partial(pack_kernel, sizes, layers, cases),
        "pack_setup",
        (meta,),
        (rows, factor_blocks),
        [((loads_span.stop, LANES), BF16)] * (PLANES + layers),
    )
    received = swap_blocks(packed)
    near = [packed[-1]] + received
    count = len(near)
    theirs = [pltpu.VMEM((count - 1, cases, LANES), F32)]

    [dual] = call(dual_kernel, "fetch_dual", (), (), [(dual_ops.shape, BF16)], [dma((1,))], (dual_ops,), (packed[-1],))
    residual, message = call(
        functools.partial(first_restrict_kernel, sizes, dims, layers),
        "restrict_residual",
        (meta,),
        (rows, *received),
        [full, coded],
        [pltpu.VMEM((PLANES, cases, LANES), BF16)],
        after=(dual,),
    )
    coeffs = swap_all(message).reshape(subs * half, LANES)

    message, direction, applied, sums = call(
        functools.partial(first_kernel, sizes, dims, count),
        "first_direction",
        (meta,),
        (coeffs, residual, rows, dual, *near),
        [((subs, cases, LANES), BF16), full, half_full, ((half, LANES), F32)],
        theirs,
    )
    image, message = call(
        functools.partial(restrict_kernel, sizes),
        "restrict_image",
        (meta,),
        (rows, swap_all(message), applied, sums),
        [full, coded],
    )
    change = swap_all(message).reshape(subs * half, LANES)

    message, residual, multipliers, direction, applied = call(
        functools.partial(second_kernel, sizes, dims, count),
        "second_direction",
        (meta,),
        (coeffs, change, residual, image, direction, rows, dual, *near),
        [((subs, cases + half, LANES), BF16), full, full, full, half_full],
        theirs,
    )
    arrived = swap_all(message)
    out = ((1, cases, width), F32)
    multipliers, residual = call(
        functools.partial(last_kernel, sizes),
        "finish",
        (meta,),
        (arrived, applied, residual, multipliers, direction),
        [out, out],
    )
    return multipliers, residual


def solution(mesh):
    rows = P(AXES, None, None)
    return jax.shard_map(
        body,
        mesh=mesh,
        in_specs=(rows, rows, rows, P(AXES, None, None, None), P(AXES, None), P(AXES, None), P(AXES, None)),
        out_specs=(rows, rows),
        check_vma=False,
    )
```

```python
import functools

import jax
import jax.numpy as jnp
from jax import lax
from jax.experimental import pallas as pl
from jax.experimental.pallas import tpu as pltpu
from jax.sharding import PartitionSpec as P

PLANES = 6
AXES = ("fine", "coarse")
LANES = 128
HALF = 64
BF16 = jnp.bfloat16
F32 = jnp.float32
GAMMA = 48
DELTA = 49


def lane_ids(rows):
    return lax.broadcasted_iota(jnp.int32, (rows, LANES), 1)


def dot(a, b):
    return lax.dot_general(a, b, (((1,), (0,)), ((), ())), preferred_element_type=F32)


def wanted_blocks(sizes, layers, meta_ref):
    slots = [slot_of(sizes, meta_ref[0, b]) for b in range(PLANES)]
    blocks = []
    for slot in range(PLANES):
        blocks.append(sum(jnp.where(slots[b] == slot, b, 0) for b in range(PLANES)))
    if layers == 1:
        return blocks + [jnp.where(lax.axis_index("coarse") == 0, PLANES + 1, PLANES)]
    return blocks + [PLANES, PLANES + 1]


def lanes_of(block):
    start = block * LANES
    return pl.ds(start if isinstance(start, int) else pl.multiple_of(start, LANES), LANES)


def facing_subs(sizes, partners_ref):
    fine_count, coarse_count = sizes
    fine = lax.axis_index("fine")
    coarse = lax.axis_index("coarse")
    me = fine * coarse_count + coarse
    subs = [partners_ref[0, b] * coarse_count + coarse for b in range(PLANES)]
    subs.append(jnp.where(coarse > 0, me - 1, me))
    subs.append(jnp.where(coarse < coarse_count - 1, me + 1, me))
    return subs


def slot_of(sizes, partner):
    fine_count = sizes[0]
    fine = lax.axis_index("fine")
    ahead = jnp.where(fine % 2 == 0, partner - fine, fine - partner)
    ahead = jnp.where(ahead < 0, ahead + fine_count, ahead)
    return PLANES - 1 - (ahead - 1) // 2


def live_mask(counts_ref, block):
    return (lane_ids(1) < counts_ref[0, PLANES + block]).astype(F32)


def post_blocks(out_ref, targets, rows):
    cases = rows.shape[0]
    for block, target in enumerate(targets):
        out_ref[target, :cases, :] = rows[:, block * LANES : (block + 1) * LANES]


def fetch(pairs, sems):
    copies = [pltpu.make_async_copy(source, target, sems.at[i]) for i, (source, target) in enumerate(pairs)]
    for copy in copies:
        copy.start()
    return copies


def pack_kernel(sizes, layers, cases, meta_ref, rows_ref, factors_ref, *outs):
    terms, modes = factors_ref.shape[1:3]
    gap = jnp.zeros((modes, HALF - modes), F32)
    parts = []
    for term in range(terms):
        whole = factors_ref[0, term]
        high = whole.astype(BF16).astype(F32)
        parts.append(jnp.concatenate([high, gap, whole - high, gap], axis=1))
    factors = jnp.concatenate(parts, axis=0).astype(BF16)
    row = lax.broadcasted_iota(jnp.int32, (16, LANES), 0)
    ids = jnp.zeros((16, LANES), F32)
    for term in range(terms):
        sub = meta_ref[0, 2 * PLANES + 2 + term]
        ids = jnp.where(row == term, (sub // 16).astype(F32), ids)
        ids = jnp.where(row == 8 + term, (sub % 16).astype(F32), ids)
    ids = ids.astype(BF16)
    places = layout_of(terms, modes)
    for out_ref, block in zip(outs, wanted_blocks(sizes, layers, meta_ref)):
        out_ref[places["factors"], :] = factors
        out_ref[places["ids"], :] = ids
        out_ref[places["loads"], :] = rows_ref[:cases, lanes_of(block)]
        out_ref[places["basis"], :] = rows_ref[cases:, lanes_of(block)]


def layout_of(terms, modes):
    sizes = (("factors", terms * modes), ("basis", modes), ("ids", 16), ("loads", 16))
    places, start = {}, 0
    for name, rows in sizes:
        places[name] = slice(start, start + rows)
        start += rows
    return places


def dual_kernel(dual_ref, after_ref, out_ref, sems):
    for copy in fetch([(dual_ref, out_ref)], sems):
        copy.wait()


def difference(counts_ref, mine, facing):
    result, ours, theirs = [], [], []
    for block, other in enumerate(facing):
        mask = live_mask(counts_ref, block)
        left = mine[:, block * LANES : (block + 1) * LANES].astype(F32) * mask
        right = other.astype(F32) * mask
        result.append(left - right)
        ours.append(left.astype(BF16))
        theirs.append(right.astype(BF16))
    return result, ours, theirs


def first_restrict_kernel(sizes, dims, layers, meta_ref, rows_ref, *refs):
    near_refs, (_, out_ref, message_ref, scratch_ref) = refs[: PLANES + layers], refs[PLANES + layers :]
    span = layout_of(*dims)["loads"]
    cases = out_ref.shape[0]
    for slot in range(PLANES):
        scratch_ref[slot] = near_refs[slot][span, :]
    facing = [scratch_ref[slot_of(sizes, meta_ref[0, b])] for b in range(PLANES)]
    facing += [near_refs[PLANES][span, :], near_refs[-1][span, :]]
    restrict(meta_ref, rows_ref[:cases, :], facing, rows_ref[cases:, :], out_ref, message_ref)


def twice(basis):
    gap = jnp.zeros((HALF - basis.shape[0], basis.shape[1]), BF16)
    return jnp.concatenate([basis, gap, basis, gap], axis=0)


def times_basis(rows, doubled):
    return lax.dot_general(rows, doubled, (((1,), (1,)), ((), ())), preferred_element_type=F32)


def fold(coefficients):
    half = coefficients.shape[0] // 2
    return jnp.where(lane_ids(half) < HALF, coefficients[:half], coefficients[half:])


def encode(sums):
    top = sums.astype(BF16).astype(F32)
    middle = (sums - top).astype(BF16).astype(F32)
    bottom = sums - top - middle
    return top + pltpu.roll(middle, 2, 1) + pltpu.roll(bottom, 4, 1)


def decode(totals):
    return totals + pltpu.roll(totals, LANES - 2, 1) + pltpu.roll(totals, LANES - 4, 1)


def restrict(meta_ref, mine, facing, basis, out_ref, message_ref):
    cases = mine.shape[0]
    result, ours, theirs = difference(meta_ref, mine, facing)
    for block, values in enumerate(result):
        out_ref[:, block * LANES : (block + 1) * LANES] = values
    both = jnp.concatenate([jnp.concatenate(ours, axis=1), jnp.concatenate(theirs, axis=1)], axis=0)
    coefficients = times_basis(both, twice(basis))
    message = fold(coefficients[:cases] - coefficients[cases:])
    message_ref[...] = jnp.broadcast_to(message[None], message_ref.shape)


def shares(sizes, dims, layers, meta_ref, applied_ref, near_refs, rows_ref, sums):
    cases = applied_ref.shape[0]
    span = layout_of(*dims)["basis"]
    masked = []
    for block in range(PLANES + 2):
        part = applied_ref[:, block * LANES : (block + 1) * LANES].astype(F32)
        masked.append((part * live_mask(meta_ref, block)).astype(BF16))
    own = fold(times_basis(jnp.concatenate(masked, axis=1), twice(rows_ref[cases:, :])))
    high = own.astype(BF16).astype(F32)
    tiles = [high + encode(sums), own - high]
    for near_ref, block in zip(near_refs[1:], wanted_blocks(sizes, layers, meta_ref)):
        part = applied_ref[:, lanes_of(block)].astype(F32) * live_mask(meta_ref, block)
        tiles.append(fold(times_basis(part.astype(BF16), twice(near_ref[span, :]))))
    return jnp.concatenate(tiles, axis=0).astype(BF16)


def collect(sizes, layers, cases, own_ref, others_ref, changes_ref):
    fine_count, coarse_count = sizes
    half = cases // 2
    coarse = lax.axis_index("coarse")

    def tile(layer, fine, index):
        rows = slice(cases + index * half, cases + (index + 1) * half)
        if layers == 1:
            source = own_ref if layer == 0 else others_ref
            return source[fine, rows, :].astype(F32)
        return others_ref[layer, fine, rows, :].astype(F32)

    def one(fine, totals):
        for layer in range(coarse_count):
            first = tile(layer, fine, 0)
            totals = totals + first
            value = first + tile(layer, fine, 1)
            for slot in range(PLANES):
                distance = 2 * (PLANES - slot) - 1
                partner = jnp.where(fine % 2 == 0, fine + distance, fine - distance) if layers > 1 else (
                    fine + distance if fine % 2 == 0 else fine - distance
                )
                value = value - tile(layer, (partner + fine_count) % fine_count, 2 + slot)
            if layers == 1:
                value = value - tile(1 - layer, fine, 2 + PLANES)
                place = fine * 2 + (coarse if layer == 0 else 1 - coarse)
            else:
                if layer > 0:
                    value = value - tile(layer - 1, fine, 3 + PLANES)
                if layer < coarse_count - 1:
                    value = value - tile(layer + 1, fine, 2 + PLANES)
                place = fine * coarse_count + layer
            changes_ref[place] = value
        return totals

    totals = jnp.zeros((half, LANES), F32)
    if layers > 1:
        return decode(lax.fori_loop(0, fine_count, one, totals))
    for fine in range(fine_count):
        totals = one(fine, totals)
    return decode(totals)


def solve(coeffs, near, terms, modes):
    half = 8
    places = layout_of(terms, modes)
    high = coeffs.astype(BF16)
    low = (coeffs - high.astype(F32)).astype(BF16)
    table = jnp.concatenate([high, low], axis=1)
    chunks = coeffs.shape[0] // LANES
    lanes = lane_ids(half).astype(F32)
    step = lax.broadcasted_iota(jnp.int32, (half, LANES), 0).astype(F32)
    picks = []
    for packed in near:
        ids = packed[places["ids"], :].astype(F32)
        ids = (ids[:8] * 16.0 + ids[8:]) * float(half)
        for term in range(terms):
            target = ids[term : term + 1] + step
            picks.append(
                jnp.concatenate([(target == lanes + float(LANES * c)).astype(F32) for c in range(chunks)], axis=1)
            )
    picks = jnp.concatenate(picks, axis=0).astype(BF16)
    picked = dot(picks, table)
    left = lane_ids(half) < HALF
    gap = jnp.zeros((HALF - modes, LANES), BF16)
    solutions = []
    for index, packed in enumerate(near):
        sides = []
        for part in range(2):
            columns = []
            for pair in range(0, terms, 2):
                first, second = [
                    picked[(index * terms + term) * half : (index * terms + term + 1) * half, part * LANES : (part + 1) * LANES]
                    for term in (pair, pair + 1)
                ]
                top = jnp.where(left, first, pltpu.roll(second, HALF, 1))
                bottom = jnp.where(left, pltpu.roll(first, HALF, 1), second)
                columns.append(jnp.concatenate([top, bottom], axis=0))
            sides.append(jnp.concatenate(columns, axis=1))
        rows = jnp.concatenate(sides, axis=0).astype(BF16)
        factors = []
        for term in range(terms):
            factors += [packed[term * modes : (term + 1) * modes, :], gap]
        product = dot(rows, jnp.concatenate(factors, axis=0))
        product = product[: 2 * half] + product[2 * half :]
        product = product + pltpu.roll(product, HALF, 1)
        solutions.append(product[:, :modes].astype(BF16))
    return solutions


def advance(sizes, dims, meta_ref, coeffs, residual, near_refs, rows_ref, dual_ref, theirs_ref, direction_ref,
            applied_ref):
    terms, modes = dims
    span = layout_of(terms, modes)["basis"]
    near = [ref[...] for ref in near_refs]
    solutions = solve(coeffs, near, terms, modes)
    mine = dot(solutions[0], rows_ref[residual.shape[0] :, :]).astype(BF16).astype(F32)
    for index, packed in enumerate(near[1:]):
        theirs_ref[index] = dot(solutions[index + 1], packed[span, :]).astype(BF16).astype(F32)
    pieces = []
    for block in range(PLANES + 2):
        if block < PLANES:
            place = slot_of(sizes, meta_ref[0, block])
        else:
            place = min(block, len(near) - 2)
        here = slice(block * LANES, (block + 1) * LANES)
        pieces.append(residual[:, here] + live_mask(meta_ref, block) * (mine[:, here] - theirs_ref[place]))
    direction = jnp.concatenate(pieces, axis=1)
    direction_ref[...] = direction
    applied = dot(direction.astype(BF16), dual_ref[0]).astype(BF16)
    applied_ref[...] = applied
    gamma = jnp.sum(residual * direction, axis=1, keepdims=True)
    delta = 2.0 * jnp.sum(direction * applied.astype(F32), axis=1, keepdims=True)
    half = gamma.shape[0] // 2
    lanes = lane_ids(half)
    sums = jnp.zeros((half, LANES), F32)
    for lane, values in ((GAMMA, gamma), (DELTA, delta)):
        sums = jnp.where(lanes == lane, values[:half], sums)
        sums = jnp.where(lanes == HALF + lane, values[half:], sums)
    return applied, sums


def first_kernel(sizes, dims, layers, count, meta_ref, coeffs_ref, residual_ref, rows_ref, dual_ref, *refs):
    near_refs = refs[:count]
    message_ref, direction_ref, applied_ref, theirs_ref = refs[count:]
    applied, sums = advance(
        sizes, dims, meta_ref, coeffs_ref[...], residual_ref[...], near_refs, rows_ref, dual_ref, theirs_ref,
        direction_ref, applied_ref,
    )
    cases = applied.shape[0]
    tiles = shares(sizes, dims, layers, meta_ref, applied_ref, near_refs, rows_ref, sums)
    message_ref[:, :cases, :] = jnp.zeros((message_ref.shape[0], cases, LANES), BF16)
    message_ref[:, cases:, :] = jnp.broadcast_to(tiles[None], (message_ref.shape[0],) + tiles.shape)
    post_blocks(message_ref, [meta_ref[0, b] for b in range(PLANES)], applied)
    if layers == 1:
        block = wanted_blocks(sizes, layers, meta_ref)[-1]
        message_ref[lax.axis_index("fine"), :cases, :] = applied_ref[:, lanes_of(block)]


def steps_from(totals):
    low = totals[:, GAMMA : GAMMA + 1] / totals[:, DELTA : DELTA + 1]
    high = totals[:, HALF + GAMMA : HALF + GAMMA + 1] / totals[:, HALF + DELTA : HALF + DELTA + 1]
    return low, high


def second_kernel(sizes, dims, layers, count, meta_ref, coeffs_ref, residual_ref, before_ref, applied_before_ref,
                  rows_ref, dual_ref, own_ref, *refs):
    others_refs, refs = refs[: 1 if layers == 1 else 3], refs[1 if layers == 1 else 3 :]
    near_refs = refs[:count]
    message_ref, residual_out, multipliers_out, direction_ref, applied_ref, theirs_ref, changes_ref = refs[count:]
    cases = residual_ref.shape[0]
    half = cases // 2
    low, high = steps_from(collect(sizes, layers, cases, own_ref, others_refs[0], changes_ref))
    step = jnp.concatenate([low, high], axis=0)
    packed_step = jnp.where(lane_ids(half) < HALF, low, high)
    coeffs = coeffs_ref[...] - (changes_ref[...] * packed_step[None]).reshape(coeffs_ref.shape)
    facing = [own_ref[meta_ref[0, b], :cases, :] for b in range(PLANES)]
    if layers == 1:
        facing += [others_refs[0][lax.axis_index("fine"), :cases, :]] * 2
    else:
        facing += [ref[...] for ref in others_refs[1:]]
    image, _, _ = difference(meta_ref, applied_before_ref[...], facing)
    residual = residual_ref[...] - step * jnp.concatenate(image, axis=1)
    residual_out[...] = residual
    multipliers_out[...] = step * before_ref[...]
    applied, sums = advance(
        sizes, dims, meta_ref, coeffs, residual, near_refs, rows_ref, dual_ref, theirs_ref, direction_ref, applied_ref
    )
    message_ref[:, :cases, :] = jnp.zeros((message_ref.shape[0], cases, LANES), BF16)
    message_ref[:, cases:, :] = jnp.broadcast_to(encode(sums).astype(BF16)[None], (message_ref.shape[0], half, LANES))
    post_blocks(message_ref, facing_subs(sizes, meta_ref), applied)


def last_kernel(sizes, meta_ref, arrived_ref, applied_ref, residual_ref, multipliers_ref, direction_ref,
                multipliers_out, residual_out):
    cases = applied_ref.shape[0]
    totals = jnp.sum(arrived_ref[:, cases:, :].astype(F32), axis=0)
    step = jnp.concatenate(steps_from(decode(totals)), axis=0)
    facing = [arrived_ref[target, :cases, :] for target in facing_subs(sizes, meta_ref)]
    image, _, _ = difference(meta_ref, applied_ref[...], facing)
    fine = lax.axis_index("fine")
    for block in range(PLANES + 2):
        span = slice(block * LANES, (block + 1) * LANES)
        if block < PLANES:
            sign = jnp.where(fine < meta_ref[0, block], 1.0, -1.0).astype(F32)
        else:
            sign = -1.0 if block == PLANES else 1.0
        multipliers_out[0, :, span] = sign * (multipliers_ref[:, span] + step * direction_ref[:, span])
        residual_out[0, :, span] = sign * (residual_ref[:, span] - step * image[block])


SMEM = pl.BlockSpec(memory_space=pltpu.SMEM)
VMEM = pl.BlockSpec(memory_space=pltpu.VMEM)


HBM = pl.BlockSpec(memory_space=pltpu.HBM)
ANY = pl.BlockSpec(memory_space=pl.ANY)


def call(kernel, name, scalars, arrays, outs, scratch=(), far=(), after=()):
    return pl.pallas_call(
        kernel,
        name=name,
        out_shape=[jax.ShapeDtypeStruct(shape, dtype) for shape, dtype in outs],
        in_specs=[SMEM] * len(scalars) + [VMEM] * len(arrays) + [HBM] * len(far) + [ANY] * len(after),
        out_specs=[VMEM] * len(outs),
        scratch_shapes=list(scratch),
        compiler_params=pltpu.CompilerParams(vmem_limit_bytes=40 * 1024 * 1024),
    )(*scalars, *arrays, *far, *after)


def body(load_cases, dual_ops, coarse_basis, factor_blocks, pattern, partners, row_counts):
    cases, width = load_cases.shape[1:]
    terms, modes = factor_blocks.shape[1:3]
    fine_count = lax.axis_size("fine")
    coarse_count = lax.axis_size("coarse")
    subs = fine_count * coarse_count
    sizes = (fine_count, coarse_count)
    dims = (terms, modes)
    half = cases // 2
    layers = 1 if coarse_count == 2 else 2

    def swap_all(message):
        return lax.all_to_all(message, AXES, 0, 0, tiled=True)

    def swap_slot(message, slot):
        distance = 2 * (PLANES - slot) - 1
        pairs = [(i, (i + distance if i % 2 == 0 else i - distance) % fine_count) for i in range(fine_count)]
        return lax.ppermute(message, "fine", pairs)

    def swap_blocks(messages):
        received = [swap_slot(messages[slot], slot) for slot in range(PLANES)]
        if layers == 1:
            return received + [lax.ppermute(messages[PLANES], "coarse", [(0, 1), (1, 0)])]
        up = [(i, i + 1) for i in range(coarse_count - 1)]
        lower = lax.ppermute(messages[PLANES + 1], "coarse", up)
        return received + [lower, lax.ppermute(messages[PLANES], "coarse", [(j, i) for i, j in up])]

    full = ((cases, width), F32)
    half_full = ((cases, width), BF16)
    coded = ((subs, half, LANES), F32)
    dma = pltpu.SemaphoreType.DMA

    meta = jnp.concatenate([partners, row_counts, pattern], axis=1)
    rows = jnp.concatenate([load_cases[0], coarse_basis[0]], axis=0)
    loads_span = layout_of(terms, modes)["loads"]
    packed = call(
        functools.partial(pack_kernel, sizes, layers, cases),
        "pack_setup",
        (meta,),
        (rows, factor_blocks),
        [((loads_span.stop, LANES), BF16)] * (PLANES + layers),
    )
    received = swap_blocks(packed)
    near = [packed[-1]] + received
    count = len(near)
    theirs = [pltpu.VMEM((count - 1, cases, LANES), F32)]

    [dual] = call(dual_kernel, "fetch_dual", (), (), [(dual_ops.shape, BF16)], [dma((1,))], (dual_ops,), (packed[-1],))
    residual, message = call(
        functools.partial(first_restrict_kernel, sizes, dims, layers),
        "restrict_residual",
        (meta,),
        (rows, *received),
        [full, coded],
        [pltpu.VMEM((PLANES, cases, LANES), BF16)],
        after=(dual,),
    )
    coeffs = swap_all(message).reshape(subs * half, LANES)

    tiles = 2 + PLANES + layers
    message, direction, applied = call(
        functools.partial(first_kernel, sizes, dims, layers, count),
        "first_direction",
        (meta,),
        (coeffs, residual, rows, dual, *near),
        [((fine_count, cases + tiles * half, LANES), BF16), full, half_full],
        theirs,
    )
    own = lax.all_to_all(message, "fine", 0, 0, tiled=True)
    if layers == 1:
        others = [lax.ppermute(own, "coarse", [(0, 1), (1, 0)])]
    else:
        up = [(i, i + 1) for i in range(coarse_count - 1)]
        lower = lax.ppermute(applied[:, (PLANES + 1) * LANES :], "coarse", up)
        upper = lax.ppermute(applied[:, PLANES * LANES : (PLANES + 1) * LANES], "coarse", [(j, i) for i, j in up])
        others = [lax.all_gather(own, "coarse"), lower, upper]

    message, residual, multipliers, direction, applied = call(
        functools.partial(second_kernel, sizes, dims, layers, count),
        "second_direction",
        (meta,),
        (coeffs, residual, direction, applied, rows, dual, own, *others, *near),
        [((subs, cases + half, LANES), BF16), full, full, full, half_full],
        theirs + [pltpu.VMEM((subs, half, LANES), F32)],
    )
    arrived = swap_all(message)
    out = ((1, cases, width), F32)
    multipliers, residual = call(
        functools.partial(last_kernel, sizes),
        "finish",
        (meta,),
        (arrived, applied, residual, multipliers, direction),
        [out, out],
    )
    return multipliers, residual


def solution(mesh):
    rows = P(AXES, None, None)
    return jax.shard_map(
        body,
        mesh=mesh,
        in_specs=(rows, rows, rows, P(AXES, None, None, None), P(AXES, None), P(AXES, None), P(AXES, None)),
        out_specs=(rows, rows),
        check_vma=False,
    )
```

```python
import functools

import jax
import jax.numpy as jnp
from jax import lax
from jax.experimental import pallas as pl
from jax.experimental.pallas import tpu as pltpu
from jax.sharding import PartitionSpec as P

PLANES = 6
AXES = ("fine", "coarse")
LANES = 128
HALF = 64
BF16 = jnp.bfloat16
F32 = jnp.float32
GAMMA = 48
DELTA = 49


def lane_ids(rows):
    return lax.broadcasted_iota(jnp.int32, (rows, LANES), 1)


def dot(a, b):
    return lax.dot_general(a, b, (((1,), (0,)), ((), ())), preferred_element_type=F32)


def wanted_blocks(sizes, layers, meta_ref):
    slots = [slot_of(sizes, meta_ref[0, b]) for b in range(PLANES)]
    blocks = []
    for slot in range(PLANES):
        blocks.append(sum(jnp.where(slots[b] == slot, b, 0) for b in range(PLANES)))
    if layers == 1:
        return blocks + [jnp.where(lax.axis_index("coarse") == 0, PLANES + 1, PLANES)]
    return blocks + [PLANES, PLANES + 1]


def lanes_of(block):
    start = block * LANES
    return pl.ds(start if isinstance(start, int) else pl.multiple_of(start, LANES), LANES)


def facing_subs(sizes, partners_ref):
    fine_count, coarse_count = sizes
    fine = lax.axis_index("fine")
    coarse = lax.axis_index("coarse")
    me = fine * coarse_count + coarse
    subs = [partners_ref[0, b] * coarse_count + coarse for b in range(PLANES)]
    subs.append(jnp.where(coarse > 0, me - 1, me))
    subs.append(jnp.where(coarse < coarse_count - 1, me + 1, me))
    return subs


def slot_of(sizes, partner):
    fine_count = sizes[0]
    fine = lax.axis_index("fine")
    ahead = jnp.where(fine % 2 == 0, partner - fine, fine - partner)
    ahead = jnp.where(ahead < 0, ahead + fine_count, ahead)
    return PLANES - 1 - (ahead - 1) // 2


def live_mask(counts_ref, block):
    return (lane_ids(1) < counts_ref[0, PLANES + block]).astype(F32)


def post_blocks(out_ref, targets, rows):
    cases = rows.shape[0]
    for block, target in enumerate(targets):
        out_ref[target, :cases, :] = rows[:, block * LANES : (block + 1) * LANES]


def post_plane(sizes, layers, meta_ref, rows_ref, message_ref):
    cases = rows_ref.shape[0]
    message_ref[:, :cases, :] = jnp.zeros((message_ref.shape[0], cases, LANES), BF16)
    if layers == 1:
        block = wanted_blocks(sizes, layers, meta_ref)[-1]
        message_ref[lax.axis_index("fine"), :cases, :] = rows_ref[:, lanes_of(block)]
        targets = [meta_ref[0, b] for b in range(PLANES)]
    else:
        targets = facing_subs(sizes, meta_ref)
    post_blocks(message_ref, targets, rows_ref[...])


def facing_plane(meta_ref, own_ref, other_ref, cases):
    facing = [own_ref[meta_ref[0, b], :cases, :] for b in range(PLANES)]
    return facing + [other_ref[lax.axis_index("fine"), :cases, :]] * 2


def fetch(pairs, sems):
    copies = [pltpu.make_async_copy(source, target, sems.at[i]) for i, (source, target) in enumerate(pairs)]
    for copy in copies:
        copy.start()
    return copies


def pack_kernel(sizes, layers, cases, meta_ref, rows_ref, factors_ref, *outs):
    terms, modes = factors_ref.shape[1:3]
    gap = jnp.zeros((modes, HALF - modes), F32)
    parts = []
    for term in range(terms):
        whole = factors_ref[0, term]
        high = whole.astype(BF16).astype(F32)
        parts.append(jnp.concatenate([high, gap, whole - high, gap], axis=1))
    factors = jnp.concatenate(parts, axis=0).astype(BF16)
    row = lax.broadcasted_iota(jnp.int32, (16, LANES), 0)
    ids = jnp.zeros((16, LANES), F32)
    for term in range(terms):
        sub = meta_ref[0, 2 * PLANES + 2 + term]
        ids = jnp.where(row == term, (sub // 16).astype(F32), ids)
        ids = jnp.where(row == 8 + term, (sub % 16).astype(F32), ids)
    ids = ids.astype(BF16)
    places = layout_of(terms, modes)
    for out_ref, block in zip(outs, wanted_blocks(sizes, layers, meta_ref)):
        out_ref[places["factors"], :] = factors
        out_ref[places["ids"], :] = ids
        out_ref[places["loads"], :] = rows_ref[:cases, lanes_of(block)]
        out_ref[places["basis"], :] = rows_ref[cases:, lanes_of(block)]


def layout_of(terms, modes):
    sizes = (("factors", terms * modes), ("basis", modes), ("ids", 16), ("loads", 16))
    places, start = {}, 0
    for name, rows in sizes:
        places[name] = slice(start, start + rows)
        start += rows
    return places


def dual_kernel(dual_ref, after_ref, out_ref, sems):
    for copy in fetch([(dual_ref, out_ref)], sems):
        copy.wait()


def difference(counts_ref, mine, facing):
    result, ours, theirs = [], [], []
    for block, other in enumerate(facing):
        mask = live_mask(counts_ref, block)
        left = mine[:, block * LANES : (block + 1) * LANES].astype(F32) * mask
        right = other.astype(F32) * mask
        result.append(left - right)
        ours.append(left.astype(BF16))
        theirs.append(right.astype(BF16))
    return result, ours, theirs


def first_restrict_kernel(sizes, dims, layers, meta_ref, rows_ref, *refs):
    near_refs, (_, out_ref, message_ref, scratch_ref) = refs[: PLANES + layers], refs[PLANES + layers :]
    span = layout_of(*dims)["loads"]
    cases = out_ref.shape[0]
    for slot in range(PLANES):
        scratch_ref[slot] = near_refs[slot][span, :]
    facing = [scratch_ref[slot_of(sizes, meta_ref[0, b])] for b in range(PLANES)]
    facing += [near_refs[PLANES][span, :], near_refs[-1][span, :]]
    restrict(meta_ref, rows_ref[:cases, :], facing, rows_ref[cases:, :], out_ref, message_ref)


def twice(basis):
    gap = jnp.zeros((HALF - basis.shape[0], basis.shape[1]), BF16)
    return jnp.concatenate([basis, gap, basis, gap], axis=0)


def times_basis(rows, doubled):
    return lax.dot_general(rows, doubled, (((1,), (1,)), ((), ())), preferred_element_type=F32)


def fold(coefficients):
    half = coefficients.shape[0] // 2
    return jnp.where(lane_ids(half) < HALF, coefficients[:half], coefficients[half:])


def encode(sums):
    top = sums.astype(BF16).astype(F32)
    middle = (sums - top).astype(BF16).astype(F32)
    bottom = sums - top - middle
    return top + pltpu.roll(middle, 2, 1) + pltpu.roll(bottom, 4, 1)


def decode(totals):
    return totals + pltpu.roll(totals, LANES - 2, 1) + pltpu.roll(totals, LANES - 4, 1)


def restrict(meta_ref, mine, facing, basis, out_ref, message_ref):
    cases = mine.shape[0]
    result, ours, theirs = difference(meta_ref, mine, facing)
    for block, values in enumerate(result):
        out_ref[:, block * LANES : (block + 1) * LANES] = values
    both = jnp.concatenate([jnp.concatenate(ours, axis=1), jnp.concatenate(theirs, axis=1)], axis=0)
    coefficients = times_basis(both, twice(basis))
    message = fold(coefficients[:cases] - coefficients[cases:])
    message_ref[...] = jnp.broadcast_to(message[None], message_ref.shape)


def shares(sizes, dims, layers, meta_ref, applied_ref, near_refs, rows_ref, sums):
    cases = applied_ref.shape[0]
    span = layout_of(*dims)["basis"]
    masked = []
    for block in range(PLANES + 2):
        part = applied_ref[:, block * LANES : (block + 1) * LANES].astype(F32)
        masked.append((part * live_mask(meta_ref, block)).astype(BF16))
    own = fold(times_basis(jnp.concatenate(masked, axis=1), twice(rows_ref[cases:, :])))
    high = own.astype(BF16).astype(F32)
    tiles = [high + encode(sums), own - high]
    for near_ref, block in zip(near_refs[1:], wanted_blocks(sizes, layers, meta_ref)):
        part = applied_ref[:, lanes_of(block)].astype(F32) * live_mask(meta_ref, block)
        tiles.append(fold(times_basis(part.astype(BF16), twice(near_ref[span, :]))))
    return jnp.concatenate(tiles, axis=0).astype(BF16)


def collect(sizes, layers, cases, own_ref, others_ref, changes_ref):
    fine_count, coarse_count = sizes
    half = cases // 2
    coarse = lax.axis_index("coarse")

    def tile(layer, fine, index):
        rows = slice(cases + index * half, cases + (index + 1) * half)
        if layers == 1:
            source = own_ref if layer == 0 else others_ref
            return source[fine, rows, :].astype(F32)
        return others_ref[layer, fine, rows, :].astype(F32)

    def one(fine, totals):
        for layer in range(coarse_count):
            first = tile(layer, fine, 0)
            totals = totals + first
            value = first + tile(layer, fine, 1)
            for slot in range(PLANES):
                distance = 2 * (PLANES - slot) - 1
                partner = jnp.where(fine % 2 == 0, fine + distance, fine - distance) if layers > 1 else (
                    fine + distance if fine % 2 == 0 else fine - distance
                )
                value = value - tile(layer, (partner + fine_count) % fine_count, 2 + slot)
            if layers == 1:
                value = value - tile(1 - layer, fine, 2 + PLANES)
                place = fine * 2 + (coarse if layer == 0 else 1 - coarse)
            else:
                if layer > 0:
                    value = value - tile(layer - 1, fine, 3 + PLANES)
                if layer < coarse_count - 1:
                    value = value - tile(layer + 1, fine, 2 + PLANES)
                place = fine * coarse_count + layer
            changes_ref[place] = value
        return totals

    totals = jnp.zeros((half, LANES), F32)
    if layers > 1:
        return decode(lax.fori_loop(0, fine_count, one, totals))
    for fine in range(fine_count):
        totals = one(fine, totals)
    return decode(totals)


def solve(coeffs, near, terms, modes):
    half = 8
    places = layout_of(terms, modes)
    high = coeffs.astype(BF16)
    low = (coeffs - high.astype(F32)).astype(BF16)
    table = jnp.concatenate([high, low], axis=1)
    chunks = coeffs.shape[0] // LANES
    lanes = lane_ids(half).astype(F32)
    step = lax.broadcasted_iota(jnp.int32, (half, LANES), 0).astype(F32)
    picks = []
    for packed in near:
        ids = packed[places["ids"], :].astype(F32)
        ids = (ids[:8] * 16.0 + ids[8:]) * float(half)
        for term in range(terms):
            target = ids[term : term + 1] + step
            picks.append(
                jnp.concatenate([(target == lanes + float(LANES * c)).astype(F32) for c in range(chunks)], axis=1)
            )
    picks = jnp.concatenate(picks, axis=0).astype(BF16)
    picked = dot(picks, table)
    left = lane_ids(half) < HALF
    gap = jnp.zeros((HALF - modes, LANES), BF16)
    solutions = []
    for index, packed in enumerate(near):
        sides = []
        for part in range(2):
            columns = []
            for pair in range(0, terms, 2):
                first, second = [
                    picked[(index * terms + term) * half : (index * terms + term + 1) * half, part * LANES : (part + 1) * LANES]
                    for term in (pair, pair + 1)
                ]
                top = jnp.where(left, first, pltpu.roll(second, HALF, 1))
                bottom = jnp.where(left, pltpu.roll(first, HALF, 1), second)
                columns.append(jnp.concatenate([top, bottom], axis=0))
            sides.append(jnp.concatenate(columns, axis=1))
        rows = jnp.concatenate(sides, axis=0).astype(BF16)
        factors = []
        for term in range(terms):
            factors += [packed[term * modes : (term + 1) * modes, :], gap]
        product = dot(rows, jnp.concatenate(factors, axis=0))
        product = product[: 2 * half] + product[2 * half :]
        product = product + pltpu.roll(product, HALF, 1)
        solutions.append(product[:, :modes].astype(BF16))
    return solutions


def advance(sizes, dims, meta_ref, coeffs, residual, near_refs, rows_ref, dual_ref, theirs_ref, direction_ref,
            applied_ref):
    terms, modes = dims
    span = layout_of(terms, modes)["basis"]
    near = [ref[...] for ref in near_refs]
    solutions = solve(coeffs, near, terms, modes)
    mine = dot(solutions[0], rows_ref[residual.shape[0] :, :]).astype(BF16).astype(F32)
    for index, packed in enumerate(near[1:]):
        theirs_ref[index] = dot(solutions[index + 1], packed[span, :]).astype(BF16).astype(F32)
    pieces = []
    for block in range(PLANES + 2):
        if block < PLANES:
            place = slot_of(sizes, meta_ref[0, block])
        else:
            place = min(block, len(near) - 2)
        here = slice(block * LANES, (block + 1) * LANES)
        pieces.append(residual[:, here] + live_mask(meta_ref, block) * (mine[:, here] - theirs_ref[place]))
    direction = jnp.concatenate(pieces, axis=1)
    direction_ref[...] = direction
    applied = dot(direction.astype(BF16), dual_ref[0]).astype(BF16)
    applied_ref[...] = applied
    gamma = jnp.sum(residual * direction, axis=1, keepdims=True)
    delta = 2.0 * jnp.sum(direction * applied.astype(F32), axis=1, keepdims=True)
    half = gamma.shape[0] // 2
    lanes = lane_ids(half)
    sums = jnp.zeros((half, LANES), F32)
    for lane, values in ((GAMMA, gamma), (DELTA, delta)):
        sums = jnp.where(lanes == lane, values[:half], sums)
        sums = jnp.where(lanes == HALF + lane, values[half:], sums)
    return applied, sums


def first_kernel(sizes, dims, layers, count, meta_ref, residual_ref, rows_ref, dual_ref, *refs):
    gathered_refs, refs = refs[: 3 - layers], refs[3 - layers :]
    near_refs = refs[:count]
    message_ref, direction_ref, applied_ref, coeffs_ref, theirs_ref = refs[count:]
    if layers == 1:
        coarse = lax.axis_index("coarse")
        for fine in range(sizes[0]):
            coeffs_ref[2 * fine + coarse] = gathered_refs[0][fine]
            coeffs_ref[2 * fine + 1 - coarse] = gathered_refs[1][fine]
    else:
        coeffs_ref[...] = gathered_refs[0][...]
    _, sums = advance(
        sizes, dims, meta_ref, coeffs_ref[...].reshape(-1, LANES), residual_ref[...], near_refs, rows_ref, dual_ref,
        theirs_ref, direction_ref, applied_ref,
    )
    cases = applied_ref.shape[0]
    tiles = shares(sizes, dims, layers, meta_ref, applied_ref, near_refs, rows_ref, sums)
    message_ref[:, cases:, :] = jnp.broadcast_to(tiles[None], (message_ref.shape[0],) + tiles.shape)
    if layers == 1:
        post_plane(sizes, layers, meta_ref, applied_ref, message_ref)
    else:
        message_ref[:, :cases, :] = jnp.zeros((message_ref.shape[0], cases, LANES), BF16)
        post_blocks(message_ref, [meta_ref[0, b] for b in range(PLANES)], applied_ref[...])


def steps_from(totals):
    low = totals[:, GAMMA : GAMMA + 1] / totals[:, DELTA : DELTA + 1]
    high = totals[:, HALF + GAMMA : HALF + GAMMA + 1] / totals[:, HALF + DELTA : HALF + DELTA + 1]
    return low, high


def second_kernel(sizes, dims, layers, count, meta_ref, coeffs_ref, residual_ref, before_ref, applied_before_ref,
                  rows_ref, dual_ref, own_ref, *refs):
    others_refs, refs = refs[: 1 if layers == 1 else 3], refs[1 if layers == 1 else 3 :]
    near_refs = refs[:count]
    message_ref, residual_out, multipliers_out, direction_ref, applied_ref, theirs_ref, changes_ref = refs[count:]
    cases = residual_ref.shape[0]
    half = cases // 2
    low, high = steps_from(collect(sizes, layers, cases, own_ref, others_refs[0], changes_ref))
    step = jnp.concatenate([low, high], axis=0)
    packed_step = jnp.where(lane_ids(half) < HALF, low, high)
    coeffs = (coeffs_ref[...] - changes_ref[...] * packed_step[None]).reshape(-1, LANES)
    facing = facing_plane(meta_ref, own_ref, others_refs[0] if layers == 1 else own_ref, cases)
    if layers > 1:
        facing[PLANES:] = [ref[...] for ref in others_refs[1:]]
    image, _, _ = difference(meta_ref, applied_before_ref[...], facing)
    residual = residual_ref[...] - step * jnp.concatenate(image, axis=1)
    residual_out[...] = residual
    multipliers_out[...] = step * before_ref[...]
    _, sums = advance(
        sizes, dims, meta_ref, coeffs, residual, near_refs, rows_ref, dual_ref, theirs_ref, direction_ref, applied_ref
    )
    message_ref[:, cases:, :] = jnp.broadcast_to(encode(sums).astype(BF16)[None], (message_ref.shape[0], half, LANES))
    post_plane(sizes, layers, meta_ref, applied_ref, message_ref)


def last_kernel(sizes, layers, meta_ref, applied_ref, residual_ref, multipliers_ref, direction_ref, *refs):
    arrived_refs, (multipliers_out, residual_out) = refs[:-2], refs[-2:]
    cases = applied_ref.shape[0]
    totals = sum(jnp.sum(ref[:, cases:, :].astype(F32), axis=0) for ref in arrived_refs)
    step = jnp.concatenate(steps_from(decode(totals)), axis=0)
    if layers == 1:
        facing = facing_plane(meta_ref, arrived_refs[0], arrived_refs[1], cases)
    else:
        facing = [arrived_refs[0][target, :cases, :] for target in facing_subs(sizes, meta_ref)]
    image, _, _ = difference(meta_ref, applied_ref[...], facing)
    fine = lax.axis_index("fine")
    for block in range(PLANES + 2):
        span = slice(block * LANES, (block + 1) * LANES)
        if block < PLANES:
            sign = jnp.where(fine < meta_ref[0, block], 1.0, -1.0).astype(F32)
        else:
            sign = -1.0 if block == PLANES else 1.0
        multipliers_out[0, :, span] = sign * (multipliers_ref[:, span] + step * direction_ref[:, span])
        residual_out[0, :, span] = sign * (residual_ref[:, span] - step * image[block])


SMEM = pl.BlockSpec(memory_space=pltpu.SMEM)
VMEM = pl.BlockSpec(memory_space=pltpu.VMEM)


HBM = pl.BlockSpec(memory_space=pltpu.HBM)
ANY = pl.BlockSpec(memory_space=pl.ANY)


def call(kernel, name, scalars, arrays, outs, scratch=(), far=(), after=()):
    return pl.pallas_call(
        kernel,
        name=name,
        out_shape=[jax.ShapeDtypeStruct(shape, dtype) for shape, dtype in outs],
        in_specs=[SMEM] * len(scalars) + [VMEM] * len(arrays) + [HBM] * len(far) + [ANY] * len(after),
        out_specs=[VMEM] * len(outs),
        scratch_shapes=list(scratch),
        compiler_params=pltpu.CompilerParams(vmem_limit_bytes=40 * 1024 * 1024),
    )(*scalars, *arrays, *far, *after)


def body(load_cases, dual_ops, coarse_basis, factor_blocks, pattern, partners, row_counts):
    cases, width = load_cases.shape[1:]
    terms, modes = factor_blocks.shape[1:3]
    fine_count = lax.axis_size("fine")
    coarse_count = lax.axis_size("coarse")
    subs = fine_count * coarse_count
    sizes = (fine_count, coarse_count)
    dims = (terms, modes)
    half = cases // 2
    layers = 1 if coarse_count == 2 else 2

    def swap_cores(array):
        return lax.ppermute(array, "coarse", [(0, 1), (1, 0)])

    def swap_all(message):
        if layers == 1:
            own = lax.all_to_all(message, "fine", 0, 0, tiled=True)
            return [own, swap_cores(own)]
        return [lax.all_to_all(message, AXES, 0, 0, tiled=True)]

    def swap_slot(message, slot):
        distance = 2 * (PLANES - slot) - 1
        pairs = [(i, (i + distance if i % 2 == 0 else i - distance) % fine_count) for i in range(fine_count)]
        return lax.ppermute(message, "fine", pairs)

    def swap_blocks(messages):
        received = [swap_slot(messages[slot], slot) for slot in range(PLANES)]
        if layers == 1:
            return received + [swap_cores(messages[PLANES])]
        up = [(i, i + 1) for i in range(coarse_count - 1)]
        lower = lax.ppermute(messages[PLANES + 1], "coarse", up)
        return received + [lower, lax.ppermute(messages[PLANES], "coarse", [(j, i) for i, j in up])]

    full = ((cases, width), F32)
    half_full = ((cases, width), BF16)
    peers = fine_count if layers == 1 else subs
    dma = pltpu.SemaphoreType.DMA

    meta = jnp.concatenate([partners, row_counts, pattern], axis=1)
    rows = jnp.concatenate([load_cases[0], coarse_basis[0]], axis=0)
    loads_span = layout_of(terms, modes)["loads"]
    packed = call(
        functools.partial(pack_kernel, sizes, layers, cases),
        "pack_setup",
        (meta,),
        (rows, factor_blocks),
        [((loads_span.stop, LANES), BF16)] * (PLANES + layers),
    )
    received = swap_blocks(packed)
    near = [packed[-1]] + received
    count = len(near)
    theirs = [pltpu.VMEM((count - 1, cases, LANES), F32)]

    [dual] = call(dual_kernel, "fetch_dual", (), (), [(dual_ops.shape, BF16)], [dma((1,))], (dual_ops,), (packed[-1],))
    residual, message = call(
        functools.partial(first_restrict_kernel, sizes, dims, layers),
        "restrict_residual",
        (meta,),
        (rows, *received),
        [full, ((peers, half, LANES), F32)],
        [pltpu.VMEM((PLANES, cases, LANES), BF16)],
        after=(dual,),
    )
    gathered = swap_all(message)

    tiles = 2 + PLANES + layers
    message, direction, applied, coeffs = call(
        functools.partial(first_kernel, sizes, dims, layers, count),
        "first_direction",
        (meta,),
        (residual, rows, dual, *gathered, *near),
        [((fine_count, cases + tiles * half, LANES), BF16), full, half_full, ((subs, half, LANES), F32)],
        theirs,
    )
    own = lax.all_to_all(message, "fine", 0, 0, tiled=True)
    if layers == 1:
        others = [swap_cores(own)]
    else:
        up = [(i, i + 1) for i in range(coarse_count - 1)]
        lower = lax.ppermute(applied[:, (PLANES + 1) * LANES :], "coarse", up)
        upper = lax.ppermute(applied[:, PLANES * LANES : (PLANES + 1) * LANES], "coarse", [(j, i) for i, j in up])
        others = [lax.all_gather(own, "coarse"), lower, upper]

    message, residual, multipliers, direction, applied = call(
        functools.partial(second_kernel, sizes, dims, layers, count),
        "second_direction",
        (meta,),
        (coeffs, residual, direction, applied, rows, dual, own, *others, *near),
        [((peers, cases + half, LANES), BF16), full, full, full, half_full],
        theirs + [pltpu.VMEM((subs, half, LANES), F32)],
    )
    out = ((1, cases, width), F32)
    multipliers, residual = call(
        functools.partial(last_kernel, sizes, layers),
        "finish",
        (meta,),
        (applied, residual, multipliers, direction, *swap_all(message)),
        [out, out],
    )
    return multipliers, residual


def solution(mesh):
    rows = P(AXES, None, None)
    return jax.shard_map(
        body,
        mesh=mesh,
        in_specs=(rows, rows, rows, P(AXES, None, None, None), P(AXES, None), P(AXES, None), P(AXES, None)),
        out_specs=(rows, rows),
        check_vma=False,
    )
```

```python
import functools

import jax
import jax.numpy as jnp
from jax import lax
from jax.experimental import pallas as pl
from jax.experimental.pallas import tpu as pltpu
from jax.sharding import PartitionSpec as P

PLANES = 6
DISTANCES = (11, 7, 3, 5, 9, 1)
AXES = ("fine", "coarse")
LANES = 128
HALF = 64
BF16 = jnp.bfloat16
F32 = jnp.float32
GAMMA = 48
DELTA = 49


def lane_ids(rows):
    return lax.broadcasted_iota(jnp.int32, (rows, LANES), 1)


def dot(a, b):
    return lax.dot_general(a, b, (((1,), (0,)), ((), ())), preferred_element_type=F32)


def wanted_blocks(sizes, layers, meta_ref):
    slots = [slot_of(sizes, meta_ref[0, b]) for b in range(PLANES)]
    blocks = []
    for slot in range(PLANES):
        blocks.append(sum(jnp.where(slots[b] == slot, b, 0) for b in range(PLANES)))
    if layers == 1:
        return blocks + [jnp.where(lax.axis_index("coarse") == 0, PLANES + 1, PLANES)]
    return blocks + [PLANES, PLANES + 1]


def lanes_of(block):
    start = block * LANES
    return pl.ds(start if isinstance(start, int) else pl.multiple_of(start, LANES), LANES)


def facing_subs(sizes, partners_ref):
    fine_count, coarse_count = sizes
    fine = lax.axis_index("fine")
    coarse = lax.axis_index("coarse")
    me = fine * coarse_count + coarse
    subs = [partners_ref[0, b] * coarse_count + coarse for b in range(PLANES)]
    subs.append(jnp.where(coarse > 0, me - 1, me))
    subs.append(jnp.where(coarse < coarse_count - 1, me + 1, me))
    return subs


def slot_of(sizes, partner):
    fine_count = sizes[0]
    fine = lax.axis_index("fine")
    ahead = jnp.where(fine % 2 == 0, partner - fine, fine - partner)
    ahead = jnp.where(ahead < 0, ahead + fine_count, ahead)
    return sum(jnp.where(ahead == distance, slot, 0) for slot, distance in enumerate(DISTANCES))


def live_mask(counts_ref, block):
    return (lane_ids(1) < counts_ref[0, PLANES + block]).astype(F32)


def post_blocks(out_ref, targets, rows):
    cases = rows.shape[0]
    for block, target in enumerate(targets):
        out_ref[target, :cases, :] = rows[:, block * LANES : (block + 1) * LANES]


def fetch(pairs, sems):
    copies = [pltpu.make_async_copy(source, target, sems.at[i]) for i, (source, target) in enumerate(pairs)]
    for copy in copies:
        copy.start()
    return copies


def pack_kernel(sizes, layers, cases, meta_ref, rows_ref, factors_ref, *outs):
    terms, modes = factors_ref.shape[1:3]
    gap = jnp.zeros((modes, HALF - modes), F32)
    parts = []
    for term in range(terms):
        whole = factors_ref[0, term]
        high = whole.astype(BF16).astype(F32)
        parts.append(jnp.concatenate([high, gap, whole - high, gap], axis=1))
    factors = jnp.concatenate(parts, axis=0).astype(BF16)
    row = lax.broadcasted_iota(jnp.int32, (16, LANES), 0)
    ids = jnp.zeros((16, LANES), F32)
    for term in range(terms):
        sub = meta_ref[0, 2 * PLANES + 2 + term]
        ids = jnp.where(row == term, (sub // 16).astype(F32), ids)
        ids = jnp.where(row == 8 + term, (sub % 16).astype(F32), ids)
    ids = ids.astype(BF16)
    places = layout_of(terms, modes)
    for out_ref, block in zip(outs, wanted_blocks(sizes, layers, meta_ref)):
        out_ref[places["factors"], :] = factors
        out_ref[places["ids"], :] = ids
        out_ref[places["loads"], :] = rows_ref[:cases, lanes_of(block)]
        out_ref[places["basis"], :] = rows_ref[cases:, lanes_of(block)]


def layout_of(terms, modes):
    sizes = (("factors", terms * modes), ("basis", modes), ("ids", 16), ("loads", 16))
    places, start = {}, 0
    for name, rows in sizes:
        places[name] = slice(start, start + rows)
        start += rows
    return places


def dual_kernel(dual_ref, after_ref, out_ref, sems):
    for copy in fetch([(dual_ref, out_ref)], sems):
        copy.wait()


def difference(counts_ref, mine, facing):
    result, ours, theirs = [], [], []
    for block, other in enumerate(facing):
        mask = live_mask(counts_ref, block)
        left = mine[:, block * LANES : (block + 1) * LANES].astype(F32) * mask
        right = other.astype(F32) * mask
        result.append(left - right)
        ours.append(left.astype(BF16))
        theirs.append(right.astype(BF16))
    return result, ours, theirs


def first_restrict_kernel(sizes, dims, layers, meta_ref, rows_ref, *refs):
    near_refs, (_, out_ref, message_ref, scratch_ref) = refs[: PLANES + layers], refs[PLANES + layers :]
    span = layout_of(*dims)["loads"]
    cases = out_ref.shape[0]
    for slot in range(PLANES):
        scratch_ref[slot] = near_refs[slot][span, :]
    facing = [scratch_ref[slot_of(sizes, meta_ref[0, b])] for b in range(PLANES)]
    facing += [near_refs[PLANES][span, :], near_refs[-1][span, :]]
    restrict(meta_ref, rows_ref[:cases, :], facing, rows_ref[cases:, :], out_ref, message_ref)


def twice(basis):
    gap = jnp.zeros((HALF - basis.shape[0], basis.shape[1]), BF16)
    return jnp.concatenate([basis, gap, basis, gap], axis=0)


def times_basis(rows, doubled):
    return lax.dot_general(rows, doubled, (((1,), (1,)), ((), ())), preferred_element_type=F32)


def fold(coefficients):
    half = coefficients.shape[0] // 2
    return jnp.where(lane_ids(half) < HALF, coefficients[:half], coefficients[half:])


def encode(sums):
    top = sums.astype(BF16).astype(F32)
    middle = (sums - top).astype(BF16).astype(F32)
    bottom = sums - top - middle
    return top + pltpu.roll(middle, 2, 1) + pltpu.roll(bottom, 4, 1)


def decode(totals):
    return totals + pltpu.roll(totals, LANES - 2, 1) + pltpu.roll(totals, LANES - 4, 1)


def restrict(meta_ref, mine, facing, basis, out_ref, message_ref):
    cases = mine.shape[0]
    result, ours, theirs = difference(meta_ref, mine, facing)
    for block, values in enumerate(result):
        out_ref[:, block * LANES : (block + 1) * LANES] = values
    both = jnp.concatenate([jnp.concatenate(ours, axis=1), jnp.concatenate(theirs, axis=1)], axis=0)
    coefficients = times_basis(both, twice(basis))
    message = fold(coefficients[:cases] - coefficients[cases:])
    message_ref[...] = jnp.broadcast_to(message[None], message_ref.shape)


def seat(part, modes):
    gap = HALF - modes
    lane = lane_ids(8) % HALF
    return (lane >= part * gap) & (lane < (part + 1) * gap), modes - part * gap


def board(hosts, guest, modes):
    seated = []
    for part, host in enumerate(hosts):
        mask, move = seat(part, modes)
        seated.append(host + pltpu.roll(jnp.where(mask, guest, 0.0), move, 1))
    return seated


def alight(hosts, modes):
    guest = jnp.zeros((8, LANES), F32)
    for part, host in enumerate(hosts):
        mask, move = seat(part, modes)
        guest = jnp.where(mask, pltpu.roll(host, LANES - move, 1), guest)
    return guest


def shares(sizes, dims, layers, meta_ref, applied_ref, near_refs, rows_ref, sums):
    cases = applied_ref.shape[0]
    span = layout_of(*dims)["basis"]
    masked = []
    for block in range(PLANES + 2):
        part = applied_ref[:, block * LANES : (block + 1) * LANES].astype(F32)
        masked.append((part * live_mask(meta_ref, block)).astype(BF16))
    own = fold(times_basis(jnp.concatenate(masked, axis=1), twice(rows_ref[cases:, :])))
    high = own.astype(BF16).astype(F32)
    tiles = []
    for near_ref, block in zip(near_refs[1:], wanted_blocks(sizes, layers, meta_ref)):
        part = applied_ref[:, lanes_of(block)].astype(F32) * live_mask(meta_ref, block)
        tiles.append(fold(times_basis(part.astype(BF16), twice(near_ref[span, :]))))
    modes = dims[1]
    hosts = board(tiles[:3], own - high, modes) + board(tiles[3:PLANES], tiles[PLANES], modes)
    return jnp.concatenate([high + encode(sums)] + hosts + tiles[PLANES + 1 :], axis=0).astype(BF16)


def collect(sizes, dims, layers, cases, own_ref, others_ref, changes_ref):
    fine_count, coarse_count = sizes
    half = cases // 2
    coarse = lax.axis_index("coarse")

    def tile(layer, fine, index):
        rows = slice(cases + index * half, cases + (index + 1) * half)
        if layers == 1:
            source = own_ref if layer == 0 else others_ref
            return source[fine, rows, :].astype(F32)
        return others_ref[layer, fine, rows, :].astype(F32)

    def one(fine, totals):
        for layer in range(coarse_count):
            first = tile(layer, fine, 0)
            totals = totals + first
            value = first + alight([tile(layer, fine, 1 + slot) for slot in range(3)], dims[1])
            for slot in range(PLANES):
                distance = DISTANCES[slot]
                partner = jnp.where(fine % 2 == 0, fine + distance, fine - distance) if layers > 1 else (
                    fine + distance if fine % 2 == 0 else fine - distance
                )
                value = value - tile(layer, (partner + fine_count) % fine_count, 1 + slot)
            if layers == 1:
                value = value - alight([tile(1 - layer, fine, 4 + slot) for slot in range(3)], dims[1])
                place = fine * 2 + (coarse if layer == 0 else 1 - coarse)
            else:
                if layer > 0:
                    value = value - tile(layer - 1, fine, 1 + PLANES)
                if layer < coarse_count - 1:
                    value = value - alight([tile(layer + 1, fine, 4 + slot) for slot in range(3)], dims[1])
                place = fine * coarse_count + layer
            changes_ref[place] = value
        return totals

    totals = jnp.zeros((half, LANES), F32)
    if layers > 1:
        return decode(lax.fori_loop(0, fine_count, one, totals))
    for fine in range(fine_count):
        totals = one(fine, totals)
    return decode(totals)


def solve(coeffs, near, terms, modes):
    half = 8
    places = layout_of(terms, modes)
    high = coeffs.astype(BF16)
    low = (coeffs - high.astype(F32)).astype(BF16)
    table = jnp.concatenate([high, low], axis=1)
    chunks = coeffs.shape[0] // LANES
    lanes = lane_ids(half).astype(F32)
    step = lax.broadcasted_iota(jnp.int32, (half, LANES), 0).astype(F32)
    picks = []
    for packed in near:
        ids = packed[places["ids"], :].astype(F32)
        ids = (ids[:8] * 16.0 + ids[8:]) * float(half)
        for term in range(terms):
            target = ids[term : term + 1] + step
            picks.append(
                jnp.concatenate([(target == lanes + float(LANES * c)).astype(F32) for c in range(chunks)], axis=1)
            )
    picks = jnp.concatenate(picks, axis=0).astype(BF16)
    picked = dot(picks, table)
    left = lane_ids(half) < HALF
    gap = jnp.zeros((HALF - modes, LANES), BF16)
    solutions = []
    for index, packed in enumerate(near):
        sides = []
        for part in range(2):
            columns = []
            for pair in range(0, terms, 2):
                first, second = [
                    picked[(index * terms + term) * half : (index * terms + term + 1) * half, part * LANES : (part + 1) * LANES]
                    for term in (pair, pair + 1)
                ]
                top = jnp.where(left, first, pltpu.roll(second, HALF, 1))
                bottom = jnp.where(left, pltpu.roll(first, HALF, 1), second)
                columns.append(jnp.concatenate([top, bottom], axis=0))
            sides.append(jnp.concatenate(columns, axis=1))
        rows = jnp.concatenate(sides, axis=0).astype(BF16)
        factors = []
        for term in range(terms):
            factors += [packed[term * modes : (term + 1) * modes, :], gap]
        product = dot(rows, jnp.concatenate(factors, axis=0))
        product = product[: 2 * half] + product[2 * half :]
        product = product + pltpu.roll(product, HALF, 1)
        solutions.append(product[:, :modes].astype(BF16))
    return solutions


def advance(sizes, dims, meta_ref, coeffs, residual, near_refs, rows_ref, dual_ref, theirs_ref, direction_ref,
            applied_ref):
    terms, modes = dims
    span = layout_of(terms, modes)["basis"]
    near = [ref[...] for ref in near_refs]
    solutions = solve(coeffs, near, terms, modes)
    mine = dot(solutions[0], rows_ref[residual.shape[0] :, :]).astype(BF16).astype(F32)
    for index, packed in enumerate(near[1:]):
        theirs_ref[index] = dot(solutions[index + 1], packed[span, :]).astype(BF16).astype(F32)
    pieces = []
    for block in range(PLANES + 2):
        if block < PLANES:
            place = slot_of(sizes, meta_ref[0, block])
        else:
            place = min(block, len(near) - 2)
        here = slice(block * LANES, (block + 1) * LANES)
        pieces.append(residual[:, here] + live_mask(meta_ref, block) * (mine[:, here] - theirs_ref[place]))
    direction = jnp.concatenate(pieces, axis=1)
    direction_ref[...] = direction
    applied = dot(direction.astype(BF16), dual_ref[0]).astype(BF16)
    applied_ref[...] = applied
    gamma = jnp.sum(residual * direction, axis=1, keepdims=True)
    delta = 2.0 * jnp.sum(direction * applied.astype(F32), axis=1, keepdims=True)
    half = gamma.shape[0] // 2
    lanes = lane_ids(half)
    sums = jnp.zeros((half, LANES), F32)
    for lane, values in ((GAMMA, gamma), (DELTA, delta)):
        sums = jnp.where(lanes == lane, values[:half], sums)
        sums = jnp.where(lanes == HALF + lane, values[half:], sums)
    return applied, sums


def first_kernel(sizes, dims, layers, count, meta_ref, coeffs_ref, residual_ref, rows_ref, dual_ref, *refs):
    near_refs = refs[:count]
    message_ref, direction_ref, applied_ref, theirs_ref = refs[count:]
    applied, sums = advance(
        sizes, dims, meta_ref, coeffs_ref[...], residual_ref[...], near_refs, rows_ref, dual_ref, theirs_ref,
        direction_ref, applied_ref,
    )
    cases = applied.shape[0]
    tiles = shares(sizes, dims, layers, meta_ref, applied_ref, near_refs, rows_ref, sums)
    message_ref[:, :cases, :] = jnp.zeros((message_ref.shape[0], cases, LANES), BF16)
    message_ref[:, cases:, :] = jnp.broadcast_to(tiles[None], (message_ref.shape[0],) + tiles.shape)
    post_blocks(message_ref, [meta_ref[0, b] for b in range(PLANES)], applied)
    if layers == 1:
        block = wanted_blocks(sizes, layers, meta_ref)[-1]
        message_ref[lax.axis_index("fine"), :cases, :] = applied_ref[:, lanes_of(block)]


def steps_from(totals):
    low = totals[:, GAMMA : GAMMA + 1] / totals[:, DELTA : DELTA + 1]
    high = totals[:, HALF + GAMMA : HALF + GAMMA + 1] / totals[:, HALF + DELTA : HALF + DELTA + 1]
    return low, high


def second_kernel(sizes, dims, layers, count, meta_ref, coeffs_ref, residual_ref, before_ref, applied_before_ref,
                  rows_ref, dual_ref, own_ref, *refs):
    others_refs, refs = refs[: 1 if layers == 1 else 3], refs[1 if layers == 1 else 3 :]
    near_refs = refs[:count]
    message_ref, residual_out, multipliers_out, direction_ref, applied_ref, theirs_ref, changes_ref = refs[count:]
    cases = residual_ref.shape[0]
    half = cases // 2
    low, high = steps_from(collect(sizes, dims, layers, cases, own_ref, others_refs[0], changes_ref))
    step = jnp.concatenate([low, high], axis=0)
    packed_step = jnp.where(lane_ids(half) < HALF, low, high)
    coeffs = coeffs_ref[...] - (changes_ref[...] * packed_step[None]).reshape(coeffs_ref.shape)
    facing = [own_ref[meta_ref[0, b], :cases, :] for b in range(PLANES)]
    if layers == 1:
        facing += [others_refs[0][lax.axis_index("fine"), :cases, :]] * 2
    else:
        facing += [ref[...] for ref in others_refs[1:]]
    image, _, _ = difference(meta_ref, applied_before_ref[...], facing)
    residual = residual_ref[...] - step * jnp.concatenate(image, axis=1)
    residual_out[...] = residual
    multipliers_out[...] = step * before_ref[...]
    applied, sums = advance(
        sizes, dims, meta_ref, coeffs, residual, near_refs, rows_ref, dual_ref, theirs_ref, direction_ref, applied_ref
    )
    message_ref[:, :cases, :] = jnp.zeros((message_ref.shape[0], cases, LANES), BF16)
    message_ref[:, cases:, :] = jnp.broadcast_to(encode(sums).astype(BF16)[None], (message_ref.shape[0], half, LANES))
    post_blocks(message_ref, facing_subs(sizes, meta_ref), applied)


def last_kernel(sizes, meta_ref, arrived_ref, applied_ref, residual_ref, multipliers_ref, direction_ref,
                multipliers_out, residual_out):
    cases = applied_ref.shape[0]
    totals = jnp.sum(arrived_ref[:, cases:, :].astype(F32), axis=0)
    step = jnp.concatenate(steps_from(decode(totals)), axis=0)
    facing = [arrived_ref[target, :cases, :] for target in facing_subs(sizes, meta_ref)]
    image, _, _ = difference(meta_ref, applied_ref[...], facing)
    fine = lax.axis_index("fine")
    for block in range(PLANES + 2):
        span = slice(block * LANES, (block + 1) * LANES)
        if block < PLANES:
            sign = jnp.where(fine < meta_ref[0, block], 1.0, -1.0).astype(F32)
        else:
            sign = -1.0 if block == PLANES else 1.0
        multipliers_out[0, :, span] = sign * (multipliers_ref[:, span] + step * direction_ref[:, span])
        residual_out[0, :, span] = sign * (residual_ref[:, span] - step * image[block])


SMEM = pl.BlockSpec(memory_space=pltpu.SMEM)
VMEM = pl.BlockSpec(memory_space=pltpu.VMEM)


HBM = pl.BlockSpec(memory_space=pltpu.HBM)
ANY = pl.BlockSpec(memory_space=pl.ANY)


def call(kernel, name, scalars, arrays, outs, scratch=(), far=(), after=()):
    return pl.pallas_call(
        kernel,
        name=name,
        out_shape=[jax.ShapeDtypeStruct(shape, dtype) for shape, dtype in outs],
        in_specs=[SMEM] * len(scalars) + [VMEM] * len(arrays) + [HBM] * len(far) + [ANY] * len(after),
        out_specs=[VMEM] * len(outs),
        scratch_shapes=list(scratch),
        compiler_params=pltpu.CompilerParams(vmem_limit_bytes=40 * 1024 * 1024),
    )(*scalars, *arrays, *far, *after)


def body(load_cases, dual_ops, coarse_basis, factor_blocks, pattern, partners, row_counts):
    cases, width = load_cases.shape[1:]
    terms, modes = factor_blocks.shape[1:3]
    fine_count = lax.axis_size("fine")
    coarse_count = lax.axis_size("coarse")
    subs = fine_count * coarse_count
    sizes = (fine_count, coarse_count)
    dims = (terms, modes)
    half = cases // 2
    layers = 1 if coarse_count == 2 else 2

    def swap_all(message):
        return lax.all_to_all(message, AXES, 0, 0, tiled=True)

    def swap_slot(message, slot):
        distance = DISTANCES[slot]
        pairs = [(i, (i + distance if i % 2 == 0 else i - distance) % fine_count) for i in range(fine_count)]
        return lax.ppermute(message, "fine", pairs)

    def swap_blocks(messages):
        received = [swap_slot(messages[slot], slot) for slot in range(PLANES)]
        if layers == 1:
            return received + [lax.ppermute(messages[PLANES], "coarse", [(0, 1), (1, 0)])]
        up = [(i, i + 1) for i in range(coarse_count - 1)]
        lower = lax.ppermute(messages[PLANES + 1], "coarse", up)
        return received + [lower, lax.ppermute(messages[PLANES], "coarse", [(j, i) for i, j in up])]

    full = ((cases, width), F32)
    half_full = ((cases, width), BF16)
    coded = ((subs, half, LANES), F32)
    dma = pltpu.SemaphoreType.DMA

    meta = jnp.concatenate([partners, row_counts, pattern], axis=1)
    rows = jnp.concatenate([load_cases[0], coarse_basis[0]], axis=0)
    loads_span = layout_of(terms, modes)["loads"]
    packed = call(
        functools.partial(pack_kernel, sizes, layers, cases),
        "pack_setup",
        (meta,),
        (rows, factor_blocks),
        [((loads_span.stop, LANES), BF16)] * (PLANES + layers),
    )
    received = swap_blocks(packed)
    near = [packed[-1]] + received
    count = len(near)
    theirs = [pltpu.VMEM((count - 1, cases, LANES), F32)]

    [dual] = call(dual_kernel, "fetch_dual", (), (), [(dual_ops.shape, BF16)], [dma((1,))], (dual_ops,), (packed[-1],))
    residual, message = call(
        functools.partial(first_restrict_kernel, sizes, dims, layers),
        "restrict_residual",
        (meta,),
        (rows, *received),
        [full, coded],
        [pltpu.VMEM((PLANES, cases, LANES), BF16)],
        after=(dual,),
    )
    coeffs = swap_all(message).reshape(subs * half, LANES)

    tiles = PLANES + layers
    message, direction, applied = call(
        functools.partial(first_kernel, sizes, dims, layers, count),
        "first_direction",
        (meta,),
        (coeffs, residual, rows, dual, *near),
        [((fine_count, cases + tiles * half, LANES), BF16), full, half_full],
        theirs,
    )
    own = lax.all_to_all(message, "fine", 0, 0, tiled=True)
    if layers == 1:
        others = [lax.ppermute(own, "coarse", [(0, 1), (1, 0)])]
    else:
        up = [(i, i + 1) for i in range(coarse_count - 1)]
        lower = lax.ppermute(applied[:, (PLANES + 1) * LANES :], "coarse", up)
        upper = lax.ppermute(applied[:, PLANES * LANES : (PLANES + 1) * LANES], "coarse", [(j, i) for i, j in up])
        others = [lax.all_gather(own, "coarse"), lower, upper]

    message, residual, multipliers, direction, applied = call(
        functools.partial(second_kernel, sizes, dims, layers, count),
        "second_direction",
        (meta,),
        (coeffs, residual, direction, applied, rows, dual, own, *others, *near),
        [((subs, cases + half, LANES), BF16), full, full, full, half_full],
        theirs + [pltpu.VMEM((subs, half, LANES), F32)],
    )
    arrived = swap_all(message)
    out = ((1, cases, width), F32)
    multipliers, residual = call(
        functools.partial(last_kernel, sizes),
        "finish",
        (meta,),
        (arrived, applied, residual, multipliers, direction),
        [out, out],
    )
    return multipliers, residual


def solution(mesh):
    rows = P(AXES, None, None)
    return jax.shard_map(
        body,
        mesh=mesh,
        in_specs=(rows, rows, rows, P(AXES, None, None, None), P(AXES, None), P(AXES, None), P(AXES, None)),
        out_specs=(rows, rows),
        check_vma=False,
    )
```

```python
import functools

import jax
import jax.numpy as jnp
from jax import lax
from jax.experimental import pallas as pl
from jax.experimental.pallas import tpu as pltpu
from jax.sharding import PartitionSpec as P

PLANES = 6
DISTANCES = (11, 9, 7, 3, 5, 1)
AXES = ("fine", "coarse")
LANES = 128
HALF = 64
BF16 = jnp.bfloat16
F32 = jnp.float32
GAMMA = 48
DELTA = 49


def lane_ids(rows):
    return lax.broadcasted_iota(jnp.int32, (rows, LANES), 1)


def dot(a, b):
    return lax.dot_general(a, b, (((1,), (0,)), ((), ())), preferred_element_type=F32)


def wanted_blocks(sizes, layers, meta_ref):
    slots = [slot_of(sizes, meta_ref[0, b]) for b in range(PLANES)]
    blocks = []
    for slot in range(PLANES):
        blocks.append(sum(jnp.where(slots[b] == slot, b, 0) for b in range(PLANES)))
    if layers == 1:
        return blocks + [jnp.where(lax.axis_index("coarse") == 0, PLANES + 1, PLANES)]
    return blocks + [PLANES, PLANES + 1]


def lanes_of(block):
    start = block * LANES
    return pl.ds(start if isinstance(start, int) else pl.multiple_of(start, LANES), LANES)


def facing_subs(sizes, partners_ref):
    fine_count, coarse_count = sizes
    fine = lax.axis_index("fine")
    coarse = lax.axis_index("coarse")
    me = fine * coarse_count + coarse
    subs = [partners_ref[0, b] * coarse_count + coarse for b in range(PLANES)]
    subs.append(jnp.where(coarse > 0, me - 1, me))
    subs.append(jnp.where(coarse < coarse_count - 1, me + 1, me))
    return subs


def slot_of(sizes, partner):
    fine_count = sizes[0]
    fine = lax.axis_index("fine")
    ahead = jnp.where(fine % 2 == 0, partner - fine, fine - partner)
    ahead = jnp.where(ahead < 0, ahead + fine_count, ahead)
    return sum(jnp.where(ahead == distance, slot, 0) for slot, distance in enumerate(DISTANCES))


def live_mask(counts_ref, block):
    return (lane_ids(1) < counts_ref[0, PLANES + block]).astype(F32)


def post_blocks(out_ref, targets, rows):
    cases = rows.shape[0]
    for block, target in enumerate(targets):
        out_ref[target, :cases, :] = rows[:, block * LANES : (block + 1) * LANES]


def fetch(pairs, sems):
    copies = [pltpu.make_async_copy(source, target, sems.at[i]) for i, (source, target) in enumerate(pairs)]
    for copy in copies:
        copy.start()
    return copies


def pack_kernel(sizes, layers, cases, meta_ref, rows_ref, factors_ref, *outs):
    terms, modes = factors_ref.shape[1:3]
    gap = jnp.zeros((modes, HALF - modes), F32)
    parts = []
    for term in range(terms):
        whole = factors_ref[0, term]
        high = whole.astype(BF16).astype(F32)
        parts.append(jnp.concatenate([high, gap, whole - high, gap], axis=1))
    factors = jnp.concatenate(parts, axis=0).astype(BF16)
    row = lax.broadcasted_iota(jnp.int32, (16, LANES), 0)
    ids = jnp.zeros((16, LANES), F32)
    for term in range(terms):
        sub = meta_ref[0, 2 * PLANES + 2 + term]
        ids = jnp.where(row == term, (sub // 16).astype(F32), ids)
        ids = jnp.where(row == 8 + term, (sub % 16).astype(F32), ids)
    ids = ids.astype(BF16)
    places = layout_of(terms, modes)
    for out_ref, block in zip(outs, wanted_blocks(sizes, layers, meta_ref)):
        out_ref[places["factors"], :] = factors
        out_ref[places["ids"], :] = ids
        out_ref[places["loads"], :] = rows_ref[:cases, lanes_of(block)]
        out_ref[places["basis"], :] = rows_ref[cases:, lanes_of(block)]


def layout_of(terms, modes):
    sizes = (("factors", terms * modes), ("basis", modes), ("ids", 16), ("loads", 16))
    places, start = {}, 0
    for name, rows in sizes:
        places[name] = slice(start, start + rows)
        start += rows
    return places


def dual_kernel(dual_ref, after_ref, out_ref, sems):
    for copy in fetch([(dual_ref, out_ref)], sems):
        copy.wait()


def difference(counts_ref, mine, facing):
    result, ours, theirs = [], [], []
    for block, other in enumerate(facing):
        mask = live_mask(counts_ref, block)
        left = mine[:, block * LANES : (block + 1) * LANES].astype(F32) * mask
        right = other.astype(F32) * mask
        result.append(left - right)
        ours.append(left.astype(BF16))
        theirs.append(right.astype(BF16))
    return result, ours, theirs


def first_restrict_kernel(sizes, dims, layers, meta_ref, rows_ref, *refs):
    near_refs, (_, out_ref, message_ref, scratch_ref) = refs[: PLANES + layers], refs[PLANES + layers :]
    span = layout_of(*dims)["loads"]
    cases = out_ref.shape[0]
    for slot in range(PLANES):
        scratch_ref[slot] = near_refs[slot][span, :]
    facing = [scratch_ref[slot_of(sizes, meta_ref[0, b])] for b in range(PLANES)]
    facing += [near_refs[PLANES][span, :], near_refs[-1][span, :]]
    restrict(meta_ref, rows_ref[:cases, :], facing, rows_ref[cases:, :], out_ref, message_ref)


def twice(basis):
    gap = jnp.zeros((HALF - basis.shape[0], basis.shape[1]), BF16)
    return jnp.concatenate([basis, gap, basis, gap], axis=0)


def times_basis(rows, doubled):
    return lax.dot_general(rows, doubled, (((1,), (1,)), ((), ())), preferred_element_type=F32)


def fold(coefficients):
    half = coefficients.shape[0] // 2
    return jnp.where(lane_ids(half) < HALF, coefficients[:half], coefficients[half:])


def encode(sums):
    top = sums.astype(BF16).astype(F32)
    middle = (sums - top).astype(BF16).astype(F32)
    bottom = sums - top - middle
    return top + pltpu.roll(middle, 2, 1) + pltpu.roll(bottom, 4, 1)


def decode(totals):
    return totals + pltpu.roll(totals, LANES - 2, 1) + pltpu.roll(totals, LANES - 4, 1)


def restrict(meta_ref, mine, facing, basis, out_ref, message_ref):
    cases = mine.shape[0]
    result, ours, theirs = difference(meta_ref, mine, facing)
    for block, values in enumerate(result):
        out_ref[:, block * LANES : (block + 1) * LANES] = values
    both = jnp.concatenate([jnp.concatenate(ours, axis=1), jnp.concatenate(theirs, axis=1)], axis=0)
    coefficients = times_basis(both, twice(basis))
    message = fold(coefficients[:cases] - coefficients[cases:])
    message_ref[...] = jnp.broadcast_to(message[None], message_ref.shape)


def seat(part, modes):
    gap = HALF - modes
    lane = lane_ids(8) % HALF
    return (lane >= part * gap) & (lane < (part + 1) * gap), modes - part * gap


def board(hosts, guest, modes):
    seated = []
    for part, host in enumerate(hosts):
        mask, move = seat(part, modes)
        seated.append(host + pltpu.roll(jnp.where(mask, guest, 0.0), move, 1))
    return seated


def alight(hosts, modes):
    guest = jnp.zeros((8, LANES), F32)
    for part, host in enumerate(hosts):
        mask, move = seat(part, modes)
        guest = jnp.where(mask, pltpu.roll(host, LANES - move, 1), guest)
    return guest


def shares(sizes, dims, layers, meta_ref, applied_ref, near_refs, rows_ref, sums):
    cases = applied_ref.shape[0]
    span = layout_of(*dims)["basis"]
    masked = []
    for block in range(PLANES + 2):
        part = applied_ref[:, block * LANES : (block + 1) * LANES].astype(F32)
        masked.append((part * live_mask(meta_ref, block)).astype(BF16))
    own = fold(times_basis(jnp.concatenate(masked, axis=1), twice(rows_ref[cases:, :])))
    high = own.astype(BF16).astype(F32)
    tiles = []
    for near_ref, block in zip(near_refs[1:], wanted_blocks(sizes, layers, meta_ref)):
        part = applied_ref[:, lanes_of(block)].astype(F32) * live_mask(meta_ref, block)
        tiles.append(fold(times_basis(part.astype(BF16), twice(near_ref[span, :]))))
    modes = dims[1]
    hosts = board(tiles[:3], own - high, modes) + board(tiles[3:PLANES], tiles[PLANES], modes)
    return jnp.concatenate([high + encode(sums)] + hosts + tiles[PLANES + 1 :], axis=0).astype(BF16)


def collect(sizes, dims, layers, cases, own_ref, others_ref, changes_ref):
    fine_count, coarse_count = sizes
    half = cases // 2
    coarse = lax.axis_index("coarse")

    def tile(layer, fine, index):
        rows = slice(cases + index * half, cases + (index + 1) * half)
        if layers == 1:
            source = own_ref if layer == 0 else others_ref
            return source[fine, rows, :].astype(F32)
        return others_ref[layer, fine, rows, :].astype(F32)

    def one(fine, totals):
        for layer in range(coarse_count):
            first = tile(layer, fine, 0)
            totals = totals + first
            value = first + alight([tile(layer, fine, 1 + slot) for slot in range(3)], dims[1])
            for slot in range(PLANES):
                distance = DISTANCES[slot]
                partner = jnp.where(fine % 2 == 0, fine + distance, fine - distance) if layers > 1 else (
                    fine + distance if fine % 2 == 0 else fine - distance
                )
                value = value - tile(layer, (partner + fine_count) % fine_count, 1 + slot)
            if layers == 1:
                value = value - alight([tile(1 - layer, fine, 4 + slot) for slot in range(3)], dims[1])
                place = fine * 2 + (coarse if layer == 0 else 1 - coarse)
            else:
                if layer > 0:
                    value = value - tile(layer - 1, fine, 1 + PLANES)
                if layer < coarse_count - 1:
                    value = value - alight([tile(layer + 1, fine, 4 + slot) for slot in range(3)], dims[1])
                place = fine * coarse_count + layer
            changes_ref[place] = value
        return totals

    totals = jnp.zeros((half, LANES), F32)
    if layers > 1:
        return decode(lax.fori_loop(0, fine_count, one, totals))
    for fine in range(fine_count):
        totals = one(fine, totals)
    return decode(totals)


def solve(coeffs, near, terms, modes):
    half = 8
    places = layout_of(terms, modes)
    high = coeffs.astype(BF16)
    low = (coeffs - high.astype(F32)).astype(BF16)
    table = jnp.concatenate([high, low], axis=1)
    chunks = coeffs.shape[0] // LANES
    lanes = lane_ids(half).astype(F32)
    step = lax.broadcasted_iota(jnp.int32, (half, LANES), 0).astype(F32)
    picks = []
    for packed in near:
        ids = packed[places["ids"], :].astype(F32)
        ids = (ids[:8] * 16.0 + ids[8:]) * float(half)
        for term in range(terms):
            target = ids[term : term + 1] + step
            picks.append(
                jnp.concatenate([(target == lanes + float(LANES * c)).astype(F32) for c in range(chunks)], axis=1)
            )
    picks = jnp.concatenate(picks, axis=0).astype(BF16)
    picked = dot(picks, table)
    left = lane_ids(half) < HALF
    gap = jnp.zeros((HALF - modes, LANES), BF16)
    solutions = []
    for index, packed in enumerate(near):
        sides = []
        for part in range(2):
            columns = []
            for pair in range(0, terms, 2):
                first, second = [
                    picked[(index * terms + term) * half : (index * terms + term + 1) * half, part * LANES : (part + 1) * LANES]
                    for term in (pair, pair + 1)
                ]
                top = jnp.where(left, first, pltpu.roll(second, HALF, 1))
                bottom = jnp.where(left, pltpu.roll(first, HALF, 1), second)
                columns.append(jnp.concatenate([top, bottom], axis=0))
            sides.append(jnp.concatenate(columns, axis=1))
        rows = jnp.concatenate(sides, axis=0).astype(BF16)
        factors = []
        for term in range(terms):
            factors += [packed[term * modes : (term + 1) * modes, :], gap]
        product = dot(rows, jnp.concatenate(factors, axis=0))
        product = product[: 2 * half] + product[2 * half :]
        product = product + pltpu.roll(product, HALF, 1)
        solutions.append(product[:, :modes].astype(BF16))
    return solutions


def advance(sizes, dims, meta_ref, coeffs, residual, near_refs, rows_ref, dual_ref, theirs_ref, direction_ref,
            applied_ref):
    terms, modes = dims
    span = layout_of(terms, modes)["basis"]
    near = [ref[...] for ref in near_refs]
    solutions = solve(coeffs, near, terms, modes)
    mine = dot(solutions[0], rows_ref[residual.shape[0] :, :]).astype(BF16).astype(F32)
    for index, packed in enumerate(near[1:]):
        theirs_ref[index] = dot(solutions[index + 1], packed[span, :]).astype(BF16).astype(F32)
    pieces = []
    for block in range(PLANES + 2):
        if block < PLANES:
            place = slot_of(sizes, meta_ref[0, block])
        else:
            place = min(block, len(near) - 2)
        here = slice(block * LANES, (block + 1) * LANES)
        pieces.append(residual[:, here] + live_mask(meta_ref, block) * (mine[:, here] - theirs_ref[place]))
    direction = jnp.concatenate(pieces, axis=1)
    direction_ref[...] = direction
    applied = dot(direction.astype(BF16), dual_ref[0]).astype(BF16)
    applied_ref[...] = applied
    gamma = jnp.sum(residual * direction, axis=1, keepdims=True)
    delta = 2.0 * jnp.sum(direction * applied.astype(F32), axis=1, keepdims=True)
    half = gamma.shape[0] // 2
    lanes = lane_ids(half)
    sums = jnp.zeros((half, LANES), F32)
    for lane, values in ((GAMMA, gamma), (DELTA, delta)):
        sums = jnp.where(lanes == lane, values[:half], sums)
        sums = jnp.where(lanes == HALF + lane, values[half:], sums)
    return applied, sums


def first_kernel(sizes, dims, layers, count, meta_ref, coeffs_ref, residual_ref, rows_ref, dual_ref, *refs):
    near_refs = refs[:count]
    message_ref, direction_ref, applied_ref, theirs_ref = refs[count:]
    applied, sums = advance(
        sizes, dims, meta_ref, coeffs_ref[...], residual_ref[...], near_refs, rows_ref, dual_ref, theirs_ref,
        direction_ref, applied_ref,
    )
    cases = applied.shape[0]
    tiles = shares(sizes, dims, layers, meta_ref, applied_ref, near_refs, rows_ref, sums)
    message_ref[:, :cases, :] = jnp.zeros((message_ref.shape[0], cases, LANES), BF16)
    message_ref[:, cases:, :] = jnp.broadcast_to(tiles[None], (message_ref.shape[0],) + tiles.shape)
    post_blocks(message_ref, [meta_ref[0, b] for b in range(PLANES)], applied)
    if layers == 1:
        block = wanted_blocks(sizes, layers, meta_ref)[-1]
        message_ref[lax.axis_index("fine"), :cases, :] = applied_ref[:, lanes_of(block)]


def steps_from(totals):
    low = totals[:, GAMMA : GAMMA + 1] / totals[:, DELTA : DELTA + 1]
    high = totals[:, HALF + GAMMA : HALF + GAMMA + 1] / totals[:, HALF + DELTA : HALF + DELTA + 1]
    return low, high


def second_kernel(sizes, dims, layers, count, meta_ref, coeffs_ref, residual_ref, before_ref, applied_before_ref,
                  rows_ref, dual_ref, own_ref, *refs):
    others_refs, refs = refs[: 1 if layers == 1 else 3], refs[1 if layers == 1 else 3 :]
    near_refs = refs[:count]
    message_ref, residual_out, multipliers_out, direction_ref, applied_ref, theirs_ref, changes_ref = refs[count:]
    cases = residual_ref.shape[0]
    half = cases // 2
    low, high = steps_from(collect(sizes, dims, layers, cases, own_ref, others_refs[0], changes_ref))
    step = jnp.concatenate([low, high], axis=0)
    packed_step = jnp.where(lane_ids(half) < HALF, low, high)
    coeffs = coeffs_ref[...] - (changes_ref[...] * packed_step[None]).reshape(coeffs_ref.shape)
    facing = [own_ref[meta_ref[0, b], :cases, :] for b in range(PLANES)]
    if layers == 1:
        facing += [others_refs[0][lax.axis_index("fine"), :cases, :]] * 2
    else:
        facing += [ref[...] for ref in others_refs[1:]]
    image, _, _ = difference(meta_ref, applied_before_ref[...], facing)
    residual = residual_ref[...] - step * jnp.concatenate(image, axis=1)
    residual_out[...] = residual
    multipliers_out[...] = step * before_ref[...]
    applied, sums = advance(
        sizes, dims, meta_ref, coeffs, residual, near_refs, rows_ref, dual_ref, theirs_ref, direction_ref, applied_ref
    )
    message_ref[:, :cases, :] = jnp.zeros((message_ref.shape[0], cases, LANES), BF16)
    message_ref[:, cases:, :] = jnp.broadcast_to(encode(sums).astype(BF16)[None], (message_ref.shape[0], half, LANES))
    post_blocks(message_ref, facing_subs(sizes, meta_ref), applied)


def last_kernel(sizes, meta_ref, arrived_ref, applied_ref, residual_ref, multipliers_ref, direction_ref,
                multipliers_out, residual_out):
    cases = applied_ref.shape[0]
    totals = jnp.sum(arrived_ref[:, cases:, :].astype(F32), axis=0)
    step = jnp.concatenate(steps_from(decode(totals)), axis=0)
    facing = [arrived_ref[target, :cases, :] for target in facing_subs(sizes, meta_ref)]
    image, _, _ = difference(meta_ref, applied_ref[...], facing)
    fine = lax.axis_index("fine")
    for block in range(PLANES + 2):
        span = slice(block * LANES, (block + 1) * LANES)
        if block < PLANES:
            sign = jnp.where(fine < meta_ref[0, block], 1.0, -1.0).astype(F32)
        else:
            sign = -1.0 if block == PLANES else 1.0
        multipliers_out[0, :, span] = sign * (multipliers_ref[:, span] + step * direction_ref[:, span])
        residual_out[0, :, span] = sign * (residual_ref[:, span] - step * image[block])


SMEM = pl.BlockSpec(memory_space=pltpu.SMEM)
VMEM = pl.BlockSpec(memory_space=pltpu.VMEM)


HBM = pl.BlockSpec(memory_space=pltpu.HBM)
ANY = pl.BlockSpec(memory_space=pl.ANY)


def call(kernel, name, scalars, arrays, outs, scratch=(), far=(), after=()):
    return pl.pallas_call(
        kernel,
        name=name,
        out_shape=[jax.ShapeDtypeStruct(shape, dtype) for shape, dtype in outs],
        in_specs=[SMEM] * len(scalars) + [VMEM] * len(arrays) + [HBM] * len(far) + [ANY] * len(after),
        out_specs=[VMEM] * len(outs),
        scratch_shapes=list(scratch),
        compiler_params=pltpu.CompilerParams(vmem_limit_bytes=40 * 1024 * 1024),
    )(*scalars, *arrays, *far, *after)


def body(load_cases, dual_ops, coarse_basis, factor_blocks, pattern, partners, row_counts):
    cases, width = load_cases.shape[1:]
    terms, modes = factor_blocks.shape[1:3]
    fine_count = lax.axis_size("fine")
    coarse_count = lax.axis_size("coarse")
    subs = fine_count * coarse_count
    sizes = (fine_count, coarse_count)
    dims = (terms, modes)
    half = cases // 2
    layers = 1 if coarse_count == 2 else 2

    def swap_all(message):
        return lax.all_to_all(message, AXES, 0, 0, tiled=True)

    def swap_slot(message, slot):
        distance = DISTANCES[slot]
        pairs = [(i, (i + distance if i % 2 == 0 else i - distance) % fine_count) for i in range(fine_count)]
        return lax.ppermute(message, "fine", pairs)

    def swap_blocks(messages):
        received = [swap_slot(messages[slot], slot) for slot in range(PLANES)]
        if layers == 1:
            return received + [lax.ppermute(messages[PLANES], "coarse", [(0, 1), (1, 0)])]
        up = [(i, i + 1) for i in range(coarse_count - 1)]
        lower = lax.ppermute(messages[PLANES + 1], "coarse", up)
        return received + [lower, lax.ppermute(messages[PLANES], "coarse", [(j, i) for i, j in up])]

    full = ((cases, width), F32)
    half_full = ((cases, width), BF16)
    coded = ((subs, half, LANES), F32)
    dma = pltpu.SemaphoreType.DMA

    meta = jnp.concatenate([partners, row_counts, pattern], axis=1)
    rows = jnp.concatenate([load_cases[0], coarse_basis[0]], axis=0)
    loads_span = layout_of(terms, modes)["loads"]
    packed = call(
        functools.partial(pack_kernel, sizes, layers, cases),
        "pack_setup",
        (meta,),
        (rows, factor_blocks),
        [((loads_span.stop, LANES), BF16)] * (PLANES + layers),
    )
    received = swap_blocks(packed)
    near = [packed[-1]] + received
    count = len(near)
    theirs = [pltpu.VMEM((count - 1, cases, LANES), F32)]

    [dual] = call(dual_kernel, "fetch_dual", (), (), [(dual_ops.shape, BF16)], [dma((1,))], (dual_ops,), (packed[-1],))
    residual, message = call(
        functools.partial(first_restrict_kernel, sizes, dims, layers),
        "restrict_residual",
        (meta,),
        (rows, *received),
        [full, coded],
        [pltpu.VMEM((PLANES, cases, LANES), BF16)],
        after=(dual,),
    )
    coeffs = swap_all(message).reshape(subs * half, LANES)

    tiles = PLANES + layers
    message, direction, applied = call(
        functools.partial(first_kernel, sizes, dims, layers, count),
        "first_direction",
        (meta,),
        (coeffs, residual, rows, dual, *near),
        [((fine_count, cases + tiles * half, LANES), BF16), full, half_full],
        theirs,
    )
    own = lax.all_to_all(message, "fine", 0, 0, tiled=True)
    if layers == 1:
        others = [lax.ppermute(own, "coarse", [(0, 1), (1, 0)])]
    else:
        up = [(i, i + 1) for i in range(coarse_count - 1)]
        lower = lax.ppermute(applied[:, (PLANES + 1) * LANES :], "coarse", up)
        upper = lax.ppermute(applied[:, PLANES * LANES : (PLANES + 1) * LANES], "coarse", [(j, i) for i, j in up])
        others = [lax.all_gather(own, "coarse"), lower, upper]

    message, residual, multipliers, direction, applied = call(
        functools.partial(second_kernel, sizes, dims, layers, count),
        "second_direction",
        (meta,),
        (coeffs, residual, direction, applied, rows, dual, own, *others, *near),
        [((subs, cases + half, LANES), BF16), full, full, full, half_full],
        theirs + [pltpu.VMEM((subs, half, LANES), F32)],
    )
    arrived = swap_all(message)
    out = ((1, cases, width), F32)
    multipliers, residual = call(
        functools.partial(last_kernel, sizes),
        "finish",
        (meta,),
        (arrived, applied, residual, multipliers, direction),
        [out, out],
    )
    return multipliers, residual


def solution(mesh):
    rows = P(AXES, None, None)
    return jax.shard_map(
        body,
        mesh=mesh,
        in_specs=(rows, rows, rows, P(AXES, None, None, None), P(AXES, None), P(AXES, None), P(AXES, None)),
        out_specs=(rows, rows),
        check_vma=False,
    )
```

```python
import functools

import jax
import jax.numpy as jnp
from jax import lax
from jax.experimental import pallas as pl
from jax.experimental.pallas import tpu as pltpu
from jax.sharding import PartitionSpec as P

PLANES = 6
DISTANCES = (11, 9, 7, 3, 5, 1)
AXES = ("fine", "coarse")
LANES = 128
HALF = 64
BF16 = jnp.bfloat16
F32 = jnp.float32
GAMMA = 48
DELTA = 49


def lane_ids(rows):
    return lax.broadcasted_iota(jnp.int32, (rows, LANES), 1)


def dot(a, b):
    return lax.dot_general(a, b, (((1,), (0,)), ((), ())), preferred_element_type=F32)


def wanted_blocks(sizes, layers, meta_ref):
    slots = [slot_of(sizes, meta_ref[0, b]) for b in range(PLANES)]
    blocks = []
    for slot in range(PLANES):
        blocks.append(sum(jnp.where(slots[b] == slot, b, 0) for b in range(PLANES)))
    if layers == 1:
        return blocks + [jnp.where(lax.axis_index("coarse") == 0, PLANES + 1, PLANES)]
    return blocks + [PLANES, PLANES + 1]


def lanes_of(block):
    start = block * LANES
    return pl.ds(start if isinstance(start, int) else pl.multiple_of(start, LANES), LANES)


def facing_subs(sizes, partners_ref):
    fine_count, coarse_count = sizes
    fine = lax.axis_index("fine")
    coarse = lax.axis_index("coarse")
    me = fine * coarse_count + coarse
    subs = [partners_ref[0, b] * coarse_count + coarse for b in range(PLANES)]
    subs.append(jnp.where(coarse > 0, me - 1, me))
    subs.append(jnp.where(coarse < coarse_count - 1, me + 1, me))
    return subs


def slot_of(sizes, partner):
    fine_count = sizes[0]
    fine = lax.axis_index("fine")
    ahead = jnp.where(fine % 2 == 0, partner - fine, fine - partner)
    ahead = jnp.where(ahead < 0, ahead + fine_count, ahead)
    return sum(jnp.where(ahead == distance, slot, 0) for slot, distance in enumerate(DISTANCES))


def live_mask(counts_ref, block):
    return (lane_ids(1) < counts_ref[0, PLANES + block]).astype(F32)


def post_blocks(out_ref, targets, rows):
    cases = rows.shape[0]
    for block, target in enumerate(targets):
        out_ref[target, :cases, :] = rows[:, block * LANES : (block + 1) * LANES]


def fetch(pairs, sems):
    copies = [pltpu.make_async_copy(source, target, sems.at[i]) for i, (source, target) in enumerate(pairs)]
    for copy in copies:
        copy.start()
    return copies


def seat(part, rows, modes):
    gap = HALF - modes
    lane = lane_ids(rows) % HALF
    return (lane >= part * gap) & (lane < (part + 1) * gap), modes - part * gap


def board(hosts, guest, modes):
    seated = []
    for part, host in enumerate(hosts):
        mask, move = seat(part, guest.shape[0], modes)
        seated.append(host + pltpu.roll(jnp.where(mask, guest, 0.0), move, 1))
    return seated


def alight(hosts, modes):
    guest = jnp.zeros(hosts[0].shape, F32)
    for part, host in enumerate(hosts):
        mask, move = seat(part, guest.shape[0], modes)
        guest = jnp.where(mask, pltpu.roll(host, LANES - move, 1), guest)
    return guest


def pack_kernel(sizes, layers, cases, meta_ref, rows_ref, factors_ref, *outs):
    terms, modes = factors_ref.shape[1:3]
    gap = jnp.zeros((modes, HALF - modes), F32)
    parts = []
    for term in range(terms):
        whole = factors_ref[0, term]
        high = whole.astype(BF16).astype(F32)
        parts.append(jnp.concatenate([high, gap, whole - high, gap], axis=1))
    factors = jnp.concatenate(board(parts[:-1], parts[-1], modes), axis=0).astype(BF16)
    row = lax.broadcasted_iota(jnp.int32, (8, LANES), 0)
    ids = jnp.zeros((8, LANES), F32)
    for term in range(terms):
        sub = meta_ref[0, 2 * PLANES + 2 + term]
        ids = jnp.where(row == term, (sub // 16).astype(F32), ids)
        ids = jnp.where(row == terms + term, (sub % 16).astype(F32), ids)
    ids = ids.astype(BF16)
    places = layout_of(terms, modes)
    for out_ref, block in zip(outs, wanted_blocks(sizes, layers, meta_ref)):
        out_ref[places["factors"], :] = factors
        out_ref[places["ids"], :] = ids
        out_ref[places["loads"], :] = rows_ref[:cases, lanes_of(block)]
        out_ref[places["basis"], :] = rows_ref[cases:, lanes_of(block)]


def layout_of(terms, modes):
    sizes = (("factors", (terms - 1) * modes), ("basis", modes), ("loads", 16), ("ids", 8))
    places, start = {}, 0
    for name, rows in sizes:
        places[name] = slice(start, start + rows)
        start += rows
    return places


def dual_kernel(dual_ref, after_ref, out_ref, sems):
    for copy in fetch([(dual_ref, out_ref)], sems):
        copy.wait()


def difference(counts_ref, mine, facing):
    result, ours, theirs = [], [], []
    for block, other in enumerate(facing):
        mask = live_mask(counts_ref, block)
        left = mine[:, block * LANES : (block + 1) * LANES].astype(F32) * mask
        right = other.astype(F32) * mask
        result.append(left - right)
        ours.append(left.astype(BF16))
        theirs.append(right.astype(BF16))
    return result, ours, theirs


def first_restrict_kernel(sizes, dims, layers, meta_ref, rows_ref, *refs):
    near_refs, (_, out_ref, message_ref, scratch_ref) = refs[: PLANES + layers], refs[PLANES + layers :]
    span = layout_of(*dims)["loads"]
    cases = out_ref.shape[0]
    for slot in range(PLANES):
        scratch_ref[slot] = near_refs[slot][span, :]
    facing = [scratch_ref[slot_of(sizes, meta_ref[0, b])] for b in range(PLANES)]
    facing += [near_refs[PLANES][span, :], near_refs[-1][span, :]]
    restrict(meta_ref, rows_ref[:cases, :], facing, rows_ref[cases:, :], out_ref, message_ref)


def twice(basis):
    gap = jnp.zeros((HALF - basis.shape[0], basis.shape[1]), BF16)
    return jnp.concatenate([basis, gap, basis, gap], axis=0)


def times_basis(rows, doubled):
    return lax.dot_general(rows, doubled, (((1,), (1,)), ((), ())), preferred_element_type=F32)


def fold(coefficients):
    half = coefficients.shape[0] // 2
    return jnp.where(lane_ids(half) < HALF, coefficients[:half], coefficients[half:])


def encode(sums):
    top = sums.astype(BF16).astype(F32)
    middle = (sums - top).astype(BF16).astype(F32)
    bottom = sums - top - middle
    return top + pltpu.roll(middle, 2, 1) + pltpu.roll(bottom, 4, 1)


def decode(totals):
    return totals + pltpu.roll(totals, LANES - 2, 1) + pltpu.roll(totals, LANES - 4, 1)


def restrict(meta_ref, mine, facing, basis, out_ref, message_ref):
    cases = mine.shape[0]
    result, ours, theirs = difference(meta_ref, mine, facing)
    for block, values in enumerate(result):
        out_ref[:, block * LANES : (block + 1) * LANES] = values
    both = jnp.concatenate([jnp.concatenate(ours, axis=1), jnp.concatenate(theirs, axis=1)], axis=0)
    coefficients = times_basis(both, twice(basis))
    message = fold(coefficients[:cases] - coefficients[cases:])
    message_ref[...] = jnp.broadcast_to(message[None], message_ref.shape)


def shares(sizes, dims, layers, meta_ref, applied_ref, near_refs, rows_ref, sums):
    cases = applied_ref.shape[0]
    span = layout_of(*dims)["basis"]
    masked = []
    for block in range(PLANES + 2):
        part = applied_ref[:, block * LANES : (block + 1) * LANES].astype(F32)
        masked.append((part * live_mask(meta_ref, block)).astype(BF16))
    own = fold(times_basis(jnp.concatenate(masked, axis=1), twice(rows_ref[cases:, :])))
    high = own.astype(BF16).astype(F32)
    tiles = []
    for near_ref, block in zip(near_refs[1:], wanted_blocks(sizes, layers, meta_ref)):
        part = applied_ref[:, lanes_of(block)].astype(F32) * live_mask(meta_ref, block)
        tiles.append(fold(times_basis(part.astype(BF16), twice(near_ref[span, :]))))
    modes = dims[1]
    hosts = board(tiles[:3], own - high, modes) + board(tiles[3:PLANES], tiles[PLANES], modes)
    return jnp.concatenate([high + encode(sums)] + hosts + tiles[PLANES + 1 :], axis=0).astype(BF16)


def collect(sizes, dims, layers, cases, own_ref, others_ref, changes_ref):
    fine_count, coarse_count = sizes
    half = cases // 2
    coarse = lax.axis_index("coarse")

    def tile(layer, fine, index):
        rows = slice(cases + index * half, cases + (index + 1) * half)
        if layers == 1:
            source = own_ref if layer == 0 else others_ref
            return source[fine, rows, :].astype(F32)
        return others_ref[layer, fine, rows, :].astype(F32)

    def one(fine, totals):
        for layer in range(coarse_count):
            first = tile(layer, fine, 0)
            totals = totals + first
            value = first + alight([tile(layer, fine, 1 + slot) for slot in range(3)], dims[1])
            for slot in range(PLANES):
                distance = DISTANCES[slot]
                partner = jnp.where(fine % 2 == 0, fine + distance, fine - distance) if layers > 1 else (
                    fine + distance if fine % 2 == 0 else fine - distance
                )
                value = value - tile(layer, (partner + fine_count) % fine_count, 1 + slot)
            if layers == 1:
                value = value - alight([tile(1 - layer, fine, 4 + slot) for slot in range(3)], dims[1])
                place = fine * 2 + (coarse if layer == 0 else 1 - coarse)
            else:
                if layer > 0:
                    value = value - tile(layer - 1, fine, 1 + PLANES)
                if layer < coarse_count - 1:
                    value = value - alight([tile(layer + 1, fine, 4 + slot) for slot in range(3)], dims[1])
                place = fine * coarse_count + layer
            changes_ref[place] = value
        return totals

    totals = jnp.zeros((half, LANES), F32)
    if layers > 1:
        return decode(lax.fori_loop(0, fine_count, one, totals))
    for fine in range(fine_count):
        totals = one(fine, totals)
    return decode(totals)


def prepare(sizes, dims, near_refs, picks_ref, factors_ref):
    terms, modes = dims
    places = layout_of(terms, modes)
    half = 8
    chunks = sizes[0] * sizes[1] * half // LANES
    lanes = lane_ids(half).astype(F32)
    step = lax.broadcasted_iota(jnp.int32, (half, LANES), 0).astype(F32)
    gap = jnp.zeros((HALF - modes, LANES), BF16)
    for index, near_ref in enumerate(near_refs):
        ids = near_ref[places["ids"], :].astype(F32)
        ids = (ids[:terms] * 16.0 + ids[terms : 2 * terms]) * float(half)
        picks = []
        for term in range(terms):
            target = ids[term : term + 1] + step
            picks.append(
                jnp.concatenate([(target == lanes + float(LANES * c)).astype(F32) for c in range(chunks)], axis=1)
            )
        rows = terms * half
        picks_ref[index * rows : (index + 1) * rows, :] = jnp.concatenate(picks, axis=0).astype(BF16)
        packed = [near_ref[term * modes : (term + 1) * modes, :] for term in range(terms - 1)]
        packed.append(alight([part.astype(F32) for part in packed], modes).astype(BF16))
        for term, part in enumerate(packed):
            factors_ref[index, term * HALF : term * HALF + modes, :] = part
            factors_ref[index, term * HALF + modes : (term + 1) * HALF, :] = gap


def solve(coeffs, dims, picks_ref, factors_ref):
    terms, modes = dims
    half = 8
    high = coeffs.astype(BF16)
    low = (coeffs - high.astype(F32)).astype(BF16)
    picked = dot(picks_ref[...], jnp.concatenate([high, low], axis=1))
    left = lane_ids(half) < HALF
    solutions = []
    for index in range(factors_ref.shape[0]):
        sides = []
        for part in range(2):
            columns = []
            for pair in range(0, terms, 2):
                first, second = [
                    picked[(index * terms + term) * half : (index * terms + term + 1) * half, part * LANES : (part + 1) * LANES]
                    for term in (pair, pair + 1)
                ]
                top = jnp.where(left, first, pltpu.roll(second, HALF, 1))
                bottom = jnp.where(left, pltpu.roll(first, HALF, 1), second)
                columns.append(jnp.concatenate([top, bottom], axis=0))
            sides.append(jnp.concatenate(columns, axis=1))
        rows = jnp.concatenate(sides, axis=0).astype(BF16)
        product = dot(rows, factors_ref[index])
        product = product[: 2 * half] + product[2 * half :]
        product = product + pltpu.roll(product, HALF, 1)
        solutions.append(product[:, :modes].astype(BF16))
    return solutions


def advance(sizes, dims, meta_ref, coeffs, residual, near_refs, picks_ref, factors_ref, rows_ref, dual_ref, theirs_ref,
            direction_ref, applied_ref):
    span = layout_of(*dims)["basis"]
    solutions = solve(coeffs, dims, picks_ref, factors_ref)
    mine = dot(solutions[0], rows_ref[residual.shape[0] :, :]).astype(BF16).astype(F32)
    for index, near_ref in enumerate(near_refs[1:]):
        theirs_ref[index] = dot(solutions[index + 1], near_ref[span, :]).astype(BF16).astype(F32)
    pieces = []
    for block in range(PLANES + 2):
        if block < PLANES:
            place = slot_of(sizes, meta_ref[0, block])
        else:
            place = min(block, len(near_refs) - 2)
        here = slice(block * LANES, (block + 1) * LANES)
        pieces.append(residual[:, here] + live_mask(meta_ref, block) * (mine[:, here] - theirs_ref[place]))
    direction = jnp.concatenate(pieces, axis=1)
    direction_ref[...] = direction
    applied = dot(direction.astype(BF16), dual_ref[0]).astype(BF16)
    applied_ref[...] = applied
    gamma = jnp.sum(residual * direction, axis=1, keepdims=True)
    delta = 2.0 * jnp.sum(direction * applied.astype(F32), axis=1, keepdims=True)
    half = gamma.shape[0] // 2
    lanes = lane_ids(half)
    sums = jnp.zeros((half, LANES), F32)
    for lane, values in ((GAMMA, gamma), (DELTA, delta)):
        sums = jnp.where(lanes == lane, values[:half], sums)
        sums = jnp.where(lanes == HALF + lane, values[half:], sums)
    return applied, sums


def first_kernel(sizes, dims, layers, count, meta_ref, coeffs_ref, residual_ref, rows_ref, dual_ref, *refs):
    near_refs = refs[:count]
    message_ref, direction_ref, applied_ref, picks_ref, factors_ref, theirs_ref = refs[count:]
    prepare(sizes, dims, near_refs, picks_ref, factors_ref)
    applied, sums = advance(
        sizes, dims, meta_ref, coeffs_ref[...], residual_ref[...], near_refs, picks_ref, factors_ref, rows_ref, dual_ref,
        theirs_ref, direction_ref, applied_ref,
    )
    cases = applied.shape[0]
    tiles = shares(sizes, dims, layers, meta_ref, applied_ref, near_refs, rows_ref, sums)
    message_ref[:, :cases, :] = jnp.zeros((message_ref.shape[0], cases, LANES), BF16)
    message_ref[:, cases:, :] = jnp.broadcast_to(tiles[None], (message_ref.shape[0],) + tiles.shape)
    post_blocks(message_ref, [meta_ref[0, b] for b in range(PLANES)], applied)
    if layers == 1:
        block = wanted_blocks(sizes, layers, meta_ref)[-1]
        message_ref[lax.axis_index("fine"), :cases, :] = applied_ref[:, lanes_of(block)]


def steps_from(totals):
    low = totals[:, GAMMA : GAMMA + 1] / totals[:, DELTA : DELTA + 1]
    high = totals[:, HALF + GAMMA : HALF + GAMMA + 1] / totals[:, HALF + DELTA : HALF + DELTA + 1]
    return low, high


def second_kernel(sizes, dims, layers, count, meta_ref, coeffs_ref, residual_ref, before_ref, applied_before_ref,
                  picks_ref, factors_ref, rows_ref, dual_ref, own_ref, *refs):
    others_refs, refs = refs[: 1 if layers == 1 else 3], refs[1 if layers == 1 else 3 :]
    near_refs = refs[:count]
    message_ref, residual_out, multipliers_out, direction_ref, applied_ref, theirs_ref, changes_ref = refs[count:]
    cases = residual_ref.shape[0]
    half = cases // 2
    low, high = steps_from(collect(sizes, dims, layers, cases, own_ref, others_refs[0], changes_ref))
    step = jnp.concatenate([low, high], axis=0)
    packed_step = jnp.where(lane_ids(half) < HALF, low, high)
    coeffs = coeffs_ref[...] - (changes_ref[...] * packed_step[None]).reshape(coeffs_ref.shape)
    facing = [own_ref[meta_ref[0, b], :cases, :] for b in range(PLANES)]
    if layers == 1:
        facing += [others_refs[0][lax.axis_index("fine"), :cases, :]] * 2
    else:
        facing += [ref[...] for ref in others_refs[1:]]
    image, _, _ = difference(meta_ref, applied_before_ref[...], facing)
    residual = residual_ref[...] - step * jnp.concatenate(image, axis=1)
    residual_out[...] = residual
    multipliers_out[...] = step * before_ref[...]
    applied, sums = advance(
        sizes, dims, meta_ref, coeffs, residual, near_refs, picks_ref, factors_ref, rows_ref, dual_ref, theirs_ref,
        direction_ref, applied_ref,
    )
    message_ref[:, :cases, :] = jnp.zeros((message_ref.shape[0], cases, LANES), BF16)
    message_ref[:, cases:, :] = jnp.broadcast_to(encode(sums).astype(BF16)[None], (message_ref.shape[0], half, LANES))
    post_blocks(message_ref, facing_subs(sizes, meta_ref), applied)


def last_kernel(sizes, meta_ref, arrived_ref, applied_ref, residual_ref, multipliers_ref, direction_ref,
                multipliers_out, residual_out):
    cases = applied_ref.shape[0]
    totals = jnp.sum(arrived_ref[:, cases:, :].astype(F32), axis=0)
    step = jnp.concatenate(steps_from(decode(totals)), axis=0)
    facing = [arrived_ref[target, :cases, :] for target in facing_subs(sizes, meta_ref)]
    image, _, _ = difference(meta_ref, applied_ref[...], facing)
    fine = lax.axis_index("fine")
    for block in range(PLANES + 2):
        span = slice(block * LANES, (block + 1) * LANES)
        if block < PLANES:
            sign = jnp.where(fine < meta_ref[0, block], 1.0, -1.0).astype(F32)
        else:
            sign = -1.0 if block == PLANES else 1.0
        multipliers_out[0, :, span] = sign * (multipliers_ref[:, span] + step * direction_ref[:, span])
        residual_out[0, :, span] = sign * (residual_ref[:, span] - step * image[block])


SMEM = pl.BlockSpec(memory_space=pltpu.SMEM)
VMEM = pl.BlockSpec(memory_space=pltpu.VMEM)


HBM = pl.BlockSpec(memory_space=pltpu.HBM)
ANY = pl.BlockSpec(memory_space=pl.ANY)


def call(kernel, name, scalars, arrays, outs, scratch=(), far=(), after=()):
    return pl.pallas_call(
        kernel,
        name=name,
        out_shape=[jax.ShapeDtypeStruct(shape, dtype) for shape, dtype in outs],
        in_specs=[SMEM] * len(scalars) + [VMEM] * len(arrays) + [HBM] * len(far) + [ANY] * len(after),
        out_specs=[VMEM] * len(outs),
        scratch_shapes=list(scratch),
        compiler_params=pltpu.CompilerParams(vmem_limit_bytes=40 * 1024 * 1024),
    )(*scalars, *arrays, *far, *after)


def body(load_cases, dual_ops, coarse_basis, factor_blocks, pattern, partners, row_counts):
    cases, width = load_cases.shape[1:]
    terms, modes = factor_blocks.shape[1:3]
    fine_count = lax.axis_size("fine")
    coarse_count = lax.axis_size("coarse")
    subs = fine_count * coarse_count
    sizes = (fine_count, coarse_count)
    dims = (terms, modes)
    half = cases // 2
    layers = 1 if coarse_count == 2 else 2

    def swap_all(message):
        return lax.all_to_all(message, AXES, 0, 0, tiled=True)

    def swap_slot(message, slot):
        distance = DISTANCES[slot]
        pairs = [(i, (i + distance if i % 2 == 0 else i - distance) % fine_count) for i in range(fine_count)]
        return lax.ppermute(message, "fine", pairs)

    def swap_blocks(messages):
        received = [swap_slot(messages[slot], slot) for slot in range(PLANES)]
        if layers == 1:
            return received + [lax.ppermute(messages[PLANES], "coarse", [(0, 1), (1, 0)])]
        up = [(i, i + 1) for i in range(coarse_count - 1)]
        lower = lax.ppermute(messages[PLANES + 1], "coarse", up)
        return received + [lower, lax.ppermute(messages[PLANES], "coarse", [(j, i) for i, j in up])]

    full = ((cases, width), F32)
    half_full = ((cases, width), BF16)
    coded = ((subs, half, LANES), F32)
    dma = pltpu.SemaphoreType.DMA

    meta = jnp.concatenate([partners, row_counts, pattern], axis=1)
    rows = jnp.concatenate([load_cases[0], coarse_basis[0]], axis=0)
    packed = call(
        functools.partial(pack_kernel, sizes, layers, cases),
        "pack_setup",
        (meta,),
        (rows, factor_blocks),
        [((layout_of(terms, modes)["ids"].stop, LANES), BF16)] * (PLANES + layers),
    )
    received = swap_blocks(packed)
    near = [packed[-1]] + received
    count = len(near)
    theirs = [pltpu.VMEM((count - 1, cases, LANES), F32)]

    [dual] = call(dual_kernel, "fetch_dual", (), (), [(dual_ops.shape, BF16)], [dma((1,))], (dual_ops,), (packed[-1],))
    residual, message = call(
        functools.partial(first_restrict_kernel, sizes, dims, layers),
        "restrict_residual",
        (meta,),
        (rows, *received),
        [full, coded],
        [pltpu.VMEM((PLANES, cases, LANES), BF16)],
        after=(dual,),
    )
    coeffs = swap_all(message).reshape(subs * half, LANES)

    tiles = PLANES + layers
    message, direction, applied, picks, factors = call(
        functools.partial(first_kernel, sizes, dims, layers, count),
        "first_direction",
        (meta,),
        (coeffs, residual, rows, dual, *near),
        [((fine_count, cases + tiles * half, LANES), BF16), full, half_full, ((count * terms * half, subs * half), BF16),
         ((count, terms * HALF, LANES), BF16)],
        theirs,
    )
    own = lax.all_to_all(message, "fine", 0, 0, tiled=True)
    if layers == 1:
        others = [lax.ppermute(own, "coarse", [(0, 1), (1, 0)])]
    else:
        up = [(i, i + 1) for i in range(coarse_count - 1)]
        lower = lax.ppermute(applied[:, (PLANES + 1) * LANES :], "coarse", up)
        upper = lax.ppermute(applied[:, PLANES * LANES : (PLANES + 1) * LANES], "coarse", [(j, i) for i, j in up])
        others = [lax.all_gather(own, "coarse"), lower, upper]

    message, residual, multipliers, direction, applied = call(
        functools.partial(second_kernel, sizes, dims, layers, count),
        "second_direction",
        (meta,),
        (coeffs, residual, direction, applied, picks, factors, rows, dual, own, *others, *near),
        [((subs, cases + half, LANES), BF16), full, full, full, half_full],
        theirs + [pltpu.VMEM((subs, half, LANES), F32)],
    )
    arrived = swap_all(message)
    out = ((1, cases, width), F32)
    multipliers, residual = call(
        functools.partial(last_kernel, sizes),
        "finish",
        (meta,),
        (arrived, applied, residual, multipliers, direction),
        [out, out],
    )
    return multipliers, residual


def solution(mesh):
    rows = P(AXES, None, None)
    return jax.shard_map(
        body,
        mesh=mesh,
        in_specs=(rows, rows, rows, P(AXES, None, None, None), P(AXES, None), P(AXES, None), P(AXES, None)),
        out_specs=(rows, rows),
        check_vma=False,
    )
```

```python
import functools

import jax
import jax.numpy as jnp
from jax import lax
from jax.experimental import pallas as pl
from jax.experimental.pallas import tpu as pltpu
from jax.sharding import PartitionSpec as P

PLANES = 6
DISTANCES = (11, 9, 7, 3, 5, 1)
AXES = ("fine", "coarse")
LANES = 128
HALF = 64
BF16 = jnp.bfloat16
F32 = jnp.float32
GAMMA = 48
DELTA = 49


def lane_ids(rows):
    return lax.broadcasted_iota(jnp.int32, (rows, LANES), 1)


def dot(a, b):
    return lax.dot_general(a, b, (((1,), (0,)), ((), ())), preferred_element_type=F32)


def wanted_blocks(sizes, layers, meta_ref):
    slots = [slot_of(sizes, meta_ref[0, b]) for b in range(PLANES)]
    blocks = []
    for slot in range(PLANES):
        blocks.append(sum(jnp.where(slots[b] == slot, b, 0) for b in range(PLANES)))
    if layers == 1:
        return blocks + [jnp.where(lax.axis_index("coarse") == 0, PLANES + 1, PLANES)]
    return blocks + [PLANES, PLANES + 1]


def lanes_of(block):
    start = block * LANES
    return pl.ds(start if isinstance(start, int) else pl.multiple_of(start, LANES), LANES)


def facing_subs(sizes, partners_ref):
    fine_count, coarse_count = sizes
    fine = lax.axis_index("fine")
    coarse = lax.axis_index("coarse")
    me = fine * coarse_count + coarse
    subs = [partners_ref[0, b] * coarse_count + coarse for b in range(PLANES)]
    subs.append(jnp.where(coarse > 0, me - 1, me))
    subs.append(jnp.where(coarse < coarse_count - 1, me + 1, me))
    return subs


def slot_of(sizes, partner):
    fine_count = sizes[0]
    fine = lax.axis_index("fine")
    ahead = jnp.where(fine % 2 == 0, partner - fine, fine - partner)
    ahead = jnp.where(ahead < 0, ahead + fine_count, ahead)
    return sum(jnp.where(ahead == distance, slot, 0) for slot, distance in enumerate(DISTANCES))


def live_mask(counts_ref, block):
    return (lane_ids(1) < counts_ref[0, PLANES + block]).astype(F32)


def post_blocks(out_ref, targets, rows):
    cases = rows.shape[0]
    for block, target in enumerate(targets):
        out_ref[target, :cases, :] = rows[:, block * LANES : (block + 1) * LANES]


def fetch(pairs, sems):
    copies = [pltpu.make_async_copy(source, target, sems.at[i]) for i, (source, target) in enumerate(pairs)]
    for copy in copies:
        copy.start()
    return copies


def seat(part, rows, modes):
    gap = HALF - modes
    lane = lane_ids(rows) % HALF
    return (lane >= part * gap) & (lane < (part + 1) * gap), modes - part * gap


def board(hosts, guest, modes):
    seated = []
    for part, host in enumerate(hosts):
        mask, move = seat(part, guest.shape[0], modes)
        seated.append(host + pltpu.roll(jnp.where(mask, guest, 0.0), move, 1))
    return seated


def alight(hosts, modes):
    guest = jnp.zeros(hosts[0].shape, F32)
    for part, host in enumerate(hosts):
        mask, move = seat(part, guest.shape[0], modes)
        guest = jnp.where(mask, pltpu.roll(host, LANES - move, 1), guest)
    return guest


def pack_kernel(sizes, layers, partners_ref, counts_ref, pattern_ref, loads_ref, basis_ref, factors_hbm, *refs):
    meta_out, rows_ref = refs[:2]
    outs, (partners_smem, counts_smem, pattern_smem, loads, basis, factors_ref, sems) = refs[2:-7], refs[-7:]
    sources = (partners_ref, counts_ref, pattern_ref, loads_ref, basis_ref, factors_hbm)
    targets = (partners_smem, counts_smem, pattern_smem, loads, basis, factors_ref)
    for copy in fetch(list(zip(sources, targets)), sems):
        copy.wait()
    terms, modes = factors_ref.shape[1:3]
    cases = loads.shape[1]
    lane = lane_ids(1)
    meta = jnp.zeros((1, LANES), jnp.int32)
    scalars = [partners_smem[0, b] for b in range(PLANES)]
    scalars += [counts_smem[0, b] for b in range(PLANES + 2)]
    for place, scalar in enumerate(scalars):
        meta = jnp.where(lane == place, scalar, meta)
    meta_out[...] = meta
    rows_ref[:cases, :] = loads[0]
    rows_ref[cases:, :] = basis[0]
    gap = jnp.zeros((modes, HALF - modes), F32)
    parts = []
    for term in range(terms):
        whole = factors_ref[0, term]
        high = whole.astype(BF16).astype(F32)
        parts.append(jnp.concatenate([high, gap, whole - high, gap], axis=1))
    factors = jnp.concatenate(board(parts[:-1], parts[-1], modes), axis=0).astype(BF16)
    row = lax.broadcasted_iota(jnp.int32, (8, LANES), 0)
    ids = jnp.zeros((8, LANES), F32)
    for term in range(terms):
        sub = pattern_smem[0, term]
        ids = jnp.where(row == term, (sub // 16).astype(F32), ids)
        ids = jnp.where(row == terms + term, (sub % 16).astype(F32), ids)
    ids = ids.astype(BF16)
    places = layout_of(terms, modes)
    for out_ref, block in zip(outs, wanted_blocks(sizes, layers, partners_smem)):
        out_ref[places["factors"], :] = factors
        out_ref[places["ids"], :] = ids
        out_ref[places["loads"], :] = rows_ref[:cases, lanes_of(block)]
        out_ref[places["basis"], :] = rows_ref[cases:, lanes_of(block)]


def layout_of(terms, modes):
    sizes = (("factors", (terms - 1) * modes), ("basis", modes), ("loads", 16), ("ids", 8))
    places, start = {}, 0
    for name, rows in sizes:
        places[name] = slice(start, start + rows)
        start += rows
    return places


def stage_kernel(*refs):
    sources, targets, sems = refs[: len(refs) // 2], refs[len(refs) // 2 : -1], refs[-1]
    for copy in fetch(list(zip(sources, targets)), sems):
        copy.wait()


def difference(counts_ref, mine, facing):
    result, ours, theirs = [], [], []
    for block, other in enumerate(facing):
        mask = live_mask(counts_ref, block)
        left = mine[:, block * LANES : (block + 1) * LANES].astype(F32) * mask
        right = other.astype(F32) * mask
        result.append(left - right)
        ours.append(left.astype(BF16))
        theirs.append(right.astype(BF16))
    return result, ours, theirs


def first_restrict_kernel(sizes, dims, layers, meta_ref, rows_ref, *refs):
    near_refs, (_, out_ref, message_ref, scratch_ref) = refs[: PLANES + layers], refs[PLANES + layers :]
    span = layout_of(*dims)["loads"]
    cases = out_ref.shape[0]
    for slot in range(PLANES):
        scratch_ref[slot] = near_refs[slot][span, :]
    facing = [scratch_ref[slot_of(sizes, meta_ref[0, b])] for b in range(PLANES)]
    facing += [near_refs[PLANES][span, :], near_refs[-1][span, :]]
    restrict(meta_ref, rows_ref[:cases, :], facing, rows_ref[cases:, :], out_ref, message_ref)


def twice(basis):
    gap = jnp.zeros((HALF - basis.shape[0], basis.shape[1]), BF16)
    return jnp.concatenate([basis, gap, basis, gap], axis=0)


def times_basis(rows, doubled):
    return lax.dot_general(rows, doubled, (((1,), (1,)), ((), ())), preferred_element_type=F32)


def fold(coefficients):
    half = coefficients.shape[0] // 2
    return jnp.where(lane_ids(half) < HALF, coefficients[:half], coefficients[half:])


def encode(sums):
    top = sums.astype(BF16).astype(F32)
    middle = (sums - top).astype(BF16).astype(F32)
    bottom = sums - top - middle
    return top + pltpu.roll(middle, 2, 1) + pltpu.roll(bottom, 4, 1)


def decode(totals):
    return totals + pltpu.roll(totals, LANES - 2, 1) + pltpu.roll(totals, LANES - 4, 1)


def restrict(meta_ref, mine, facing, basis, out_ref, message_ref):
    cases = mine.shape[0]
    result, ours, theirs = difference(meta_ref, mine, facing)
    for block, values in enumerate(result):
        out_ref[:, block * LANES : (block + 1) * LANES] = values
    both = jnp.concatenate([jnp.concatenate(ours, axis=1), jnp.concatenate(theirs, axis=1)], axis=0)
    coefficients = times_basis(both, twice(basis))
    message = fold(coefficients[:cases] - coefficients[cases:])
    message_ref[...] = jnp.broadcast_to(message[None], message_ref.shape)


def shares(sizes, dims, layers, meta_ref, applied_ref, near_refs, rows_ref, sums):
    cases = applied_ref.shape[0]
    span = layout_of(*dims)["basis"]
    masked = []
    for block in range(PLANES + 2):
        part = applied_ref[:, block * LANES : (block + 1) * LANES].astype(F32)
        masked.append((part * live_mask(meta_ref, block)).astype(BF16))
    own = fold(times_basis(jnp.concatenate(masked, axis=1), twice(rows_ref[cases:, :])))
    high = own.astype(BF16).astype(F32)
    tiles = []
    for near_ref, block in zip(near_refs[1:], wanted_blocks(sizes, layers, meta_ref)):
        part = applied_ref[:, lanes_of(block)].astype(F32) * live_mask(meta_ref, block)
        tiles.append(fold(times_basis(part.astype(BF16), twice(near_ref[span, :]))))
    modes = dims[1]
    hosts = board(tiles[:3], own - high, modes) + board(tiles[3:PLANES], tiles[PLANES], modes)
    return jnp.concatenate([high + encode(sums)] + hosts + tiles[PLANES + 1 :], axis=0).astype(BF16)


def collect(sizes, dims, layers, cases, own_ref, others_ref, changes_ref):
    fine_count, coarse_count = sizes
    half = cases // 2
    coarse = lax.axis_index("coarse")

    def tile(layer, fine, index):
        rows = slice(cases + index * half, cases + (index + 1) * half)
        if layers == 1:
            source = own_ref if layer == 0 else others_ref
            return source[fine, rows, :].astype(F32)
        return others_ref[layer, fine, rows, :].astype(F32)

    def one(fine, totals):
        for layer in range(coarse_count):
            first = tile(layer, fine, 0)
            totals = totals + first
            value = first + alight([tile(layer, fine, 1 + slot) for slot in range(3)], dims[1])
            for slot in range(PLANES):
                distance = DISTANCES[slot]
                partner = jnp.where(fine % 2 == 0, fine + distance, fine - distance) if layers > 1 else (
                    fine + distance if fine % 2 == 0 else fine - distance
                )
                value = value - tile(layer, (partner + fine_count) % fine_count, 1 + slot)
            if layers == 1:
                value = value - alight([tile(1 - layer, fine, 4 + slot) for slot in range(3)], dims[1])
                place = fine * 2 + (coarse if layer == 0 else 1 - coarse)
            else:
                if layer > 0:
                    value = value - tile(layer - 1, fine, 1 + PLANES)
                if layer < coarse_count - 1:
                    value = value - alight([tile(layer + 1, fine, 4 + slot) for slot in range(3)], dims[1])
                place = fine * coarse_count + layer
            changes_ref[place] = value
        return totals

    totals = jnp.zeros((half, LANES), F32)
    if layers > 1:
        return decode(lax.fori_loop(0, fine_count, one, totals))
    for fine in range(fine_count):
        totals = one(fine, totals)
    return decode(totals)


def prepare(sizes, dims, near_refs, picks_ref, factors_ref):
    terms, modes = dims
    places = layout_of(terms, modes)
    half = 8
    chunks = sizes[0] * sizes[1] * half // LANES
    lanes = lane_ids(half).astype(F32)
    step = lax.broadcasted_iota(jnp.int32, (half, LANES), 0).astype(F32)
    gap = jnp.zeros((HALF - modes, LANES), BF16)
    for index, near_ref in enumerate(near_refs):
        ids = near_ref[places["ids"], :].astype(F32)
        ids = (ids[:terms] * 16.0 + ids[terms : 2 * terms]) * float(half)
        picks = []
        for term in range(terms):
            target = ids[term : term + 1] + step
            picks.append(
                jnp.concatenate([(target == lanes + float(LANES * c)).astype(F32) for c in range(chunks)], axis=1)
            )
        rows = terms * half
        picks_ref[index * rows : (index + 1) * rows, :] = jnp.concatenate(picks, axis=0).astype(BF16)
        packed = [near_ref[term * modes : (term + 1) * modes, :] for term in range(terms - 1)]
        packed.append(alight([part.astype(F32) for part in packed], modes).astype(BF16))
        for term, part in enumerate(packed):
            factors_ref[index, term * HALF : term * HALF + modes, :] = part
            factors_ref[index, term * HALF + modes : (term + 1) * HALF, :] = gap


def solve(coeffs, dims, picks_ref, factors_ref):
    terms, modes = dims
    half = 8
    high = coeffs.astype(BF16)
    low = (coeffs - high.astype(F32)).astype(BF16)
    picked = dot(picks_ref[...], jnp.concatenate([high, low], axis=1))
    left = lane_ids(half) < HALF
    solutions = []
    for index in range(factors_ref.shape[0]):
        sides = []
        for part in range(2):
            columns = []
            for pair in range(0, terms, 2):
                first, second = [
                    picked[(index * terms + term) * half : (index * terms + term + 1) * half, part * LANES : (part + 1) * LANES]
                    for term in (pair, pair + 1)
                ]
                top = jnp.where(left, first, pltpu.roll(second, HALF, 1))
                bottom = jnp.where(left, pltpu.roll(first, HALF, 1), second)
                columns.append(jnp.concatenate([top, bottom], axis=0))
            sides.append(jnp.concatenate(columns, axis=1))
        rows = jnp.concatenate(sides, axis=0).astype(BF16)
        product = dot(rows, factors_ref[index])
        product = product[: 2 * half] + product[2 * half :]
        product = product + pltpu.roll(product, HALF, 1)
        solutions.append(product[:, :modes].astype(BF16))
    return solutions


def advance(sizes, dims, meta_ref, coeffs, residual, near_refs, picks_ref, factors_ref, rows_ref, dual_ref, theirs_ref,
            direction_ref, applied_ref):
    span = layout_of(*dims)["basis"]
    solutions = solve(coeffs, dims, picks_ref, factors_ref)
    mine = dot(solutions[0], rows_ref[residual.shape[0] :, :]).astype(BF16).astype(F32)
    for index, near_ref in enumerate(near_refs[1:]):
        theirs_ref[index] = dot(solutions[index + 1], near_ref[span, :]).astype(BF16).astype(F32)
    pieces = []
    for block in range(PLANES + 2):
        if block < PLANES:
            place = slot_of(sizes, meta_ref[0, block])
        else:
            place = min(block, len(near_refs) - 2)
        here = slice(block * LANES, (block + 1) * LANES)
        pieces.append(residual[:, here] + live_mask(meta_ref, block) * (mine[:, here] - theirs_ref[place]))
    direction = jnp.concatenate(pieces, axis=1)
    direction_ref[...] = direction
    applied = dot(direction.astype(BF16), dual_ref[0]).astype(BF16)
    applied_ref[...] = applied
    gamma = jnp.sum(residual * direction, axis=1, keepdims=True)
    delta = 2.0 * jnp.sum(direction * applied.astype(F32), axis=1, keepdims=True)
    half = gamma.shape[0] // 2
    lanes = lane_ids(half)
    sums = jnp.zeros((half, LANES), F32)
    for lane, values in ((GAMMA, gamma), (DELTA, delta)):
        sums = jnp.where(lanes == lane, values[:half], sums)
        sums = jnp.where(lanes == HALF + lane, values[half:], sums)
    return applied, sums


def first_kernel(sizes, dims, layers, count, meta_ref, coeffs_ref, residual_ref, rows_ref, dual_ref, *refs):
    near_refs = refs[:count]
    message_ref, direction_ref, applied_ref, picks_ref, factors_ref, theirs_ref = refs[count:]
    prepare(sizes, dims, near_refs, picks_ref, factors_ref)
    applied, sums = advance(
        sizes, dims, meta_ref, coeffs_ref[...], residual_ref[...], near_refs, picks_ref, factors_ref, rows_ref, dual_ref,
        theirs_ref, direction_ref, applied_ref,
    )
    cases = applied.shape[0]
    tiles = shares(sizes, dims, layers, meta_ref, applied_ref, near_refs, rows_ref, sums)
    message_ref[:, :cases, :] = jnp.zeros((message_ref.shape[0], cases, LANES), BF16)
    message_ref[:, cases:, :] = jnp.broadcast_to(tiles[None], (message_ref.shape[0],) + tiles.shape)
    post_blocks(message_ref, [meta_ref[0, b] for b in range(PLANES)], applied)
    if layers == 1:
        block = wanted_blocks(sizes, layers, meta_ref)[-1]
        message_ref[lax.axis_index("fine"), :cases, :] = applied_ref[:, lanes_of(block)]


def steps_from(totals):
    low = totals[:, GAMMA : GAMMA + 1] / totals[:, DELTA : DELTA + 1]
    high = totals[:, HALF + GAMMA : HALF + GAMMA + 1] / totals[:, HALF + DELTA : HALF + DELTA + 1]
    return low, high


def second_kernel(sizes, dims, layers, count, meta_ref, coeffs_ref, residual_ref, before_ref, applied_before_ref,
                  picks_ref, factors_ref, rows_ref, dual_ref, own_ref, *refs):
    others_refs, refs = refs[: 1 if layers == 1 else 3], refs[1 if layers == 1 else 3 :]
    near_refs = refs[:count]
    message_ref, residual_out, multipliers_out, direction_ref, applied_ref, theirs_ref, changes_ref = refs[count:]
    cases = residual_ref.shape[0]
    half = cases // 2
    low, high = steps_from(collect(sizes, dims, layers, cases, own_ref, others_refs[0], changes_ref))
    step = jnp.concatenate([low, high], axis=0)
    packed_step = jnp.where(lane_ids(half) < HALF, low, high)
    coeffs = coeffs_ref[...] - (changes_ref[...] * packed_step[None]).reshape(coeffs_ref.shape)
    facing = [own_ref[meta_ref[0, b], :cases, :] for b in range(PLANES)]
    if layers == 1:
        facing += [others_refs[0][lax.axis_index("fine"), :cases, :]] * 2
    else:
        facing += [ref[...] for ref in others_refs[1:]]
    image, _, _ = difference(meta_ref, applied_before_ref[...], facing)
    residual = residual_ref[...] - step * jnp.concatenate(image, axis=1)
    residual_out[...] = residual
    multipliers_out[...] = step * before_ref[...]
    applied, sums = advance(
        sizes, dims, meta_ref, coeffs, residual, near_refs, picks_ref, factors_ref, rows_ref, dual_ref, theirs_ref,
        direction_ref, applied_ref,
    )
    message_ref[:, :cases, :] = jnp.zeros((message_ref.shape[0], cases, LANES), BF16)
    message_ref[:, cases:, :] = jnp.broadcast_to(encode(sums).astype(BF16)[None], (message_ref.shape[0], half, LANES))
    post_blocks(message_ref, facing_subs(sizes, meta_ref), applied)


def last_kernel(sizes, meta_ref, arrived_ref, applied_ref, residual_ref, multipliers_ref, direction_ref,
                multipliers_out, residual_out):
    cases = applied_ref.shape[0]
    totals = jnp.sum(arrived_ref[:, cases:, :].astype(F32), axis=0)
    step = jnp.concatenate(steps_from(decode(totals)), axis=0)
    facing = [arrived_ref[target, :cases, :] for target in facing_subs(sizes, meta_ref)]
    image, _, _ = difference(meta_ref, applied_ref[...], facing)
    fine = lax.axis_index("fine")
    for block in range(PLANES + 2):
        span = slice(block * LANES, (block + 1) * LANES)
        if block < PLANES:
            sign = jnp.where(fine < meta_ref[0, block], 1.0, -1.0).astype(F32)
        else:
            sign = -1.0 if block == PLANES else 1.0
        multipliers_out[0, :, span] = sign * (multipliers_ref[:, span] + step * direction_ref[:, span])
        residual_out[0, :, span] = sign * (residual_ref[:, span] - step * image[block])


SMEM = pl.BlockSpec(memory_space=pltpu.SMEM)
VMEM = pl.BlockSpec(memory_space=pltpu.VMEM)


HBM = pl.BlockSpec(memory_space=pltpu.HBM)
ANY = pl.BlockSpec(memory_space=pl.ANY)


def call(kernel, name, scalars, arrays, outs, scratch=(), far=(), after=(), vmem=40):
    return pl.pallas_call(
        kernel,
        name=name,
        out_shape=[jax.ShapeDtypeStruct(shape, dtype) for shape, dtype in outs],
        in_specs=[SMEM] * len(scalars) + [VMEM] * len(arrays) + [HBM] * len(far) + [ANY] * len(after),
        out_specs=[VMEM] * len(outs),
        scratch_shapes=list(scratch),
        compiler_params=pltpu.CompilerParams(vmem_limit_bytes=vmem * 1024 * 1024),
    )(*scalars, *arrays, *far, *after)


def body(load_cases, dual_ops, coarse_basis, factor_blocks, pattern, partners, row_counts):
    cases, width = load_cases.shape[1:]
    terms, modes = factor_blocks.shape[1:3]
    fine_count = lax.axis_size("fine")
    coarse_count = lax.axis_size("coarse")
    subs = fine_count * coarse_count
    sizes = (fine_count, coarse_count)
    dims = (terms, modes)
    half = cases // 2
    layers = 1 if coarse_count == 2 else 2

    def swap_all(message):
        return lax.all_to_all(message, AXES, 0, 0, tiled=True)

    def swap_slot(message, slot):
        distance = DISTANCES[slot]
        pairs = [(i, (i + distance if i % 2 == 0 else i - distance) % fine_count) for i in range(fine_count)]
        return lax.ppermute(message, "fine", pairs)

    def swap_blocks(messages):
        received = [swap_slot(messages[slot], slot) for slot in range(PLANES)]
        if layers == 1:
            return received + [lax.ppermute(messages[PLANES], "coarse", [(0, 1), (1, 0)])]
        up = [(i, i + 1) for i in range(coarse_count - 1)]
        lower = lax.ppermute(messages[PLANES + 1], "coarse", up)
        return received + [lower, lax.ppermute(messages[PLANES], "coarse", [(j, i) for i, j in up])]

    full = ((cases, width), F32)
    half_full = ((cases, width), BF16)
    coded = ((subs, half, LANES), F32)
    dma = pltpu.SemaphoreType.DMA

    inputs = (partners, row_counts, pattern, load_cases, coarse_basis, factor_blocks)
    spaces = (pltpu.SMEM,) * 3 + (pltpu.VMEM,) * 3
    meta, rows, *packed = call(
        functools.partial(pack_kernel, sizes, layers),
        "pack_setup",
        (),
        (),
        [((1, LANES), jnp.int32), ((cases + modes, width), BF16)]
        + [((layout_of(terms, modes)["ids"].stop, LANES), BF16)] * (PLANES + layers),
        [space(array.shape, array.dtype) for space, array in zip(spaces, inputs)] + [dma((6,))],
        inputs,
        vmem=60,
    )
    received = swap_blocks(packed)
    staged = (dual_ops, meta, rows, packed[-1])
    dual, meta, rows, mine = call(
        stage_kernel, "stage_operands", (), (), [(array.shape, array.dtype) for array in staged], [dma((4,))], staged
    )
    near = [mine] + received
    count = len(near)
    theirs = [pltpu.VMEM((count - 1, cases, LANES), F32)]

    residual, message = call(
        functools.partial(first_restrict_kernel, sizes, dims, layers),
        "restrict_residual",
        (meta,),
        (rows, *received),
        [full, coded],
        [pltpu.VMEM((PLANES, cases, LANES), BF16)],
        after=(dual,),
    )
    coeffs = swap_all(message).reshape(subs * half, LANES)

    tiles = PLANES + layers
    message, direction, applied, picks, factors = call(
        functools.partial(first_kernel, sizes, dims, layers, count),
        "first_direction",
        (meta,),
        (coeffs, residual, rows, dual, *near),
        [((fine_count, cases + tiles * half, LANES), BF16), full, half_full, ((count * terms * half, subs * half), BF16),
         ((count, terms * HALF, LANES), BF16)],
        theirs,
    )
    own = lax.all_to_all(message, "fine", 0, 0, tiled=True)
    if layers == 1:
        others = [lax.ppermute(own, "coarse", [(0, 1), (1, 0)])]
    else:
        up = [(i, i + 1) for i in range(coarse_count - 1)]
        lower = lax.ppermute(applied[:, (PLANES + 1) * LANES :], "coarse", up)
        upper = lax.ppermute(applied[:, PLANES * LANES : (PLANES + 1) * LANES], "coarse", [(j, i) for i, j in up])
        others = [lax.all_gather(own, "coarse"), lower, upper]

    message, residual, multipliers, direction, applied = call(
        functools.partial(second_kernel, sizes, dims, layers, count),
        "second_direction",
        (meta,),
        (coeffs, residual, direction, applied, picks, factors, rows, dual, own, *others, *near),
        [((subs, cases + half, LANES), BF16), full, full, full, half_full],
        theirs + [pltpu.VMEM((subs, half, LANES), F32)],
    )
    arrived = swap_all(message)
    out = ((1, cases, width), F32)
    multipliers, residual = call(
        functools.partial(last_kernel, sizes),
        "finish",
        (meta,),
        (arrived, applied, residual, multipliers, direction),
        [out, out],
    )
    return multipliers, residual


def solution(mesh):
    rows = P(AXES, None, None)
    return jax.shard_map(
        body,
        mesh=mesh,
        in_specs=(rows, rows, rows, P(AXES, None, None, None), P(AXES, None), P(AXES, None), P(AXES, None)),
        out_specs=(rows, rows),
        check_vma=False,
    )
```

```python
import functools

import jax
import jax.numpy as jnp
from jax import lax
from jax.experimental import pallas as pl
from jax.experimental.pallas import tpu as pltpu
from jax.sharding import PartitionSpec as P

PLANES = 6
DISTANCES = (11, 9, 7, 3, 5, 1)
AXES = ("fine", "coarse")
LANES = 128
HALF = 64
BF16 = jnp.bfloat16
F32 = jnp.float32
SPARE = 32
GAMMA = 48
DELTA = 49


def lane_ids(rows):
    return lax.broadcasted_iota(jnp.int32, (rows, LANES), 1)


def dot(a, b):
    return lax.dot_general(a, b, (((1,), (0,)), ((), ())), preferred_element_type=F32)


def wanted_blocks(sizes, layers, meta_ref):
    slots = [slot_of(sizes, meta_ref[0, b]) for b in range(PLANES)]
    blocks = []
    for slot in range(PLANES):
        blocks.append(sum(jnp.where(slots[b] == slot, b, 0) for b in range(PLANES)))
    if layers == 1:
        return blocks + [jnp.where(lax.axis_index("coarse") == 0, PLANES + 1, PLANES)]
    return blocks + [PLANES, PLANES + 1]


def lanes_of(block):
    start = block * LANES
    return pl.ds(start if isinstance(start, int) else pl.multiple_of(start, LANES), LANES)


def facing_subs(sizes, partners_ref):
    fine_count, coarse_count = sizes
    fine = lax.axis_index("fine")
    coarse = lax.axis_index("coarse")
    me = fine * coarse_count + coarse
    subs = [partners_ref[0, b] * coarse_count + coarse for b in range(PLANES)]
    subs.append(jnp.where(coarse > 0, me - 1, me))
    subs.append(jnp.where(coarse < coarse_count - 1, me + 1, me))
    return subs


def slot_of(sizes, partner):
    fine_count = sizes[0]
    fine = lax.axis_index("fine")
    ahead = jnp.where(fine % 2 == 0, partner - fine, fine - partner)
    ahead = jnp.where(ahead < 0, ahead + fine_count, ahead)
    return sum(jnp.where(ahead == distance, slot, 0) for slot, distance in enumerate(DISTANCES))


def live_mask(counts_ref, block):
    return (lane_ids(1) < counts_ref[0, PLANES + block]).astype(F32)


def post_blocks(out_ref, targets, rows):
    cases = rows.shape[0]
    for block, target in enumerate(targets):
        out_ref[target, :cases, :] = rows[:, block * LANES : (block + 1) * LANES]


def fetch(pairs, sems):
    copies = [pltpu.make_async_copy(source, target, sems.at[i]) for i, (source, target) in enumerate(pairs)]
    for copy in copies:
        copy.start()
    return copies


def seat(part, rows, modes):
    gap = HALF - modes
    lane = lane_ids(rows) % HALF
    return (lane >= part * gap) & (lane < (part + 1) * gap), modes - part * gap


def board(hosts, guest, modes):
    seated = []
    for part, host in enumerate(hosts):
        mask, move = seat(part, guest.shape[0], modes)
        seated.append(host + pltpu.roll(jnp.where(mask, guest, 0.0), move, 1))
    return seated


def alight(hosts, modes):
    guest = jnp.zeros(hosts[0].shape, F32)
    for part, host in enumerate(hosts):
        mask, move = seat(part, guest.shape[0], modes)
        guest = jnp.where(mask, pltpu.roll(host, LANES - move, 1), guest)
    return guest


def pack_kernel(sizes, layers, partners_ref, counts_ref, pattern_ref, loads_ref, basis_ref, factors_hbm, *refs):
    rows_ref, outs = refs[0], refs[1:-7]
    partners_smem, counts_smem, pattern_smem, loads, basis, factors_ref, sems = refs[-7:]
    sources = (partners_ref, counts_ref, pattern_ref, loads_ref, basis_ref, factors_hbm)
    targets = (partners_smem, counts_smem, pattern_smem, loads, basis, factors_ref)
    for copy in fetch(list(zip(sources, targets)), sems):
        copy.wait()
    terms, modes = factors_ref.shape[1:3]
    cases = loads.shape[1]
    lane = lane_ids(8)
    row = lax.broadcasted_iota(jnp.int32, (8, LANES), 0)
    digits = jnp.zeros((8, LANES), F32)
    scalars = [partners_smem[0, b] for b in range(PLANES)]
    scalars += [counts_smem[0, b] for b in range(PLANES + 2)]
    for place, scalar in enumerate(scalars):
        digit = jnp.where(row == 0, scalar // 16, scalar % 16).astype(F32)
        digits = jnp.where(lane == place, digit, digits)
    rows_ref[:cases, :] = loads[0]
    rows_ref[cases : cases + modes, :] = basis[0]
    gap = jnp.zeros((modes, HALF - modes), F32)
    parts = []
    for term in range(terms):
        whole = factors_ref[0, term]
        high = whole.astype(BF16).astype(F32)
        parts.append(jnp.concatenate([high, gap, whole - high, gap], axis=1))
    factors = jnp.concatenate(board(parts[:-1], parts[-1], modes), axis=0).astype(BF16)
    ids = jnp.zeros((8, LANES), F32)
    for term in range(terms):
        sub = pattern_smem[0, term]
        ids = jnp.where(row == term, (sub // 16).astype(F32), ids)
        ids = jnp.where(row == terms + term, (sub % 16).astype(F32), ids)
    ids = ids.astype(BF16)
    places = layout_of(terms, modes)
    start = cases + modes
    depth = modes // 2
    rows_ref[start:, :] = jnp.zeros_like(rows_ref[start:, :])
    for group in range(2 * (terms - 1)):
        rows_ref[start : start + depth, group * LANES : (group + 1) * LANES] = factors[group * depth : (group + 1) * depth]
    rows_ref[start : start + 8, 6 * LANES : 7 * LANES] = ids
    rows_ref[start : start + 8, 7 * LANES :] = digits.astype(BF16)
    for out_ref, block in zip(outs, wanted_blocks(sizes, layers, partners_smem)):
        out_ref[places["factors"], :] = factors
        out_ref[places["ids"], :] = ids
        out_ref[places["loads"], :] = rows_ref[:cases, lanes_of(block)]
        out_ref[places["basis"], :] = rows_ref[cases:start, lanes_of(block)]


def layout_of(terms, modes):
    sizes = (("factors", (terms - 1) * modes), ("basis", modes), ("loads", 16), ("ids", 8))
    places, start = {}, 0
    for name, rows in sizes:
        places[name] = slice(start, start + rows)
        start += rows
    return places


def stage_kernel(start, dual_ref, rows_ref, dual_out, rows_out, meta_out, sems):
    copies = fetch([(dual_ref, dual_out), (rows_ref, rows_out)], sems)
    copies[1].wait()
    digits = rows_out[start : start + 8, 7 * LANES :].astype(F32)
    meta_out[...] = (digits[0:1] * 16.0 + digits[1:2]).astype(jnp.int32)
    copies[0].wait()


def basis_of(rows_ref, cases):
    return rows_ref[cases : rows_ref.shape[0] - SPARE, :]


def own_setup(dims, cases, rows_ref):
    terms, modes = dims
    start, depth = cases + modes, modes // 2
    groups = [
        rows_ref[start : start + depth, group * LANES : (group + 1) * LANES] for group in range(2 * (terms - 1))
    ]
    parts = [jnp.concatenate(groups[2 * term : 2 * term + 2], axis=0) for term in range(terms - 1)]
    return parts, rows_ref[start : start + 8, 6 * LANES : 7 * LANES]


def difference(counts_ref, mine, facing):
    result, ours, theirs = [], [], []
    for block, other in enumerate(facing):
        mask = live_mask(counts_ref, block)
        left = mine[:, block * LANES : (block + 1) * LANES].astype(F32) * mask
        right = other.astype(F32) * mask
        result.append(left - right)
        ours.append(left.astype(BF16))
        theirs.append(right.astype(BF16))
    return result, ours, theirs


def first_restrict_kernel(sizes, dims, layers, meta_ref, rows_ref, *refs):
    near_refs, (_, out_ref, message_ref, scratch_ref) = refs[: PLANES + layers], refs[PLANES + layers :]
    span = layout_of(*dims)["loads"]
    cases = out_ref.shape[0]
    for slot in range(PLANES):
        scratch_ref[slot] = near_refs[slot][span, :]
    facing = [scratch_ref[slot_of(sizes, meta_ref[0, b])] for b in range(PLANES)]
    facing += [near_refs[PLANES][span, :], near_refs[-1][span, :]]
    restrict(meta_ref, rows_ref[:cases, :], facing, basis_of(rows_ref, cases), out_ref, message_ref)


def twice(basis):
    gap = jnp.zeros((HALF - basis.shape[0], basis.shape[1]), BF16)
    return jnp.concatenate([basis, gap, basis, gap], axis=0)


def times_basis(rows, doubled):
    return lax.dot_general(rows, doubled, (((1,), (1,)), ((), ())), preferred_element_type=F32)


def fold(coefficients):
    half = coefficients.shape[0] // 2
    return jnp.where(lane_ids(half) < HALF, coefficients[:half], coefficients[half:])


def encode(sums):
    top = sums.astype(BF16).astype(F32)
    middle = (sums - top).astype(BF16).astype(F32)
    bottom = sums - top - middle
    return top + pltpu.roll(middle, 2, 1) + pltpu.roll(bottom, 4, 1)


def decode(totals):
    return totals + pltpu.roll(totals, LANES - 2, 1) + pltpu.roll(totals, LANES - 4, 1)


def restrict(meta_ref, mine, facing, basis, out_ref, message_ref):
    cases = mine.shape[0]
    result, ours, theirs = difference(meta_ref, mine, facing)
    for block, values in enumerate(result):
        out_ref[:, block * LANES : (block + 1) * LANES] = values
    both = jnp.concatenate([jnp.concatenate(ours, axis=1), jnp.concatenate(theirs, axis=1)], axis=0)
    coefficients = times_basis(both, twice(basis))
    message = fold(coefficients[:cases] - coefficients[cases:])
    message_ref[...] = jnp.broadcast_to(message[None], message_ref.shape)


def shares(sizes, dims, layers, meta_ref, applied_ref, near_refs, rows_ref, sums):
    cases = applied_ref.shape[0]
    span = layout_of(*dims)["basis"]
    masked = []
    for block in range(PLANES + 2):
        part = applied_ref[:, block * LANES : (block + 1) * LANES].astype(F32)
        masked.append((part * live_mask(meta_ref, block)).astype(BF16))
    own = fold(times_basis(jnp.concatenate(masked, axis=1), twice(basis_of(rows_ref, cases))))
    high = own.astype(BF16).astype(F32)
    tiles = []
    for near_ref, block in zip(near_refs, wanted_blocks(sizes, layers, meta_ref)):
        part = applied_ref[:, lanes_of(block)].astype(F32) * live_mask(meta_ref, block)
        tiles.append(fold(times_basis(part.astype(BF16), twice(near_ref[span, :]))))
    modes = dims[1]
    hosts = board(tiles[:3], own - high, modes) + board(tiles[3:PLANES], tiles[PLANES], modes)
    return jnp.concatenate([high + encode(sums)] + hosts + tiles[PLANES + 1 :], axis=0).astype(BF16)


def collect(sizes, dims, layers, cases, own_ref, others_ref, changes_ref):
    fine_count, coarse_count = sizes
    half = cases // 2
    coarse = lax.axis_index("coarse")

    def tile(layer, fine, index):
        rows = slice(cases + index * half, cases + (index + 1) * half)
        if layers == 1:
            source = own_ref if layer == 0 else others_ref
            return source[fine, rows, :].astype(F32)
        return others_ref[layer, fine, rows, :].astype(F32)

    def one(fine, totals):
        for layer in range(coarse_count):
            first = tile(layer, fine, 0)
            totals = totals + first
            value = first + alight([tile(layer, fine, 1 + slot) for slot in range(3)], dims[1])
            for slot in range(PLANES):
                distance = DISTANCES[slot]
                partner = jnp.where(fine % 2 == 0, fine + distance, fine - distance) if layers > 1 else (
                    fine + distance if fine % 2 == 0 else fine - distance
                )
                value = value - tile(layer, (partner + fine_count) % fine_count, 1 + slot)
            if layers == 1:
                value = value - alight([tile(1 - layer, fine, 4 + slot) for slot in range(3)], dims[1])
                place = fine * 2 + (coarse if layer == 0 else 1 - coarse)
            else:
                if layer > 0:
                    value = value - tile(layer - 1, fine, 1 + PLANES)
                if layer < coarse_count - 1:
                    value = value - alight([tile(layer + 1, fine, 4 + slot) for slot in range(3)], dims[1])
                place = fine * coarse_count + layer
            changes_ref[place] = value
        return totals

    totals = jnp.zeros((half, LANES), F32)
    if layers > 1:
        return decode(lax.fori_loop(0, fine_count, one, totals))
    for fine in range(fine_count):
        totals = one(fine, totals)
    return decode(totals)


def prepare(sizes, dims, cases, rows_ref, near_refs, picks_ref, factors_ref):
    terms, modes = dims
    places = layout_of(terms, modes)
    half = 8
    chunks = sizes[0] * sizes[1] * half // LANES
    lanes = lane_ids(half).astype(F32)
    step = lax.broadcasted_iota(jnp.int32, (half, LANES), 0).astype(F32)
    gap = jnp.zeros((HALF - modes, LANES), BF16)
    setups = [own_setup(dims, cases, rows_ref)]
    for near_ref in near_refs:
        parts = [near_ref[term * modes : (term + 1) * modes, :] for term in range(terms - 1)]
        setups.append((parts, near_ref[places["ids"], :]))
    for index, (packed, ids) in enumerate(setups):
        ids = ids.astype(F32)
        ids = (ids[:terms] * 16.0 + ids[terms : 2 * terms]) * float(half)
        picks = []
        for term in range(terms):
            target = ids[term : term + 1] + step
            picks.append(
                jnp.concatenate([(target == lanes + float(LANES * c)).astype(F32) for c in range(chunks)], axis=1)
            )
        rows = terms * half
        picks_ref[index * rows : (index + 1) * rows, :] = jnp.concatenate(picks, axis=0).astype(BF16)
        packed = packed + [alight([part.astype(F32) for part in packed], modes).astype(BF16)]
        for term, part in enumerate(packed):
            factors_ref[index, term * HALF : term * HALF + modes, :] = part
            factors_ref[index, term * HALF + modes : (term + 1) * HALF, :] = gap


def solve(coeffs, dims, picks_ref, factors_ref):
    terms, modes = dims
    half = 8
    high = coeffs.astype(BF16)
    low = (coeffs - high.astype(F32)).astype(BF16)
    picked = dot(picks_ref[...], jnp.concatenate([high, low], axis=1))
    left = lane_ids(half) < HALF
    solutions = []
    for index in range(factors_ref.shape[0]):
        sides = []
        for part in range(2):
            columns = []
            for pair in range(0, terms, 2):
                first, second = [
                    picked[(index * terms + term) * half : (index * terms + term + 1) * half, part * LANES : (part + 1) * LANES]
                    for term in (pair, pair + 1)
                ]
                top = jnp.where(left, first, pltpu.roll(second, HALF, 1))
                bottom = jnp.where(left, pltpu.roll(first, HALF, 1), second)
                columns.append(jnp.concatenate([top, bottom], axis=0))
            sides.append(jnp.concatenate(columns, axis=1))
        rows = jnp.concatenate(sides, axis=0).astype(BF16)
        product = dot(rows, factors_ref[index])
        product = product[: 2 * half] + product[2 * half :]
        product = product + pltpu.roll(product, HALF, 1)
        solutions.append(product[:, :modes].astype(BF16))
    return solutions


def advance(sizes, dims, meta_ref, coeffs, residual, near_refs, picks_ref, factors_ref, rows_ref, dual_ref, theirs_ref,
            direction_ref, applied_ref):
    span = layout_of(*dims)["basis"]
    solutions = solve(coeffs, dims, picks_ref, factors_ref)
    mine = dot(solutions[0], basis_of(rows_ref, residual.shape[0])).astype(BF16).astype(F32)
    for index, near_ref in enumerate(near_refs):
        theirs_ref[index] = dot(solutions[index + 1], near_ref[span, :]).astype(BF16).astype(F32)
    pieces = []
    for block in range(PLANES + 2):
        if block < PLANES:
            place = slot_of(sizes, meta_ref[0, block])
        else:
            place = min(block, len(near_refs) - 1)
        here = slice(block * LANES, (block + 1) * LANES)
        pieces.append(residual[:, here] + live_mask(meta_ref, block) * (mine[:, here] - theirs_ref[place]))
    direction = jnp.concatenate(pieces, axis=1)
    direction_ref[...] = direction
    applied = dot(direction.astype(BF16), dual_ref[0]).astype(BF16)
    applied_ref[...] = applied
    gamma = jnp.sum(residual * direction, axis=1, keepdims=True)
    delta = 2.0 * jnp.sum(direction * applied.astype(F32), axis=1, keepdims=True)
    half = gamma.shape[0] // 2
    lanes = lane_ids(half)
    sums = jnp.zeros((half, LANES), F32)
    for lane, values in ((GAMMA, gamma), (DELTA, delta)):
        sums = jnp.where(lanes == lane, values[:half], sums)
        sums = jnp.where(lanes == HALF + lane, values[half:], sums)
    return applied, sums


def first_kernel(sizes, dims, layers, count, meta_ref, coeffs_ref, residual_ref, rows_ref, dual_ref, *refs):
    near_refs = refs[:count]
    message_ref, direction_ref, applied_ref, picks_ref, factors_ref, theirs_ref = refs[count:]
    prepare(sizes, dims, residual_ref.shape[0], rows_ref, near_refs, picks_ref, factors_ref)
    applied, sums = advance(
        sizes, dims, meta_ref, coeffs_ref[...], residual_ref[...], near_refs, picks_ref, factors_ref, rows_ref, dual_ref,
        theirs_ref, direction_ref, applied_ref,
    )
    cases = applied.shape[0]
    tiles = shares(sizes, dims, layers, meta_ref, applied_ref, near_refs, rows_ref, sums)
    message_ref[:, :cases, :] = jnp.zeros((message_ref.shape[0], cases, LANES), BF16)
    message_ref[:, cases:, :] = jnp.broadcast_to(tiles[None], (message_ref.shape[0],) + tiles.shape)
    post_blocks(message_ref, [meta_ref[0, b] for b in range(PLANES)], applied)
    if layers == 1:
        block = wanted_blocks(sizes, layers, meta_ref)[-1]
        message_ref[lax.axis_index("fine"), :cases, :] = applied_ref[:, lanes_of(block)]


def steps_from(totals):
    low = totals[:, GAMMA : GAMMA + 1] / totals[:, DELTA : DELTA + 1]
    high = totals[:, HALF + GAMMA : HALF + GAMMA + 1] / totals[:, HALF + DELTA : HALF + DELTA + 1]
    return low, high


def second_kernel(sizes, dims, layers, count, meta_ref, coeffs_ref, residual_ref, before_ref, applied_before_ref,
                  picks_ref, factors_ref, rows_ref, dual_ref, own_ref, *refs):
    others_refs, refs = refs[: 1 if layers == 1 else 3], refs[1 if layers == 1 else 3 :]
    near_refs = refs[:count]
    message_ref, residual_out, multipliers_out, direction_ref, applied_ref, theirs_ref, changes_ref = refs[count:]
    cases = residual_ref.shape[0]
    half = cases // 2
    low, high = steps_from(collect(sizes, dims, layers, cases, own_ref, others_refs[0], changes_ref))
    step = jnp.concatenate([low, high], axis=0)
    packed_step = jnp.where(lane_ids(half) < HALF, low, high)
    coeffs = coeffs_ref[...] - (changes_ref[...] * packed_step[None]).reshape(coeffs_ref.shape)
    facing = [own_ref[meta_ref[0, b], :cases, :] for b in range(PLANES)]
    if layers == 1:
        facing += [others_refs[0][lax.axis_index("fine"), :cases, :]] * 2
    else:
        facing += [ref[...] for ref in others_refs[1:]]
    image, _, _ = difference(meta_ref, applied_before_ref[...], facing)
    residual = residual_ref[...] - step * jnp.concatenate(image, axis=1)
    residual_out[...] = residual
    multipliers_out[...] = step * before_ref[...]
    applied, sums = advance(
        sizes, dims, meta_ref, coeffs, residual, near_refs, picks_ref, factors_ref, rows_ref, dual_ref, theirs_ref,
        direction_ref, applied_ref,
    )
    message_ref[:, :cases, :] = jnp.zeros((message_ref.shape[0], cases, LANES), BF16)
    message_ref[:, cases:, :] = jnp.broadcast_to(encode(sums).astype(BF16)[None], (message_ref.shape[0], half, LANES))
    post_blocks(message_ref, facing_subs(sizes, meta_ref), applied)


def last_kernel(sizes, meta_ref, arrived_ref, applied_ref, residual_ref, multipliers_ref, direction_ref,
                multipliers_out, residual_out):
    cases = applied_ref.shape[0]
    totals = jnp.sum(arrived_ref[:, cases:, :].astype(F32), axis=0)
    step = jnp.concatenate(steps_from(decode(totals)), axis=0)
    facing = [arrived_ref[target, :cases, :] for target in facing_subs(sizes, meta_ref)]
    image, _, _ = difference(meta_ref, applied_ref[...], facing)
    fine = lax.axis_index("fine")
    for block in range(PLANES + 2):
        span = slice(block * LANES, (block + 1) * LANES)
        if block < PLANES:
            sign = jnp.where(fine < meta_ref[0, block], 1.0, -1.0).astype(F32)
        else:
            sign = -1.0 if block == PLANES else 1.0
        multipliers_out[0, :, span] = sign * (multipliers_ref[:, span] + step * direction_ref[:, span])
        residual_out[0, :, span] = sign * (residual_ref[:, span] - step * image[block])


SMEM = pl.BlockSpec(memory_space=pltpu.SMEM)
VMEM = pl.BlockSpec(memory_space=pltpu.VMEM)


HBM = pl.BlockSpec(memory_space=pltpu.HBM)
ANY = pl.BlockSpec(memory_space=pl.ANY)


def call(kernel, name, scalars, arrays, outs, scratch=(), far=(), after=(), vmem=40):
    return pl.pallas_call(
        kernel,
        name=name,
        out_shape=[jax.ShapeDtypeStruct(shape, dtype) for shape, dtype in outs],
        in_specs=[SMEM] * len(scalars) + [VMEM] * len(arrays) + [HBM] * len(far) + [ANY] * len(after),
        out_specs=[VMEM] * len(outs),
        scratch_shapes=list(scratch),
        compiler_params=pltpu.CompilerParams(vmem_limit_bytes=vmem * 1024 * 1024),
    )(*scalars, *arrays, *far, *after)


def body(load_cases, dual_ops, coarse_basis, factor_blocks, pattern, partners, row_counts):
    cases, width = load_cases.shape[1:]
    terms, modes = factor_blocks.shape[1:3]
    fine_count = lax.axis_size("fine")
    coarse_count = lax.axis_size("coarse")
    subs = fine_count * coarse_count
    sizes = (fine_count, coarse_count)
    dims = (terms, modes)
    half = cases // 2
    layers = 1 if coarse_count == 2 else 2

    def swap_all(message):
        return lax.all_to_all(message, AXES, 0, 0, tiled=True)

    def swap_slot(message, slot):
        distance = DISTANCES[slot]
        pairs = [(i, (i + distance if i % 2 == 0 else i - distance) % fine_count) for i in range(fine_count)]
        return lax.ppermute(message, "fine", pairs)

    def swap_blocks(messages):
        received = [swap_slot(messages[slot], slot) for slot in range(PLANES)]
        if layers == 1:
            return received + [lax.ppermute(messages[PLANES], "coarse", [(0, 1), (1, 0)])]
        up = [(i, i + 1) for i in range(coarse_count - 1)]
        lower = lax.ppermute(messages[PLANES + 1], "coarse", up)
        return received + [lower, lax.ppermute(messages[PLANES], "coarse", [(j, i) for i, j in up])]

    full = ((cases, width), F32)
    half_full = ((cases, width), BF16)
    coded = ((subs, half, LANES), F32)
    dma = pltpu.SemaphoreType.DMA

    inputs = (partners, row_counts, pattern, load_cases, coarse_basis, factor_blocks)
    spaces = (pltpu.SMEM,) * 3 + (pltpu.VMEM,) * 3
    rows, *packed = call(
        functools.partial(pack_kernel, sizes, layers),
        "pack_setup",
        (),
        (),
        [((cases + modes + SPARE, width), BF16)]
        + [((layout_of(terms, modes)["ids"].stop, LANES), BF16)] * (PLANES + layers),
        [space(array.shape, array.dtype) for space, array in zip(spaces, inputs)] + [dma((6,))],
        inputs,
        vmem=60,
    )
    received = swap_blocks(packed)
    dual, rows, meta = call(
        functools.partial(stage_kernel, cases + modes),
        "stage_operands",
        (),
        (),
        [(dual_ops.shape, BF16), (rows.shape, BF16), ((1, LANES), jnp.int32)],
        [dma((2,))],
        (dual_ops, rows),
    )
    count = len(received)
    theirs = [pltpu.VMEM((count, cases, LANES), F32)]

    residual, message = call(
        functools.partial(first_restrict_kernel, sizes, dims, layers),
        "restrict_residual",
        (meta,),
        (rows, *received),
        [full, coded],
        [pltpu.VMEM((PLANES, cases, LANES), BF16)],
        after=(dual,),
    )
    coeffs = swap_all(message).reshape(subs * half, LANES)

    tiles = PLANES + layers
    message, direction, applied, picks, factors = call(
        functools.partial(first_kernel, sizes, dims, layers, count),
        "first_direction",
        (meta,),
        (coeffs, residual, rows, dual, *received),
        [((fine_count, cases + tiles * half, LANES), BF16), full, half_full, (((count + 1) * terms * half, subs * half), BF16),
         ((count + 1, terms * HALF, LANES), BF16)],
        theirs,
    )
    own = lax.all_to_all(message, "fine", 0, 0, tiled=True)
    if layers == 1:
        others = [lax.ppermute(own, "coarse", [(0, 1), (1, 0)])]
    else:
        up = [(i, i + 1) for i in range(coarse_count - 1)]
        lower = lax.ppermute(applied[:, (PLANES + 1) * LANES :], "coarse", up)
        upper = lax.ppermute(applied[:, PLANES * LANES : (PLANES + 1) * LANES], "coarse", [(j, i) for i, j in up])
        others = [lax.all_gather(own, "coarse"), lower, upper]

    message, residual, multipliers, direction, applied = call(
        functools.partial(second_kernel, sizes, dims, layers, count),
        "second_direction",
        (meta,),
        (coeffs, residual, direction, applied, picks, factors, rows, dual, own, *others, *received),
        [((subs, cases + half, LANES), BF16), full, full, full, half_full],
        theirs + [pltpu.VMEM((subs, half, LANES), F32)],
    )
    arrived = swap_all(message)
    out = ((1, cases, width), F32)
    multipliers, residual = call(
        functools.partial(last_kernel, sizes),
        "finish",
        (meta,),
        (arrived, applied, residual, multipliers, direction),
        [out, out],
    )
    return multipliers, residual


def solution(mesh):
    rows = P(AXES, None, None)
    return jax.shard_map(
        body,
        mesh=mesh,
        in_specs=(rows, rows, rows, P(AXES, None, None, None), P(AXES, None), P(AXES, None), P(AXES, None)),
        out_specs=(rows, rows),
        check_vma=False,
    )
```

```python
import functools

import jax
import jax.numpy as jnp
from jax import lax
from jax.experimental import pallas as pl
from jax.experimental.pallas import tpu as pltpu
from jax.sharding import PartitionSpec as P

PLANES = 6
DISTANCES = (11, 7, 3, 5, 9, 1)
AXES = ("fine", "coarse")
LANES = 128
HALF = 64
BF16 = jnp.bfloat16
F32 = jnp.float32
SPARE = 32
GAMMA = 48
DELTA = 49


def lane_ids(rows):
    return lax.broadcasted_iota(jnp.int32, (rows, LANES), 1)


def dot(a, b):
    return lax.dot_general(a, b, (((1,), (0,)), ((), ())), preferred_element_type=F32)


def wanted_blocks(sizes, layers, meta_ref):
    slots = [slot_of(sizes, meta_ref[0, b]) for b in range(PLANES)]
    blocks = []
    for slot in range(PLANES):
        blocks.append(sum(jnp.where(slots[b] == slot, b, 0) for b in range(PLANES)))
    if layers == 1:
        return blocks + [jnp.where(lax.axis_index("coarse") == 0, PLANES + 1, PLANES)]
    return blocks + [PLANES, PLANES + 1]


def lanes_of(block):
    start = block * LANES
    return pl.ds(start if isinstance(start, int) else pl.multiple_of(start, LANES), LANES)


def facing_subs(sizes, partners_ref):
    fine_count, coarse_count = sizes
    fine = lax.axis_index("fine")
    coarse = lax.axis_index("coarse")
    me = fine * coarse_count + coarse
    subs = [partners_ref[0, b] * coarse_count + coarse for b in range(PLANES)]
    subs.append(jnp.where(coarse > 0, me - 1, me))
    subs.append(jnp.where(coarse < coarse_count - 1, me + 1, me))
    return subs


def slot_of(sizes, partner):
    fine_count = sizes[0]
    fine = lax.axis_index("fine")
    ahead = jnp.where(fine % 2 == 0, partner - fine, fine - partner)
    ahead = jnp.where(ahead < 0, ahead + fine_count, ahead)
    return sum(jnp.where(ahead == distance, slot, 0) for slot, distance in enumerate(DISTANCES))


def live_mask(counts_ref, block):
    return (lane_ids(1) < counts_ref[0, PLANES + block]).astype(F32)


def post_blocks(out_ref, targets, rows):
    cases = rows.shape[0]
    for block, target in enumerate(targets):
        out_ref[target, :cases, :] = rows[:, block * LANES : (block + 1) * LANES]


def fetch(pairs, sems):
    copies = [pltpu.make_async_copy(source, target, sems.at[i]) for i, (source, target) in enumerate(pairs)]
    for copy in copies:
        copy.start()
    return copies


def seat(part, rows, modes):
    gap = HALF - modes
    lane = lane_ids(rows) % HALF
    return (lane >= part * gap) & (lane < (part + 1) * gap), modes - part * gap


def board(hosts, guest, modes):
    seated = []
    for part, host in enumerate(hosts):
        mask, move = seat(part, guest.shape[0], modes)
        seated.append(host + pltpu.roll(jnp.where(mask, guest, 0.0), move, 1))
    return seated


def alight(hosts, modes):
    guest = jnp.zeros(hosts[0].shape, F32)
    for part, host in enumerate(hosts):
        mask, move = seat(part, guest.shape[0], modes)
        guest = jnp.where(mask, pltpu.roll(host, LANES - move, 1), guest)
    return guest


def pack_kernel(sizes, layers, partners_ref, counts_ref, pattern_ref, loads_ref, basis_ref, factors_hbm, *refs):
    rows_ref, outs = refs[0], refs[1:-7]
    partners_smem, counts_smem, pattern_smem, loads, basis, factors_ref, sems = refs[-7:]
    sources = (partners_ref, counts_ref, pattern_ref, loads_ref, basis_ref, factors_hbm)
    targets = (partners_smem, counts_smem, pattern_smem, loads, basis, factors_ref)
    for copy in fetch(list(zip(sources, targets)), sems):
        copy.wait()
    terms, modes = factors_ref.shape[1:3]
    cases = loads.shape[1]
    lane = lane_ids(8)
    row = lax.broadcasted_iota(jnp.int32, (8, LANES), 0)
    digits = jnp.zeros((8, LANES), F32)
    scalars = [partners_smem[0, b] for b in range(PLANES)]
    scalars += [counts_smem[0, b] for b in range(PLANES + 2)]
    for place, scalar in enumerate(scalars):
        digit = jnp.where(row == 0, scalar // 16, scalar % 16).astype(F32)
        digits = jnp.where(lane == place, digit, digits)
    rows_ref[:cases, :] = loads[0]
    rows_ref[cases : cases + modes, :] = basis[0]
    gap = jnp.zeros((modes, HALF - modes), F32)
    parts = []
    for term in range(terms):
        whole = factors_ref[0, term]
        high = whole.astype(BF16).astype(F32)
        parts.append(jnp.concatenate([high, gap, whole - high, gap], axis=1))
    factors = jnp.concatenate(board(parts[:-1], parts[-1], modes), axis=0).astype(BF16)
    ids = jnp.zeros((8, LANES), F32)
    for term in range(terms):
        sub = pattern_smem[0, term]
        ids = jnp.where(row == term, (sub // 16).astype(F32), ids)
        ids = jnp.where(row == terms + term, (sub % 16).astype(F32), ids)
    ids = ids.astype(BF16)
    places = layout_of(terms, modes)
    start = cases + modes
    depth = modes // 2
    rows_ref[start:, :] = jnp.zeros_like(rows_ref[start:, :])
    for group in range(2 * (terms - 1)):
        rows_ref[start : start + depth, group * LANES : (group + 1) * LANES] = factors[group * depth : (group + 1) * depth]
    rows_ref[start : start + 8, 6 * LANES : 7 * LANES] = ids
    rows_ref[start : start + 8, 7 * LANES :] = digits.astype(BF16)
    for out_ref, block in zip(outs, wanted_blocks(sizes, layers, partners_smem)):
        out_ref[places["factors"], :] = factors
        out_ref[places["ids"], :] = ids
        out_ref[places["loads"], :] = rows_ref[:cases, lanes_of(block)]
        out_ref[places["basis"], :] = rows_ref[cases:start, lanes_of(block)]


def layout_of(terms, modes):
    sizes = (("factors", (terms - 1) * modes), ("basis", modes), ("loads", 16), ("ids", 8))
    places, start = {}, 0
    for name, rows in sizes:
        places[name] = slice(start, start + rows)
        start += rows
    return places


def stage_kernel(start, dual_ref, rows_ref, dual_out, rows_out, meta_out, sems):
    copies = fetch([(dual_ref, dual_out), (rows_ref, rows_out)], sems)
    copies[1].wait()
    digits = rows_out[start : start + 8, 7 * LANES :].astype(F32)
    meta_out[...] = (digits[0:1] * 16.0 + digits[1:2]).astype(jnp.int32)
    copies[0].wait()


def basis_of(rows_ref, cases):
    return rows_ref[cases : rows_ref.shape[0] - SPARE, :]


def own_setup(dims, cases, rows_ref):
    terms, modes = dims
    start, depth = cases + modes, modes // 2
    groups = [
        rows_ref[start : start + depth, group * LANES : (group + 1) * LANES] for group in range(2 * (terms - 1))
    ]
    parts = [jnp.concatenate(groups[2 * term : 2 * term + 2], axis=0) for term in range(terms - 1)]
    return parts, rows_ref[start : start + 8, 6 * LANES : 7 * LANES]


def difference(counts_ref, mine, facing):
    result, ours, theirs = [], [], []
    for block, other in enumerate(facing):
        mask = live_mask(counts_ref, block)
        left = mine[:, block * LANES : (block + 1) * LANES].astype(F32) * mask
        right = other.astype(F32) * mask
        result.append(left - right)
        ours.append(left.astype(BF16))
        theirs.append(right.astype(BF16))
    return result, ours, theirs


def first_restrict_kernel(sizes, dims, layers, meta_ref, rows_ref, *refs):
    near_refs, (_, out_ref, message_ref, scratch_ref) = refs[: PLANES + layers], refs[PLANES + layers :]
    span = layout_of(*dims)["loads"]
    cases = out_ref.shape[0]
    for slot in range(PLANES):
        scratch_ref[slot] = near_refs[slot][span, :]
    facing = [scratch_ref[slot_of(sizes, meta_ref[0, b])] for b in range(PLANES)]
    facing += [near_refs[PLANES][span, :], near_refs[-1][span, :]]
    restrict(meta_ref, rows_ref[:cases, :], facing, basis_of(rows_ref, cases), out_ref, message_ref)


def twice(basis):
    gap = jnp.zeros((HALF - basis.shape[0], basis.shape[1]), BF16)
    return jnp.concatenate([basis, gap, basis, gap], axis=0)


def times_basis(rows, doubled):
    return lax.dot_general(rows, doubled, (((1,), (1,)), ((), ())), preferred_element_type=F32)


def fold(coefficients):
    half = coefficients.shape[0] // 2
    return jnp.where(lane_ids(half) < HALF, coefficients[:half], coefficients[half:])


def encode(sums):
    top = sums.astype(BF16).astype(F32)
    middle = (sums - top).astype(BF16).astype(F32)
    bottom = sums - top - middle
    return top + pltpu.roll(middle, 2, 1) + pltpu.roll(bottom, 4, 1)


def decode(totals):
    return totals + pltpu.roll(totals, LANES - 2, 1) + pltpu.roll(totals, LANES - 4, 1)


def restrict(meta_ref, mine, facing, basis, out_ref, message_ref):
    cases = mine.shape[0]
    result, ours, theirs = difference(meta_ref, mine, facing)
    for block, values in enumerate(result):
        out_ref[:, block * LANES : (block + 1) * LANES] = values
    both = jnp.concatenate([jnp.concatenate(ours, axis=1), jnp.concatenate(theirs, axis=1)], axis=0)
    coefficients = times_basis(both, twice(basis))
    message = fold(coefficients[:cases] - coefficients[cases:])
    message_ref[...] = jnp.broadcast_to(message[None], message_ref.shape)


def shares(sizes, dims, layers, meta_ref, applied_ref, near_refs, rows_ref, sums):
    cases = applied_ref.shape[0]
    span = layout_of(*dims)["basis"]
    masked = []
    for block in range(PLANES + 2):
        part = applied_ref[:, block * LANES : (block + 1) * LANES].astype(F32)
        masked.append((part * live_mask(meta_ref, block)).astype(BF16))
    own = fold(times_basis(jnp.concatenate(masked, axis=1), twice(basis_of(rows_ref, cases))))
    high = own.astype(BF16).astype(F32)
    tiles = []
    for near_ref, block in zip(near_refs, wanted_blocks(sizes, layers, meta_ref)):
        part = applied_ref[:, lanes_of(block)].astype(F32) * live_mask(meta_ref, block)
        tiles.append(fold(times_basis(part.astype(BF16), twice(near_ref[span, :]))))
    modes = dims[1]
    hosts = board(tiles[:3], own - high, modes) + board(tiles[3:PLANES], tiles[PLANES], modes)
    return jnp.concatenate([high + encode(sums)] + hosts + tiles[PLANES + 1 :], axis=0).astype(BF16)


def collect(sizes, dims, layers, cases, own_ref, others_ref, changes_ref):
    fine_count, coarse_count = sizes
    half = cases // 2
    coarse = lax.axis_index("coarse")

    def tile(layer, fine, index):
        rows = slice(cases + index * half, cases + (index + 1) * half)
        if layers == 1:
            source = own_ref if layer == 0 else others_ref
            return source[fine, rows, :].astype(F32)
        return others_ref[layer, fine, rows, :].astype(F32)

    def one(fine, totals):
        for layer in range(coarse_count):
            first = tile(layer, fine, 0)
            totals = totals + first
            value = first + alight([tile(layer, fine, 1 + slot) for slot in range(3)], dims[1])
            for slot in range(PLANES):
                distance = DISTANCES[slot]
                partner = jnp.where(fine % 2 == 0, fine + distance, fine - distance) if layers > 1 else (
                    fine + distance if fine % 2 == 0 else fine - distance
                )
                value = value - tile(layer, (partner + fine_count) % fine_count, 1 + slot)
            if layers == 1:
                value = value - alight([tile(1 - layer, fine, 4 + slot) for slot in range(3)], dims[1])
                place = fine * 2 + (coarse if layer == 0 else 1 - coarse)
            else:
                if layer > 0:
                    value = value - tile(layer - 1, fine, 1 + PLANES)
                if layer < coarse_count - 1:
                    value = value - alight([tile(layer + 1, fine, 4 + slot) for slot in range(3)], dims[1])
                place = fine * coarse_count + layer
            changes_ref[place] = value
        return totals

    totals = jnp.zeros((half, LANES), F32)
    if layers > 1:
        return decode(lax.fori_loop(0, fine_count, one, totals))
    for fine in range(fine_count):
        totals = one(fine, totals)
    return decode(totals)


def prepare(sizes, dims, cases, rows_ref, near_refs, picks_ref, factors_ref):
    terms, modes = dims
    places = layout_of(terms, modes)
    half = 8
    chunks = sizes[0] * sizes[1] * half // LANES
    lanes = lane_ids(half).astype(F32)
    step = lax.broadcasted_iota(jnp.int32, (half, LANES), 0).astype(F32)
    gap = jnp.zeros((HALF - modes, LANES), BF16)
    setups = [own_setup(dims, cases, rows_ref)]
    for near_ref in near_refs:
        parts = [near_ref[term * modes : (term + 1) * modes, :] for term in range(terms - 1)]
        setups.append((parts, near_ref[places["ids"], :]))
    for index, (packed, ids) in enumerate(setups):
        ids = ids.astype(F32)
        ids = (ids[:terms] * 16.0 + ids[terms : 2 * terms]) * float(half)
        picks = []
        for term in range(terms):
            target = ids[term : term + 1] + step
            picks.append(
                jnp.concatenate([(target == lanes + float(LANES * c)).astype(F32) for c in range(chunks)], axis=1)
            )
        rows = terms * half
        picks_ref[index * rows : (index + 1) * rows, :] = jnp.concatenate(picks, axis=0).astype(BF16)
        packed = packed + [alight([part.astype(F32) for part in packed], modes).astype(BF16)]
        for term, part in enumerate(packed):
            factors_ref[index, term * HALF : term * HALF + modes, :] = part
            factors_ref[index, term * HALF + modes : (term + 1) * HALF, :] = gap


def solve(coeffs, dims, picks_ref, factors_ref):
    terms, modes = dims
    half = 8
    high = coeffs.astype(BF16)
    low = (coeffs - high.astype(F32)).astype(BF16)
    picked = dot(picks_ref[...], jnp.concatenate([high, low], axis=1))
    left = lane_ids(half) < HALF
    solutions = []
    for index in range(factors_ref.shape[0]):
        sides = []
        for part in range(2):
            columns = []
            for pair in range(0, terms, 2):
                first, second = [
                    picked[(index * terms + term) * half : (index * terms + term + 1) * half, part * LANES : (part + 1) * LANES]
                    for term in (pair, pair + 1)
                ]
                top = jnp.where(left, first, pltpu.roll(second, HALF, 1))
                bottom = jnp.where(left, pltpu.roll(first, HALF, 1), second)
                columns.append(jnp.concatenate([top, bottom], axis=0))
            sides.append(jnp.concatenate(columns, axis=1))
        rows = jnp.concatenate(sides, axis=0).astype(BF16)
        product = dot(rows, factors_ref[index])
        product = product[: 2 * half] + product[2 * half :]
        product = product + pltpu.roll(product, HALF, 1)
        solutions.append(product[:, :modes].astype(BF16))
    return solutions


def advance(sizes, dims, meta_ref, coeffs, residual, near_refs, picks_ref, factors_ref, rows_ref, dual_ref, theirs_ref,
            direction_ref, applied_ref):
    span = layout_of(*dims)["basis"]
    solutions = solve(coeffs, dims, picks_ref, factors_ref)
    mine = dot(solutions[0], basis_of(rows_ref, residual.shape[0])).astype(BF16).astype(F32)
    for index, near_ref in enumerate(near_refs):
        theirs_ref[index] = dot(solutions[index + 1], near_ref[span, :]).astype(BF16).astype(F32)
    pieces = []
    for block in range(PLANES + 2):
        if block < PLANES:
            place = slot_of(sizes, meta_ref[0, block])
        else:
            place = min(block, len(near_refs) - 1)
        here = slice(block * LANES, (block + 1) * LANES)
        pieces.append(residual[:, here] + live_mask(meta_ref, block) * (mine[:, here] - theirs_ref[place]))
    direction = jnp.concatenate(pieces, axis=1)
    direction_ref[...] = direction
    applied = dot(direction.astype(BF16), dual_ref[0]).astype(BF16)
    applied_ref[...] = applied
    gamma = jnp.sum(residual * direction, axis=1, keepdims=True)
    delta = 2.0 * jnp.sum(direction * applied.astype(F32), axis=1, keepdims=True)
    half = gamma.shape[0] // 2
    lanes = lane_ids(half)
    sums = jnp.zeros((half, LANES), F32)
    for lane, values in ((GAMMA, gamma), (DELTA, delta)):
        sums = jnp.where(lanes == lane, values[:half], sums)
        sums = jnp.where(lanes == HALF + lane, values[half:], sums)
    return applied, sums


def first_kernel(sizes, dims, layers, count, meta_ref, coeffs_ref, residual_ref, rows_ref, dual_ref, *refs):
    near_refs = refs[:count]
    message_ref, direction_ref, applied_ref, picks_ref, factors_ref, theirs_ref = refs[count:]
    prepare(sizes, dims, residual_ref.shape[0], rows_ref, near_refs, picks_ref, factors_ref)
    applied, sums = advance(
        sizes, dims, meta_ref, coeffs_ref[...], residual_ref[...], near_refs, picks_ref, factors_ref, rows_ref, dual_ref,
        theirs_ref, direction_ref, applied_ref,
    )
    cases = applied.shape[0]
    tiles = shares(sizes, dims, layers, meta_ref, applied_ref, near_refs, rows_ref, sums)
    message_ref[:, :cases, :] = jnp.zeros((message_ref.shape[0], cases, LANES), BF16)
    message_ref[:, cases:, :] = jnp.broadcast_to(tiles[None], (message_ref.shape[0],) + tiles.shape)
    post_blocks(message_ref, [meta_ref[0, b] for b in range(PLANES)], applied)
    if layers == 1:
        block = wanted_blocks(sizes, layers, meta_ref)[-1]
        message_ref[lax.axis_index("fine"), :cases, :] = applied_ref[:, lanes_of(block)]


def steps_from(totals):
    low = totals[:, GAMMA : GAMMA + 1] / totals[:, DELTA : DELTA + 1]
    high = totals[:, HALF + GAMMA : HALF + GAMMA + 1] / totals[:, HALF + DELTA : HALF + DELTA + 1]
    return low, high


def second_kernel(sizes, dims, layers, count, meta_ref, coeffs_ref, residual_ref, before_ref, applied_before_ref,
                  picks_ref, factors_ref, rows_ref, dual_ref, own_ref, *refs):
    others_refs, refs = refs[: 1 if layers == 1 else 3], refs[1 if layers == 1 else 3 :]
    near_refs = refs[:count]
    message_ref, residual_out, multipliers_out, direction_ref, applied_ref, theirs_ref, changes_ref = refs[count:]
    cases = residual_ref.shape[0]
    half = cases // 2
    low, high = steps_from(collect(sizes, dims, layers, cases, own_ref, others_refs[0], changes_ref))
    step = jnp.concatenate([low, high], axis=0)
    packed_step = jnp.where(lane_ids(half) < HALF, low, high)
    coeffs = coeffs_ref[...] - (changes_ref[...] * packed_step[None]).reshape(coeffs_ref.shape)
    facing = [own_ref[meta_ref[0, b], :cases, :] for b in range(PLANES)]
    if layers == 1:
        facing += [others_refs[0][lax.axis_index("fine"), :cases, :]] * 2
    else:
        facing += [ref[...] for ref in others_refs[1:]]
    image, _, _ = difference(meta_ref, applied_before_ref[...], facing)
    residual = residual_ref[...] - step * jnp.concatenate(image, axis=1)
    residual_out[...] = residual
    multipliers_out[...] = step * before_ref[...]
    applied, sums = advance(
        sizes, dims, meta_ref, coeffs, residual, near_refs, picks_ref, factors_ref, rows_ref, dual_ref, theirs_ref,
        direction_ref, applied_ref,
    )
    message_ref[:, :cases, :] = jnp.zeros((message_ref.shape[0], cases, LANES), BF16)
    message_ref[:, cases:, :] = jnp.broadcast_to(encode(sums).astype(BF16)[None], (message_ref.shape[0], half, LANES))
    post_blocks(message_ref, facing_subs(sizes, meta_ref), applied)


def last_kernel(sizes, meta_ref, arrived_ref, applied_ref, residual_ref, multipliers_ref, direction_ref,
                multipliers_out, residual_out):
    cases = applied_ref.shape[0]
    totals = jnp.sum(arrived_ref[:, cases:, :].astype(F32), axis=0)
    step = jnp.concatenate(steps_from(decode(totals)), axis=0)
    facing = [arrived_ref[target, :cases, :] for target in facing_subs(sizes, meta_ref)]
    image, _, _ = difference(meta_ref, applied_ref[...], facing)
    fine = lax.axis_index("fine")
    for block in range(PLANES + 2):
        span = slice(block * LANES, (block + 1) * LANES)
        if block < PLANES:
            sign = jnp.where(fine < meta_ref[0, block], 1.0, -1.0).astype(F32)
        else:
            sign = -1.0 if block == PLANES else 1.0
        multipliers_out[0, :, span] = sign * (multipliers_ref[:, span] + step * direction_ref[:, span])
        residual_out[0, :, span] = sign * (residual_ref[:, span] - step * image[block])


SMEM = pl.BlockSpec(memory_space=pltpu.SMEM)
VMEM = pl.BlockSpec(memory_space=pltpu.VMEM)


HBM = pl.BlockSpec(memory_space=pltpu.HBM)
ANY = pl.BlockSpec(memory_space=pl.ANY)


def call(kernel, name, scalars, arrays, outs, scratch=(), far=(), after=(), vmem=40):
    return pl.pallas_call(
        kernel,
        name=name,
        out_shape=[jax.ShapeDtypeStruct(shape, dtype) for shape, dtype in outs],
        in_specs=[SMEM] * len(scalars) + [VMEM] * len(arrays) + [HBM] * len(far) + [ANY] * len(after),
        out_specs=[VMEM] * len(outs),
        scratch_shapes=list(scratch),
        compiler_params=pltpu.CompilerParams(vmem_limit_bytes=vmem * 1024 * 1024),
    )(*scalars, *arrays, *far, *after)


def body(load_cases, dual_ops, coarse_basis, factor_blocks, pattern, partners, row_counts):
    cases, width = load_cases.shape[1:]
    terms, modes = factor_blocks.shape[1:3]
    fine_count = lax.axis_size("fine")
    coarse_count = lax.axis_size("coarse")
    subs = fine_count * coarse_count
    sizes = (fine_count, coarse_count)
    dims = (terms, modes)
    half = cases // 2
    layers = 1 if coarse_count == 2 else 2

    def swap_all(message):
        return lax.all_to_all(message, AXES, 0, 0, tiled=True)

    def swap_slot(message, slot):
        distance = DISTANCES[slot]
        pairs = [(i, (i + distance if i % 2 == 0 else i - distance) % fine_count) for i in range(fine_count)]
        return lax.ppermute(message, "fine", pairs)

    def swap_blocks(messages):
        received = [swap_slot(messages[slot], slot) for slot in range(PLANES)]
        if layers == 1:
            return received + [lax.ppermute(messages[PLANES], "coarse", [(0, 1), (1, 0)])]
        up = [(i, i + 1) for i in range(coarse_count - 1)]
        lower = lax.ppermute(messages[PLANES + 1], "coarse", up)
        return received + [lower, lax.ppermute(messages[PLANES], "coarse", [(j, i) for i, j in up])]

    full = ((cases, width), F32)
    half_full = ((cases, width), BF16)
    coded = ((subs, half, LANES), F32)
    dma = pltpu.SemaphoreType.DMA

    inputs = (partners, row_counts, pattern, load_cases, coarse_basis, factor_blocks)
    spaces = (pltpu.SMEM,) * 3 + (pltpu.VMEM,) * 3
    rows, *packed = call(
        functools.partial(pack_kernel, sizes, layers),
        "pack_setup",
        (),
        (),
        [((cases + modes + SPARE, width), BF16)]
        + [((layout_of(terms, modes)["ids"].stop, LANES), BF16)] * (PLANES + layers),
        [space(array.shape, array.dtype) for space, array in zip(spaces, inputs)] + [dma((6,))],
        inputs,
        vmem=60,
    )
    received = swap_blocks(packed)
    dual, rows, meta = call(
        functools.partial(stage_kernel, cases + modes),
        "stage_operands",
        (),
        (),
        [(dual_ops.shape, BF16), (rows.shape, BF16), ((1, LANES), jnp.int32)],
        [dma((2,))],
        (dual_ops, rows),
    )
    count = len(received)
    theirs = [pltpu.VMEM((count, cases, LANES), F32)]

    residual, message = call(
        functools.partial(first_restrict_kernel, sizes, dims, layers),
        "restrict_residual",
        (meta,),
        (rows, *received),
        [full, coded],
        [pltpu.VMEM((PLANES, cases, LANES), BF16)],
        after=(dual,),
    )
    coeffs = swap_all(message).reshape(subs * half, LANES)

    tiles = PLANES + layers
    message, direction, applied, picks, factors = call(
        functools.partial(first_kernel, sizes, dims, layers, count),
        "first_direction",
        (meta,),
        (coeffs, residual, rows, dual, *received),
        [((fine_count, cases + tiles * half, LANES), BF16), full, half_full, (((count + 1) * terms * half, subs * half), BF16),
         ((count + 1, terms * HALF, LANES), BF16)],
        theirs,
    )
    own = lax.all_to_all(message, "fine", 0, 0, tiled=True)
    if layers == 1:
        others = [lax.ppermute(own, "coarse", [(0, 1), (1, 0)])]
    else:
        up = [(i, i + 1) for i in range(coarse_count - 1)]
        lower = lax.ppermute(applied[:, (PLANES + 1) * LANES :], "coarse", up)
        upper = lax.ppermute(applied[:, PLANES * LANES : (PLANES + 1) * LANES], "coarse", [(j, i) for i, j in up])
        others = [lax.all_gather(own, "coarse"), lower, upper]

    message, residual, multipliers, direction, applied = call(
        functools.partial(second_kernel, sizes, dims, layers, count),
        "second_direction",
        (meta,),
        (coeffs, residual, direction, applied, picks, factors, rows, dual, own, *others, *received),
        [((subs, cases + half, LANES), BF16), full, full, full, half_full],
        theirs + [pltpu.VMEM((subs, half, LANES), F32)],
    )
    arrived = swap_all(message)
    out = ((1, cases, width), F32)
    multipliers, residual = call(
        functools.partial(last_kernel, sizes),
        "finish",
        (meta,),
        (arrived, applied, residual, multipliers, direction),
        [out, out],
    )
    return multipliers, residual


def solution(mesh):
    rows = P(AXES, None, None)
    return jax.shard_map(
        body,
        mesh=mesh,
        in_specs=(rows, rows, rows, P(AXES, None, None, None), P(AXES, None), P(AXES, None), P(AXES, None)),
        out_specs=(rows, rows),
        check_vma=False,
    )
```

```python
import functools

import jax
import jax.numpy as jnp
from jax import lax
from jax.experimental import pallas as pl
from jax.experimental.pallas import tpu as pltpu
from jax.sharding import PartitionSpec as P

PLANES = 6
DISTANCES = (7, 11, 3, 5, 9, 1)
AXES = ("fine", "coarse")
LANES = 128
HALF = 64
BF16 = jnp.bfloat16
F32 = jnp.float32
SPARE = 32
GAMMA = 48
DELTA = 49


def lane_ids(rows):
    return lax.broadcasted_iota(jnp.int32, (rows, LANES), 1)


def dot(a, b):
    return lax.dot_general(a, b, (((1,), (0,)), ((), ())), preferred_element_type=F32)


def wanted_blocks(sizes, layers, meta_ref):
    slots = [slot_of(sizes, meta_ref[0, b]) for b in range(PLANES)]
    blocks = []
    for slot in range(PLANES):
        blocks.append(sum(jnp.where(slots[b] == slot, b, 0) for b in range(PLANES)))
    if layers == 1:
        return blocks + [jnp.where(lax.axis_index("coarse") == 0, PLANES + 1, PLANES)]
    return blocks + [PLANES, PLANES + 1]


def lanes_of(block):
    start = block * LANES
    return pl.ds(start if isinstance(start, int) else pl.multiple_of(start, LANES), LANES)


def facing_subs(sizes, partners_ref):
    fine_count, coarse_count = sizes
    fine = lax.axis_index("fine")
    coarse = lax.axis_index("coarse")
    me = fine * coarse_count + coarse
    subs = [partners_ref[0, b] * coarse_count + coarse for b in range(PLANES)]
    subs.append(jnp.where(coarse > 0, me - 1, me))
    subs.append(jnp.where(coarse < coarse_count - 1, me + 1, me))
    return subs


def slot_of(sizes, partner):
    fine_count = sizes[0]
    fine = lax.axis_index("fine")
    ahead = jnp.where(fine % 2 == 0, partner - fine, fine - partner)
    ahead = jnp.where(ahead < 0, ahead + fine_count, ahead)
    return sum(jnp.where(ahead == distance, slot, 0) for slot, distance in enumerate(DISTANCES))


def live_mask(counts_ref, block):
    return (lane_ids(1) < counts_ref[0, PLANES + block]).astype(F32)


def post_blocks(out_ref, targets, rows):
    cases = rows.shape[0]
    for block, target in enumerate(targets):
        out_ref[target, :cases, :] = rows[:, block * LANES : (block + 1) * LANES]


def fetch(pairs, sems):
    copies = [pltpu.make_async_copy(source, target, sems.at[i]) for i, (source, target) in enumerate(pairs)]
    for copy in copies:
        copy.start()
    return copies


def seat(part, rows, modes):
    gap = HALF - modes
    lane = lane_ids(rows) % HALF
    return (lane >= part * gap) & (lane < (part + 1) * gap), modes - part * gap


def board(hosts, guest, modes):
    seated = []
    for part, host in enumerate(hosts):
        mask, move = seat(part, guest.shape[0], modes)
        seated.append(host + pltpu.roll(jnp.where(mask, guest, 0.0), move, 1))
    return seated


def alight(hosts, modes):
    guest = jnp.zeros(hosts[0].shape, F32)
    for part, host in enumerate(hosts):
        mask, move = seat(part, guest.shape[0], modes)
        guest = jnp.where(mask, pltpu.roll(host, LANES - move, 1), guest)
    return guest


def pack_kernel(sizes, layers, partners_ref, counts_ref, pattern_ref, loads_ref, basis_ref, factors_hbm, *refs):
    rows_ref, outs = refs[0], refs[1:-7]
    partners_smem, counts_smem, pattern_smem, loads, basis, factors_ref, sems = refs[-7:]
    sources = (partners_ref, counts_ref, pattern_ref, loads_ref, basis_ref, factors_hbm)
    targets = (partners_smem, counts_smem, pattern_smem, loads, basis, factors_ref)
    for copy in fetch(list(zip(sources, targets)), sems):
        copy.wait()
    terms, modes = factors_ref.shape[1:3]
    cases = loads.shape[1]
    lane = lane_ids(8)
    row = lax.broadcasted_iota(jnp.int32, (8, LANES), 0)
    digits = jnp.zeros((8, LANES), F32)
    scalars = [partners_smem[0, b] for b in range(PLANES)]
    scalars += [counts_smem[0, b] for b in range(PLANES + 2)]
    for place, scalar in enumerate(scalars):
        digit = jnp.where(row == 0, scalar // 16, scalar % 16).astype(F32)
        digits = jnp.where(lane == place, digit, digits)
    rows_ref[:cases, :] = loads[0]
    rows_ref[cases : cases + modes, :] = basis[0]
    gap = jnp.zeros((modes, HALF - modes), F32)
    parts = []
    for term in range(terms):
        whole = factors_ref[0, term]
        high = whole.astype(BF16).astype(F32)
        parts.append(jnp.concatenate([high, gap, whole - high, gap], axis=1))
    factors = jnp.concatenate(board(parts[:-1], parts[-1], modes), axis=0).astype(BF16)
    ids = jnp.zeros((8, LANES), F32)
    for term in range(terms):
        sub = pattern_smem[0, term]
        ids = jnp.where(row == term, (sub // 16).astype(F32), ids)
        ids = jnp.where(row == terms + term, (sub % 16).astype(F32), ids)
    ids = ids.astype(BF16)
    places = layout_of(terms, modes)
    start = cases + modes
    depth = modes // 2
    rows_ref[start:, :] = jnp.zeros_like(rows_ref[start:, :])
    for group in range(2 * (terms - 1)):
        rows_ref[start : start + depth, group * LANES : (group + 1) * LANES] = factors[group * depth : (group + 1) * depth]
    rows_ref[start : start + 8, 6 * LANES : 7 * LANES] = ids
    rows_ref[start : start + 8, 7 * LANES :] = digits.astype(BF16)
    for out_ref, block in zip(outs, wanted_blocks(sizes, layers, partners_smem)):
        out_ref[places["factors"], :] = factors
        out_ref[places["ids"], :] = ids
        out_ref[places["loads"], :] = rows_ref[:cases, lanes_of(block)]
        out_ref[places["basis"], :] = rows_ref[cases:start, lanes_of(block)]


def layout_of(terms, modes):
    sizes = (("factors", (terms - 1) * modes), ("basis", modes), ("loads", 16), ("ids", 8))
    places, start = {}, 0
    for name, rows in sizes:
        places[name] = slice(start, start + rows)
        start += rows
    return places


def stage_kernel(start, dual_ref, rows_ref, dual_out, rows_out, meta_out, sems):
    copies = fetch([(dual_ref, dual_out), (rows_ref, rows_out)], sems)
    copies[1].wait()
    digits = rows_out[start : start + 8, 7 * LANES :].astype(F32)
    meta_out[...] = (digits[0:1] * 16.0 + digits[1:2]).astype(jnp.int32)
    copies[0].wait()


def basis_of(rows_ref, cases):
    return rows_ref[cases : rows_ref.shape[0] - SPARE, :]


def own_setup(dims, cases, rows_ref):
    terms, modes = dims
    start, depth = cases + modes, modes // 2
    groups = [
        rows_ref[start : start + depth, group * LANES : (group + 1) * LANES] for group in range(2 * (terms - 1))
    ]
    parts = [jnp.concatenate(groups[2 * term : 2 * term + 2], axis=0) for term in range(terms - 1)]
    return parts, rows_ref[start : start + 8, 6 * LANES : 7 * LANES]


def difference(counts_ref, mine, facing):
    result, ours, theirs = [], [], []
    for block, other in enumerate(facing):
        mask = live_mask(counts_ref, block)
        left = mine[:, block * LANES : (block + 1) * LANES].astype(F32) * mask
        right = other.astype(F32) * mask
        result.append(left - right)
        ours.append(left.astype(BF16))
        theirs.append(right.astype(BF16))
    return result, ours, theirs


def first_restrict_kernel(sizes, dims, layers, meta_ref, rows_ref, *refs):
    near_refs, (_, out_ref, message_ref, scratch_ref) = refs[: PLANES + layers], refs[PLANES + layers :]
    span = layout_of(*dims)["loads"]
    cases = out_ref.shape[0]
    for slot in range(PLANES):
        scratch_ref[slot] = near_refs[slot][span, :]
    facing = [scratch_ref[slot_of(sizes, meta_ref[0, b])] for b in range(PLANES)]
    facing += [near_refs[PLANES][span, :], near_refs[-1][span, :]]
    restrict(meta_ref, rows_ref[:cases, :], facing, basis_of(rows_ref, cases), out_ref, message_ref)


def twice(basis):
    gap = jnp.zeros((HALF - basis.shape[0], basis.shape[1]), BF16)
    return jnp.concatenate([basis, gap, basis, gap], axis=0)


def times_basis(rows, doubled):
    return lax.dot_general(rows, doubled, (((1,), (1,)), ((), ())), preferred_element_type=F32)


def fold(coefficients):
    half = coefficients.shape[0] // 2
    return jnp.where(lane_ids(half) < HALF, coefficients[:half], coefficients[half:])


def encode(sums):
    top = sums.astype(BF16).astype(F32)
    middle = (sums - top).astype(BF16).astype(F32)
    bottom = sums - top - middle
    return top + pltpu.roll(middle, 2, 1) + pltpu.roll(bottom, 4, 1)


def decode(totals):
    return totals + pltpu.roll(totals, LANES - 2, 1) + pltpu.roll(totals, LANES - 4, 1)


def restrict(meta_ref, mine, facing, basis, out_ref, message_ref):
    cases = mine.shape[0]
    result, ours, theirs = difference(meta_ref, mine, facing)
    for block, values in enumerate(result):
        out_ref[:, block * LANES : (block + 1) * LANES] = values
    both = jnp.concatenate([jnp.concatenate(ours, axis=1), jnp.concatenate(theirs, axis=1)], axis=0)
    coefficients = times_basis(both, twice(basis))
    message = fold(coefficients[:cases] - coefficients[cases:])
    message_ref[...] = jnp.broadcast_to(message[None], message_ref.shape)


def shares(sizes, dims, layers, meta_ref, applied_ref, near_refs, rows_ref, sums):
    cases = applied_ref.shape[0]
    span = layout_of(*dims)["basis"]
    masked = []
    for block in range(PLANES + 2):
        part = applied_ref[:, block * LANES : (block + 1) * LANES].astype(F32)
        masked.append((part * live_mask(meta_ref, block)).astype(BF16))
    own = fold(times_basis(jnp.concatenate(masked, axis=1), twice(basis_of(rows_ref, cases))))
    high = own.astype(BF16).astype(F32)
    tiles = []
    for near_ref, block in zip(near_refs, wanted_blocks(sizes, layers, meta_ref)):
        part = applied_ref[:, lanes_of(block)].astype(F32) * live_mask(meta_ref, block)
        tiles.append(fold(times_basis(part.astype(BF16), twice(near_ref[span, :]))))
    modes = dims[1]
    hosts = board(tiles[:3], own - high, modes) + board(tiles[3:PLANES], tiles[PLANES], modes)
    return jnp.concatenate([high + encode(sums)] + hosts + tiles[PLANES + 1 :], axis=0).astype(BF16)


def collect(sizes, dims, layers, cases, own_ref, others_ref, changes_ref):
    fine_count, coarse_count = sizes
    half = cases // 2
    coarse = lax.axis_index("coarse")

    def tile(layer, fine, index):
        rows = slice(cases + index * half, cases + (index + 1) * half)
        if layers == 1:
            source = own_ref if layer == 0 else others_ref
            return source[fine, rows, :].astype(F32)
        return others_ref[layer, fine, rows, :].astype(F32)

    def one(fine, totals):
        for layer in range(coarse_count):
            first = tile(layer, fine, 0)
            totals = totals + first
            value = first + alight([tile(layer, fine, 1 + slot) for slot in range(3)], dims[1])
            for slot in range(PLANES):
                distance = DISTANCES[slot]
                partner = jnp.where(fine % 2 == 0, fine + distance, fine - distance) if layers > 1 else (
                    fine + distance if fine % 2 == 0 else fine - distance
                )
                value = value - tile(layer, (partner + fine_count) % fine_count, 1 + slot)
            if layers == 1:
                value = value - alight([tile(1 - layer, fine, 4 + slot) for slot in range(3)], dims[1])
                place = fine * 2 + (coarse if layer == 0 else 1 - coarse)
            else:
                if layer > 0:
                    value = value - tile(layer - 1, fine, 1 + PLANES)
                if layer < coarse_count - 1:
                    value = value - alight([tile(layer + 1, fine, 4 + slot) for slot in range(3)], dims[1])
                place = fine * coarse_count + layer
            changes_ref[place] = value
        return totals

    totals = jnp.zeros((half, LANES), F32)
    if layers > 1:
        return decode(lax.fori_loop(0, fine_count, one, totals))
    for fine in range(fine_count):
        totals = one(fine, totals)
    return decode(totals)


def prepare(sizes, dims, cases, rows_ref, near_refs, picks_ref, factors_ref):
    terms, modes = dims
    places = layout_of(terms, modes)
    half = 8
    chunks = sizes[0] * sizes[1] * half // LANES
    lanes = lane_ids(half).astype(F32)
    step = lax.broadcasted_iota(jnp.int32, (half, LANES), 0).astype(F32)
    gap = jnp.zeros((HALF - modes, LANES), BF16)
    setups = [own_setup(dims, cases, rows_ref)]
    for near_ref in near_refs:
        parts = [near_ref[term * modes : (term + 1) * modes, :] for term in range(terms - 1)]
        setups.append((parts, near_ref[places["ids"], :]))
    for index, (packed, ids) in enumerate(setups):
        ids = ids.astype(F32)
        ids = (ids[:terms] * 16.0 + ids[terms : 2 * terms]) * float(half)
        picks = []
        for term in range(terms):
            target = ids[term : term + 1] + step
            picks.append(
                jnp.concatenate([(target == lanes + float(LANES * c)).astype(F32) for c in range(chunks)], axis=1)
            )
        rows = terms * half
        picks_ref[index * rows : (index + 1) * rows, :] = jnp.concatenate(picks, axis=0).astype(BF16)
        packed = packed + [alight([part.astype(F32) for part in packed], modes).astype(BF16)]
        for term, part in enumerate(packed):
            factors_ref[index, term * HALF : term * HALF + modes, :] = part
            factors_ref[index, term * HALF + modes : (term + 1) * HALF, :] = gap


def solve(coeffs, dims, picks_ref, factors_ref):
    terms, modes = dims
    half = 8
    high = coeffs.astype(BF16)
    low = (coeffs - high.astype(F32)).astype(BF16)
    picked = dot(picks_ref[...], jnp.concatenate([high, low], axis=1))
    left = lane_ids(half) < HALF
    solutions = []
    for index in range(factors_ref.shape[0]):
        sides = []
        for part in range(2):
            columns = []
            for pair in range(0, terms, 2):
                first, second = [
                    picked[(index * terms + term) * half : (index * terms + term + 1) * half, part * LANES : (part + 1) * LANES]
                    for term in (pair, pair + 1)
                ]
                top = jnp.where(left, first, pltpu.roll(second, HALF, 1))
                bottom = jnp.where(left, pltpu.roll(first, HALF, 1), second)
                columns.append(jnp.concatenate([top, bottom], axis=0))
            sides.append(jnp.concatenate(columns, axis=1))
        rows = jnp.concatenate(sides, axis=0).astype(BF16)
        product = dot(rows, factors_ref[index])
        product = product[: 2 * half] + product[2 * half :]
        product = product + pltpu.roll(product, HALF, 1)
        solutions.append(product[:, :modes].astype(BF16))
    return solutions


def advance(sizes, dims, meta_ref, coeffs, residual, near_refs, picks_ref, factors_ref, rows_ref, dual_ref, theirs_ref,
            direction_ref, applied_ref):
    span = layout_of(*dims)["basis"]
    solutions = solve(coeffs, dims, picks_ref, factors_ref)
    mine = dot(solutions[0], basis_of(rows_ref, residual.shape[0])).astype(BF16).astype(F32)
    for index, near_ref in enumerate(near_refs):
        theirs_ref[index] = dot(solutions[index + 1], near_ref[span, :]).astype(BF16).astype(F32)
    pieces = []
    for block in range(PLANES + 2):
        if block < PLANES:
            place = slot_of(sizes, meta_ref[0, block])
        else:
            place = min(block, len(near_refs) - 1)
        here = slice(block * LANES, (block + 1) * LANES)
        pieces.append(residual[:, here] + live_mask(meta_ref, block) * (mine[:, here] - theirs_ref[place]))
    direction = jnp.concatenate(pieces, axis=1)
    direction_ref[...] = direction
    applied = dot(direction.astype(BF16), dual_ref[0]).astype(BF16)
    applied_ref[...] = applied
    gamma = jnp.sum(residual * direction, axis=1, keepdims=True)
    delta = 2.0 * jnp.sum(direction * applied.astype(F32), axis=1, keepdims=True)
    half = gamma.shape[0] // 2
    lanes = lane_ids(half)
    sums = jnp.zeros((half, LANES), F32)
    for lane, values in ((GAMMA, gamma), (DELTA, delta)):
        sums = jnp.where(lanes == lane, values[:half], sums)
        sums = jnp.where(lanes == HALF + lane, values[half:], sums)
    return applied, sums


def first_kernel(sizes, dims, layers, count, meta_ref, coeffs_ref, residual_ref, rows_ref, dual_ref, *refs):
    near_refs = refs[:count]
    message_ref, direction_ref, applied_ref, picks_ref, factors_ref, theirs_ref = refs[count:]
    prepare(sizes, dims, residual_ref.shape[0], rows_ref, near_refs, picks_ref, factors_ref)
    applied, sums = advance(
        sizes, dims, meta_ref, coeffs_ref[...], residual_ref[...], near_refs, picks_ref, factors_ref, rows_ref, dual_ref,
        theirs_ref, direction_ref, applied_ref,
    )
    cases = applied.shape[0]
    tiles = shares(sizes, dims, layers, meta_ref, applied_ref, near_refs, rows_ref, sums)
    message_ref[:, :cases, :] = jnp.zeros((message_ref.shape[0], cases, LANES), BF16)
    message_ref[:, cases:, :] = jnp.broadcast_to(tiles[None], (message_ref.shape[0],) + tiles.shape)
    post_blocks(message_ref, [meta_ref[0, b] for b in range(PLANES)], applied)
    if layers == 1:
        block = wanted_blocks(sizes, layers, meta_ref)[-1]
        message_ref[lax.axis_index("fine"), :cases, :] = applied_ref[:, lanes_of(block)]


def steps_from(totals):
    low = totals[:, GAMMA : GAMMA + 1] / totals[:, DELTA : DELTA + 1]
    high = totals[:, HALF + GAMMA : HALF + GAMMA + 1] / totals[:, HALF + DELTA : HALF + DELTA + 1]
    return low, high


def second_kernel(sizes, dims, layers, count, meta_ref, coeffs_ref, residual_ref, before_ref, applied_before_ref,
                  picks_ref, factors_ref, rows_ref, dual_ref, own_ref, *refs):
    others_refs, refs = refs[: 1 if layers == 1 else 3], refs[1 if layers == 1 else 3 :]
    near_refs = refs[:count]
    message_ref, residual_out, multipliers_out, direction_ref, applied_ref, theirs_ref, changes_ref = refs[count:]
    cases = residual_ref.shape[0]
    half = cases // 2
    low, high = steps_from(collect(sizes, dims, layers, cases, own_ref, others_refs[0], changes_ref))
    step = jnp.concatenate([low, high], axis=0)
    packed_step = jnp.where(lane_ids(half) < HALF, low, high)
    coeffs = coeffs_ref[...] - (changes_ref[...] * packed_step[None]).reshape(coeffs_ref.shape)
    facing = [own_ref[meta_ref[0, b], :cases, :] for b in range(PLANES)]
    if layers == 1:
        facing += [others_refs[0][lax.axis_index("fine"), :cases, :]] * 2
    else:
        facing += [ref[...] for ref in others_refs[1:]]
    image, _, _ = difference(meta_ref, applied_before_ref[...], facing)
    residual = residual_ref[...] - step * jnp.concatenate(image, axis=1)
    residual_out[...] = residual
    multipliers_out[...] = step * before_ref[...]
    applied, sums = advance(
        sizes, dims, meta_ref, coeffs, residual, near_refs, picks_ref, factors_ref, rows_ref, dual_ref, theirs_ref,
        direction_ref, applied_ref,
    )
    message_ref[:, :cases, :] = jnp.zeros((message_ref.shape[0], cases, LANES), BF16)
    message_ref[:, cases:, :] = jnp.broadcast_to(encode(sums).astype(BF16)[None], (message_ref.shape[0], half, LANES))
    post_blocks(message_ref, facing_subs(sizes, meta_ref), applied)


def last_kernel(sizes, meta_ref, arrived_ref, applied_ref, residual_ref, multipliers_ref, direction_ref,
                multipliers_out, residual_out):
    cases = applied_ref.shape[0]
    totals = jnp.sum(arrived_ref[:, cases:, :].astype(F32), axis=0)
    step = jnp.concatenate(steps_from(decode(totals)), axis=0)
    facing = [arrived_ref[target, :cases, :] for target in facing_subs(sizes, meta_ref)]
    image, _, _ = difference(meta_ref, applied_ref[...], facing)
    fine = lax.axis_index("fine")
    for block in range(PLANES + 2):
        span = slice(block * LANES, (block + 1) * LANES)
        if block < PLANES:
            sign = jnp.where(fine < meta_ref[0, block], 1.0, -1.0).astype(F32)
        else:
            sign = -1.0 if block == PLANES else 1.0
        multipliers_out[0, :, span] = sign * (multipliers_ref[:, span] + step * direction_ref[:, span])
        residual_out[0, :, span] = sign * (residual_ref[:, span] - step * image[block])


SMEM = pl.BlockSpec(memory_space=pltpu.SMEM)
VMEM = pl.BlockSpec(memory_space=pltpu.VMEM)


HBM = pl.BlockSpec(memory_space=pltpu.HBM)
ANY = pl.BlockSpec(memory_space=pl.ANY)


def call(kernel, name, scalars, arrays, outs, scratch=(), far=(), after=(), vmem=40):
    return pl.pallas_call(
        kernel,
        name=name,
        out_shape=[jax.ShapeDtypeStruct(shape, dtype) for shape, dtype in outs],
        in_specs=[SMEM] * len(scalars) + [VMEM] * len(arrays) + [HBM] * len(far) + [ANY] * len(after),
        out_specs=[VMEM] * len(outs),
        scratch_shapes=list(scratch),
        compiler_params=pltpu.CompilerParams(vmem_limit_bytes=vmem * 1024 * 1024),
    )(*scalars, *arrays, *far, *after)


def body(load_cases, dual_ops, coarse_basis, factor_blocks, pattern, partners, row_counts):
    cases, width = load_cases.shape[1:]
    terms, modes = factor_blocks.shape[1:3]
    fine_count = lax.axis_size("fine")
    coarse_count = lax.axis_size("coarse")
    subs = fine_count * coarse_count
    sizes = (fine_count, coarse_count)
    dims = (terms, modes)
    half = cases // 2
    layers = 1 if coarse_count == 2 else 2

    def swap_all(message):
        return lax.all_to_all(message, AXES, 0, 0, tiled=True)

    def swap_slot(message, slot):
        distance = DISTANCES[slot]
        pairs = [(i, (i + distance if i % 2 == 0 else i - distance) % fine_count) for i in range(fine_count)]
        return lax.ppermute(message, "fine", pairs)

    def swap_blocks(messages):
        received = [swap_slot(messages[slot], slot) for slot in range(PLANES)]
        if layers == 1:
            return received + [lax.ppermute(messages[PLANES], "coarse", [(0, 1), (1, 0)])]
        up = [(i, i + 1) for i in range(coarse_count - 1)]
        lower = lax.ppermute(messages[PLANES + 1], "coarse", up)
        return received + [lower, lax.ppermute(messages[PLANES], "coarse", [(j, i) for i, j in up])]

    full = ((cases, width), F32)
    half_full = ((cases, width), BF16)
    coded = ((subs, half, LANES), F32)
    dma = pltpu.SemaphoreType.DMA

    inputs = (partners, row_counts, pattern, load_cases, coarse_basis, factor_blocks)
    spaces = (pltpu.SMEM,) * 3 + (pltpu.VMEM,) * 3
    rows, *packed = call(
        functools.partial(pack_kernel, sizes, layers),
        "pack_setup",
        (),
        (),
        [((cases + modes + SPARE, width), BF16)]
        + [((layout_of(terms, modes)["ids"].stop, LANES), BF16)] * (PLANES + layers),
        [space(array.shape, array.dtype) for space, array in zip(spaces, inputs)] + [dma((6,))],
        inputs,
        vmem=60,
    )
    received = swap_blocks(packed)
    dual, rows, meta = call(
        functools.partial(stage_kernel, cases + modes),
        "stage_operands",
        (),
        (),
        [(dual_ops.shape, BF16), (rows.shape, BF16), ((1, LANES), jnp.int32)],
        [dma((2,))],
        (dual_ops, rows),
    )
    count = len(received)
    theirs = [pltpu.VMEM((count, cases, LANES), F32)]

    residual, message = call(
        functools.partial(first_restrict_kernel, sizes, dims, layers),
        "restrict_residual",
        (meta,),
        (rows, *received),
        [full, coded],
        [pltpu.VMEM((PLANES, cases, LANES), BF16)],
        after=(dual,),
    )
    coeffs = swap_all(message).reshape(subs * half, LANES)

    tiles = PLANES + layers
    message, direction, applied, picks, factors = call(
        functools.partial(first_kernel, sizes, dims, layers, count),
        "first_direction",
        (meta,),
        (coeffs, residual, rows, dual, *received),
        [((fine_count, cases + tiles * half, LANES), BF16), full, half_full, (((count + 1) * terms * half, subs * half), BF16),
         ((count + 1, terms * HALF, LANES), BF16)],
        theirs,
    )
    own = lax.all_to_all(message, "fine", 0, 0, tiled=True)
    if layers == 1:
        others = [lax.ppermute(own, "coarse", [(0, 1), (1, 0)])]
    else:
        up = [(i, i + 1) for i in range(coarse_count - 1)]
        lower = lax.ppermute(applied[:, (PLANES + 1) * LANES :], "coarse", up)
        upper = lax.ppermute(applied[:, PLANES * LANES : (PLANES + 1) * LANES], "coarse", [(j, i) for i, j in up])
        others = [lax.all_gather(own, "coarse"), lower, upper]

    message, residual, multipliers, direction, applied = call(
        functools.partial(second_kernel, sizes, dims, layers, count),
        "second_direction",
        (meta,),
        (coeffs, residual, direction, applied, picks, factors, rows, dual, own, *others, *received),
        [((subs, cases + half, LANES), BF16), full, full, full, half_full],
        theirs + [pltpu.VMEM((subs, half, LANES), F32)],
    )
    arrived = swap_all(message)
    out = ((1, cases, width), F32)
    multipliers, residual = call(
        functools.partial(last_kernel, sizes),
        "finish",
        (meta,),
        (arrived, applied, residual, multipliers, direction),
        [out, out],
    )
    return multipliers, residual


def solution(mesh):
    rows = P(AXES, None, None)
    return jax.shard_map(
        body,
        mesh=mesh,
        in_specs=(rows, rows, rows, P(AXES, None, None, None), P(AXES, None), P(AXES, None), P(AXES, None)),
        out_specs=(rows, rows),
        check_vma=False,
    )
```

```python
import functools

import jax
import jax.numpy as jnp
from jax import lax
from jax.experimental import pallas as pl
from jax.experimental.pallas import tpu as pltpu
from jax.sharding import PartitionSpec as P

PLANES = 6
DISTANCES = (11, 7, 3, 9, 5, 1)
AXES = ("fine", "coarse")
LANES = 128
HALF = 64
BF16 = jnp.bfloat16
F32 = jnp.float32
SPARE = 32
GAMMA = 48
DELTA = 49


def lane_ids(rows):
    return lax.broadcasted_iota(jnp.int32, (rows, LANES), 1)


def dot(a, b):
    return lax.dot_general(a, b, (((1,), (0,)), ((), ())), preferred_element_type=F32)


def wanted_blocks(sizes, layers, meta_ref):
    slots = [slot_of(sizes, meta_ref[0, b]) for b in range(PLANES)]
    blocks = []
    for slot in range(PLANES):
        blocks.append(sum(jnp.where(slots[b] == slot, b, 0) for b in range(PLANES)))
    if layers == 1:
        return blocks + [jnp.where(lax.axis_index("coarse") == 0, PLANES + 1, PLANES)]
    return blocks + [PLANES, PLANES + 1]


def lanes_of(block):
    start = block * LANES
    return pl.ds(start if isinstance(start, int) else pl.multiple_of(start, LANES), LANES)


def facing_subs(sizes, partners_ref):
    fine_count, coarse_count = sizes
    fine = lax.axis_index("fine")
    coarse = lax.axis_index("coarse")
    me = fine * coarse_count + coarse
    subs = [partners_ref[0, b] * coarse_count + coarse for b in range(PLANES)]
    subs.append(jnp.where(coarse > 0, me - 1, me))
    subs.append(jnp.where(coarse < coarse_count - 1, me + 1, me))
    return subs


def slot_of(sizes, partner):
    fine_count = sizes[0]
    fine = lax.axis_index("fine")
    ahead = jnp.where(fine % 2 == 0, partner - fine, fine - partner)
    ahead = jnp.where(ahead < 0, ahead + fine_count, ahead)
    return sum(jnp.where(ahead == distance, slot, 0) for slot, distance in enumerate(DISTANCES))


def live_mask(counts_ref, block):
    return (lane_ids(1) < counts_ref[0, PLANES + block]).astype(F32)


def post_blocks(out_ref, targets, rows):
    cases = rows.shape[0]
    for block, target in enumerate(targets):
        out_ref[target, :cases, :] = rows[:, block * LANES : (block + 1) * LANES]


def fetch(pairs, sems):
    copies = [pltpu.make_async_copy(source, target, sems.at[i]) for i, (source, target) in enumerate(pairs)]
    for copy in copies:
        copy.start()
    return copies


def seat(part, rows, modes):
    gap = HALF - modes
    lane = lane_ids(rows) % HALF
    return (lane >= part * gap) & (lane < (part + 1) * gap), modes - part * gap


def board(hosts, guest, modes):
    seated = []
    for part, host in enumerate(hosts):
        mask, move = seat(part, guest.shape[0], modes)
        seated.append(host + pltpu.roll(jnp.where(mask, guest, 0.0), move, 1))
    return seated


def alight(hosts, modes):
    guest = jnp.zeros(hosts[0].shape, F32)
    for part, host in enumerate(hosts):
        mask, move = seat(part, guest.shape[0], modes)
        guest = jnp.where(mask, pltpu.roll(host, LANES - move, 1), guest)
    return guest


def pack_kernel(sizes, layers, partners_ref, counts_ref, pattern_ref, loads_ref, basis_ref, factors_hbm, *refs):
    rows_ref, outs = refs[0], refs[1:-7]
    partners_smem, counts_smem, pattern_smem, loads, basis, factors_ref, sems = refs[-7:]
    sources = (partners_ref, counts_ref, pattern_ref, loads_ref, basis_ref, factors_hbm)
    targets = (partners_smem, counts_smem, pattern_smem, loads, basis, factors_ref)
    for copy in fetch(list(zip(sources, targets)), sems):
        copy.wait()
    terms, modes = factors_ref.shape[1:3]
    cases = loads.shape[1]
    lane = lane_ids(8)
    row = lax.broadcasted_iota(jnp.int32, (8, LANES), 0)
    digits = jnp.zeros((8, LANES), F32)
    scalars = [partners_smem[0, b] for b in range(PLANES)]
    scalars += [counts_smem[0, b] for b in range(PLANES + 2)]
    for place, scalar in enumerate(scalars):
        digit = jnp.where(row == 0, scalar // 16, scalar % 16).astype(F32)
        digits = jnp.where(lane == place, digit, digits)
    rows_ref[:cases, :] = loads[0]
    rows_ref[cases : cases + modes, :] = basis[0]
    gap = jnp.zeros((modes, HALF - modes), F32)
    parts = []
    for term in range(terms):
        whole = factors_ref[0, term]
        high = whole.astype(BF16).astype(F32)
        parts.append(jnp.concatenate([high, gap, whole - high, gap], axis=1))
    factors = jnp.concatenate(board(parts[:-1], parts[-1], modes), axis=0).astype(BF16)
    ids = jnp.zeros((8, LANES), F32)
    for term in range(terms):
        sub = pattern_smem[0, term]
        ids = jnp.where(row == term, (sub // 16).astype(F32), ids)
        ids = jnp.where(row == terms + term, (sub % 16).astype(F32), ids)
    ids = ids.astype(BF16)
    places = layout_of(terms, modes)
    start = cases + modes
    depth = modes // 2
    rows_ref[start:, :] = jnp.zeros_like(rows_ref[start:, :])
    for group in range(2 * (terms - 1)):
        rows_ref[start : start + depth, group * LANES : (group + 1) * LANES] = factors[group * depth : (group + 1) * depth]
    rows_ref[start : start + 8, 6 * LANES : 7 * LANES] = ids
    rows_ref[start : start + 8, 7 * LANES :] = digits.astype(BF16)
    for out_ref, block in zip(outs, wanted_blocks(sizes, layers, partners_smem)):
        out_ref[places["factors"], :] = factors
        out_ref[places["ids"], :] = ids
        out_ref[places["loads"], :] = rows_ref[:cases, lanes_of(block)]
        out_ref[places["basis"], :] = rows_ref[cases:start, lanes_of(block)]


def layout_of(terms, modes):
    sizes = (("factors", (terms - 1) * modes), ("basis", modes), ("loads", 16), ("ids", 8))
    places, start = {}, 0
    for name, rows in sizes:
        places[name] = slice(start, start + rows)
        start += rows
    return places


def stage_kernel(start, dual_ref, rows_ref, dual_out, rows_out, meta_out, sems):
    copies = fetch([(dual_ref, dual_out), (rows_ref, rows_out)], sems)
    copies[1].wait()
    digits = rows_out[start : start + 8, 7 * LANES :].astype(F32)
    meta_out[...] = (digits[0:1] * 16.0 + digits[1:2]).astype(jnp.int32)
    copies[0].wait()


def basis_of(rows_ref, cases):
    return rows_ref[cases : rows_ref.shape[0] - SPARE, :]


def own_setup(dims, cases, rows_ref):
    terms, modes = dims
    start, depth = cases + modes, modes // 2
    groups = [
        rows_ref[start : start + depth, group * LANES : (group + 1) * LANES] for group in range(2 * (terms - 1))
    ]
    parts = [jnp.concatenate(groups[2 * term : 2 * term + 2], axis=0) for term in range(terms - 1)]
    return parts, rows_ref[start : start + 8, 6 * LANES : 7 * LANES]


def difference(counts_ref, mine, facing):
    result, ours, theirs = [], [], []
    for block, other in enumerate(facing):
        mask = live_mask(counts_ref, block)
        left = mine[:, block * LANES : (block + 1) * LANES].astype(F32) * mask
        right = other.astype(F32) * mask
        result.append(left - right)
        ours.append(left.astype(BF16))
        theirs.append(right.astype(BF16))
    return result, ours, theirs


def first_restrict_kernel(sizes, dims, layers, meta_ref, rows_ref, *refs):
    near_refs, (_, out_ref, message_ref, scratch_ref) = refs[: PLANES + layers], refs[PLANES + layers :]
    span = layout_of(*dims)["loads"]
    cases = out_ref.shape[0]
    for slot in range(PLANES):
        scratch_ref[slot] = near_refs[slot][span, :]
    facing = [scratch_ref[slot_of(sizes, meta_ref[0, b])] for b in range(PLANES)]
    facing += [near_refs[PLANES][span, :], near_refs[-1][span, :]]
    restrict(meta_ref, rows_ref[:cases, :], facing, basis_of(rows_ref, cases), out_ref, message_ref)


def twice(basis):
    gap = jnp.zeros((HALF - basis.shape[0], basis.shape[1]), BF16)
    return jnp.concatenate([basis, gap, basis, gap], axis=0)


def times_basis(rows, doubled):
    return lax.dot_general(rows, doubled, (((1,), (1,)), ((), ())), preferred_element_type=F32)


def fold(coefficients):
    half = coefficients.shape[0] // 2
    return jnp.where(lane_ids(half) < HALF, coefficients[:half], coefficients[half:])


def encode(sums):
    top = sums.astype(BF16).astype(F32)
    middle = (sums - top).astype(BF16).astype(F32)
    bottom = sums - top - middle
    return top + pltpu.roll(middle, 2, 1) + pltpu.roll(bottom, 4, 1)


def decode(totals):
    return totals + pltpu.roll(totals, LANES - 2, 1) + pltpu.roll(totals, LANES - 4, 1)


def restrict(meta_ref, mine, facing, basis, out_ref, message_ref):
    cases = mine.shape[0]
    result, ours, theirs = difference(meta_ref, mine, facing)
    for block, values in enumerate(result):
        out_ref[:, block * LANES : (block + 1) * LANES] = values
    both = jnp.concatenate([jnp.concatenate(ours, axis=1), jnp.concatenate(theirs, axis=1)], axis=0)
    coefficients = times_basis(both, twice(basis))
    message = fold(coefficients[:cases] - coefficients[cases:])
    message_ref[...] = jnp.broadcast_to(message[None], message_ref.shape)


def shares(sizes, dims, layers, meta_ref, applied_ref, near_refs, rows_ref, sums):
    cases = applied_ref.shape[0]
    span = layout_of(*dims)["basis"]
    masked = []
    for block in range(PLANES + 2):
        part = applied_ref[:, block * LANES : (block + 1) * LANES].astype(F32)
        masked.append((part * live_mask(meta_ref, block)).astype(BF16))
    own = fold(times_basis(jnp.concatenate(masked, axis=1), twice(basis_of(rows_ref, cases))))
    high = own.astype(BF16).astype(F32)
    tiles = []
    for near_ref, block in zip(near_refs, wanted_blocks(sizes, layers, meta_ref)):
        part = applied_ref[:, lanes_of(block)].astype(F32) * live_mask(meta_ref, block)
        tiles.append(fold(times_basis(part.astype(BF16), twice(near_ref[span, :]))))
    modes = dims[1]
    hosts = board(tiles[:3], own - high, modes) + board(tiles[3:PLANES], tiles[PLANES], modes)
    return jnp.concatenate([high + encode(sums)] + hosts + tiles[PLANES + 1 :], axis=0).astype(BF16)


def collect(sizes, dims, layers, cases, own_ref, others_ref, changes_ref):
    fine_count, coarse_count = sizes
    half = cases // 2
    coarse = lax.axis_index("coarse")

    def tile(layer, fine, index):
        rows = slice(cases + index * half, cases + (index + 1) * half)
        if layers == 1:
            source = own_ref if layer == 0 else others_ref
            return source[fine, rows, :].astype(F32)
        return others_ref[layer, fine, rows, :].astype(F32)

    def one(fine, totals):
        for layer in range(coarse_count):
            first = tile(layer, fine, 0)
            totals = totals + first
            value = first + alight([tile(layer, fine, 1 + slot) for slot in range(3)], dims[1])
            for slot in range(PLANES):
                distance = DISTANCES[slot]
                partner = jnp.where(fine % 2 == 0, fine + distance, fine - distance) if layers > 1 else (
                    fine + distance if fine % 2 == 0 else fine - distance
                )
                value = value - tile(layer, (partner + fine_count) % fine_count, 1 + slot)
            if layers == 1:
                value = value - alight([tile(1 - layer, fine, 4 + slot) for slot in range(3)], dims[1])
                place = fine * 2 + (coarse if layer == 0 else 1 - coarse)
            else:
                if layer > 0:
                    value = value - tile(layer - 1, fine, 1 + PLANES)
                if layer < coarse_count - 1:
                    value = value - alight([tile(layer + 1, fine, 4 + slot) for slot in range(3)], dims[1])
                place = fine * coarse_count + layer
            changes_ref[place] = value
        return totals

    totals = jnp.zeros((half, LANES), F32)
    if layers > 1:
        return decode(lax.fori_loop(0, fine_count, one, totals))
    for fine in range(fine_count):
        totals = one(fine, totals)
    return decode(totals)


def prepare(sizes, dims, cases, rows_ref, near_refs, picks_ref, factors_ref):
    terms, modes = dims
    places = layout_of(terms, modes)
    half = 8
    chunks = sizes[0] * sizes[1] * half // LANES
    lanes = lane_ids(half).astype(F32)
    step = lax.broadcasted_iota(jnp.int32, (half, LANES), 0).astype(F32)
    gap = jnp.zeros((HALF - modes, LANES), BF16)
    setups = [own_setup(dims, cases, rows_ref)]
    for near_ref in near_refs:
        parts = [near_ref[term * modes : (term + 1) * modes, :] for term in range(terms - 1)]
        setups.append((parts, near_ref[places["ids"], :]))
    for index, (packed, ids) in enumerate(setups):
        ids = ids.astype(F32)
        ids = (ids[:terms] * 16.0 + ids[terms : 2 * terms]) * float(half)
        picks = []
        for term in range(terms):
            target = ids[term : term + 1] + step
            picks.append(
                jnp.concatenate([(target == lanes + float(LANES * c)).astype(F32) for c in range(chunks)], axis=1)
            )
        rows = terms * half
        picks_ref[index * rows : (index + 1) * rows, :] = jnp.concatenate(picks, axis=0).astype(BF16)
        packed = packed + [alight([part.astype(F32) for part in packed], modes).astype(BF16)]
        for term, part in enumerate(packed):
            factors_ref[index, term * HALF : term * HALF + modes, :] = part
            factors_ref[index, term * HALF + modes : (term + 1) * HALF, :] = gap


def solve(coeffs, dims, picks_ref, factors_ref):
    terms, modes = dims
    half = 8
    high = coeffs.astype(BF16)
    low = (coeffs - high.astype(F32)).astype(BF16)
    picked = dot(picks_ref[...], jnp.concatenate([high, low], axis=1))
    left = lane_ids(half) < HALF
    solutions = []
    for index in range(factors_ref.shape[0]):
        sides = []
        for part in range(2):
            columns = []
            for pair in range(0, terms, 2):
                first, second = [
                    picked[(index * terms + term) * half : (index * terms + term + 1) * half, part * LANES : (part + 1) * LANES]
                    for term in (pair, pair + 1)
                ]
                top = jnp.where(left, first, pltpu.roll(second, HALF, 1))
                bottom = jnp.where(left, pltpu.roll(first, HALF, 1), second)
                columns.append(jnp.concatenate([top, bottom], axis=0))
            sides.append(jnp.concatenate(columns, axis=1))
        rows = jnp.concatenate(sides, axis=0).astype(BF16)
        product = dot(rows, factors_ref[index])
        product = product[: 2 * half] + product[2 * half :]
        product = product + pltpu.roll(product, HALF, 1)
        solutions.append(product[:, :modes].astype(BF16))
    return solutions


def advance(sizes, dims, meta_ref, coeffs, residual, near_refs, picks_ref, factors_ref, rows_ref, dual_ref, theirs_ref,
            direction_ref, applied_ref):
    span = layout_of(*dims)["basis"]
    solutions = solve(coeffs, dims, picks_ref, factors_ref)
    mine = dot(solutions[0], basis_of(rows_ref, residual.shape[0])).astype(BF16).astype(F32)
    for index, near_ref in enumerate(near_refs):
        theirs_ref[index] = dot(solutions[index + 1], near_ref[span, :]).astype(BF16).astype(F32)
    pieces = []
    for block in range(PLANES + 2):
        if block < PLANES:
            place = slot_of(sizes, meta_ref[0, block])
        else:
            place = min(block, len(near_refs) - 1)
        here = slice(block * LANES, (block + 1) * LANES)
        pieces.append(residual[:, here] + live_mask(meta_ref, block) * (mine[:, here] - theirs_ref[place]))
    direction = jnp.concatenate(pieces, axis=1)
    direction_ref[...] = direction
    applied = dot(direction.astype(BF16), dual_ref[0]).astype(BF16)
    applied_ref[...] = applied
    gamma = jnp.sum(residual * direction, axis=1, keepdims=True)
    delta = 2.0 * jnp.sum(direction * applied.astype(F32), axis=1, keepdims=True)
    half = gamma.shape[0] // 2
    lanes = lane_ids(half)
    sums = jnp.zeros((half, LANES), F32)
    for lane, values in ((GAMMA, gamma), (DELTA, delta)):
        sums = jnp.where(lanes == lane, values[:half], sums)
        sums = jnp.where(lanes == HALF + lane, values[half:], sums)
    return applied, sums


def first_kernel(sizes, dims, layers, count, meta_ref, coeffs_ref, residual_ref, rows_ref, dual_ref, *refs):
    near_refs = refs[:count]
    message_ref, direction_ref, applied_ref, picks_ref, factors_ref, theirs_ref = refs[count:]
    prepare(sizes, dims, residual_ref.shape[0], rows_ref, near_refs, picks_ref, factors_ref)
    applied, sums = advance(
        sizes, dims, meta_ref, coeffs_ref[...], residual_ref[...], near_refs, picks_ref, factors_ref, rows_ref, dual_ref,
        theirs_ref, direction_ref, applied_ref,
    )
    cases = applied.shape[0]
    tiles = shares(sizes, dims, layers, meta_ref, applied_ref, near_refs, rows_ref, sums)
    message_ref[:, :cases, :] = jnp.zeros((message_ref.shape[0], cases, LANES), BF16)
    message_ref[:, cases:, :] = jnp.broadcast_to(tiles[None], (message_ref.shape[0],) + tiles.shape)
    post_blocks(message_ref, [meta_ref[0, b] for b in range(PLANES)], applied)
    if layers == 1:
        block = wanted_blocks(sizes, layers, meta_ref)[-1]
        message_ref[lax.axis_index("fine"), :cases, :] = applied_ref[:, lanes_of(block)]


def steps_from(totals):
    low = totals[:, GAMMA : GAMMA + 1] / totals[:, DELTA : DELTA + 1]
    high = totals[:, HALF + GAMMA : HALF + GAMMA + 1] / totals[:, HALF + DELTA : HALF + DELTA + 1]
    return low, high


def second_kernel(sizes, dims, layers, count, meta_ref, coeffs_ref, residual_ref, before_ref, applied_before_ref,
                  picks_ref, factors_ref, rows_ref, dual_ref, own_ref, *refs):
    others_refs, refs = refs[: 1 if layers == 1 else 3], refs[1 if layers == 1 else 3 :]
    near_refs = refs[:count]
    message_ref, residual_out, multipliers_out, direction_ref, applied_ref, theirs_ref, changes_ref = refs[count:]
    cases = residual_ref.shape[0]
    half = cases // 2
    low, high = steps_from(collect(sizes, dims, layers, cases, own_ref, others_refs[0], changes_ref))
    step = jnp.concatenate([low, high], axis=0)
    packed_step = jnp.where(lane_ids(half) < HALF, low, high)
    coeffs = coeffs_ref[...] - (changes_ref[...] * packed_step[None]).reshape(coeffs_ref.shape)
    facing = [own_ref[meta_ref[0, b], :cases, :] for b in range(PLANES)]
    if layers == 1:
        facing += [others_refs[0][lax.axis_index("fine"), :cases, :]] * 2
    else:
        facing += [ref[...] for ref in others_refs[1:]]
    image, _, _ = difference(meta_ref, applied_before_ref[...], facing)
    residual = residual_ref[...] - step * jnp.concatenate(image, axis=1)
    residual_out[...] = residual
    multipliers_out[...] = step * before_ref[...]
    applied, sums = advance(
        sizes, dims, meta_ref, coeffs, residual, near_refs, picks_ref, factors_ref, rows_ref, dual_ref, theirs_ref,
        direction_ref, applied_ref,
    )
    message_ref[:, :cases, :] = jnp.zeros((message_ref.shape[0], cases, LANES), BF16)
    message_ref[:, cases:, :] = jnp.broadcast_to(encode(sums).astype(BF16)[None], (message_ref.shape[0], half, LANES))
    post_blocks(message_ref, facing_subs(sizes, meta_ref), applied)


def last_kernel(sizes, meta_ref, arrived_ref, applied_ref, residual_ref, multipliers_ref, direction_ref,
                multipliers_out, residual_out):
    cases = applied_ref.shape[0]
    totals = jnp.sum(arrived_ref[:, cases:, :].astype(F32), axis=0)
    step = jnp.concatenate(steps_from(decode(totals)), axis=0)
    facing = [arrived_ref[target, :cases, :] for target in facing_subs(sizes, meta_ref)]
    image, _, _ = difference(meta_ref, applied_ref[...], facing)
    fine = lax.axis_index("fine")
    for block in range(PLANES + 2):
        span = slice(block * LANES, (block + 1) * LANES)
        if block < PLANES:
            sign = jnp.where(fine < meta_ref[0, block], 1.0, -1.0).astype(F32)
        else:
            sign = -1.0 if block == PLANES else 1.0
        multipliers_out[0, :, span] = sign * (multipliers_ref[:, span] + step * direction_ref[:, span])
        residual_out[0, :, span] = sign * (residual_ref[:, span] - step * image[block])


SMEM = pl.BlockSpec(memory_space=pltpu.SMEM)
VMEM = pl.BlockSpec(memory_space=pltpu.VMEM)


HBM = pl.BlockSpec(memory_space=pltpu.HBM)
ANY = pl.BlockSpec(memory_space=pl.ANY)


def call(kernel, name, scalars, arrays, outs, scratch=(), far=(), after=(), vmem=40):
    return pl.pallas_call(
        kernel,
        name=name,
        out_shape=[jax.ShapeDtypeStruct(shape, dtype) for shape, dtype in outs],
        in_specs=[SMEM] * len(scalars) + [VMEM] * len(arrays) + [HBM] * len(far) + [ANY] * len(after),
        out_specs=[VMEM] * len(outs),
        scratch_shapes=list(scratch),
        compiler_params=pltpu.CompilerParams(vmem_limit_bytes=vmem * 1024 * 1024),
    )(*scalars, *arrays, *far, *after)


def body(load_cases, dual_ops, coarse_basis, factor_blocks, pattern, partners, row_counts):
    cases, width = load_cases.shape[1:]
    terms, modes = factor_blocks.shape[1:3]
    fine_count = lax.axis_size("fine")
    coarse_count = lax.axis_size("coarse")
    subs = fine_count * coarse_count
    sizes = (fine_count, coarse_count)
    dims = (terms, modes)
    half = cases // 2
    layers = 1 if coarse_count == 2 else 2

    def swap_all(message):
        return lax.all_to_all(message, AXES, 0, 0, tiled=True)

    def swap_slot(message, slot):
        distance = DISTANCES[slot]
        pairs = [(i, (i + distance if i % 2 == 0 else i - distance) % fine_count) for i in range(fine_count)]
        return lax.ppermute(message, "fine", pairs)

    def swap_blocks(messages):
        received = [swap_slot(messages[slot], slot) for slot in range(PLANES)]
        if layers == 1:
            return received + [lax.ppermute(messages[PLANES], "coarse", [(0, 1), (1, 0)])]
        up = [(i, i + 1) for i in range(coarse_count - 1)]
        lower = lax.ppermute(messages[PLANES + 1], "coarse", up)
        return received + [lower, lax.ppermute(messages[PLANES], "coarse", [(j, i) for i, j in up])]

    full = ((cases, width), F32)
    half_full = ((cases, width), BF16)
    coded = ((subs, half, LANES), F32)
    dma = pltpu.SemaphoreType.DMA

    inputs = (partners, row_counts, pattern, load_cases, coarse_basis, factor_blocks)
    spaces = (pltpu.SMEM,) * 3 + (pltpu.VMEM,) * 3
    rows, *packed = call(
        functools.partial(pack_kernel, sizes, layers),
        "pack_setup",
        (),
        (),
        [((cases + modes + SPARE, width), BF16)]
        + [((layout_of(terms, modes)["ids"].stop, LANES), BF16)] * (PLANES + layers),
        [space(array.shape, array.dtype) for space, array in zip(spaces, inputs)] + [dma((6,))],
        inputs,
        vmem=60,
    )
    received = swap_blocks(packed)
    dual, rows, meta = call(
        functools.partial(stage_kernel, cases + modes),
        "stage_operands",
        (),
        (),
        [(dual_ops.shape, BF16), (rows.shape, BF16), ((1, LANES), jnp.int32)],
        [dma((2,))],
        (dual_ops, rows),
    )
    count = len(received)
    theirs = [pltpu.VMEM((count, cases, LANES), F32)]

    residual, message = call(
        functools.partial(first_restrict_kernel, sizes, dims, layers),
        "restrict_residual",
        (meta,),
        (rows, *received),
        [full, coded],
        [pltpu.VMEM((PLANES, cases, LANES), BF16)],
        after=(dual,),
    )
    coeffs = swap_all(message).reshape(subs * half, LANES)

    tiles = PLANES + layers
    message, direction, applied, picks, factors = call(
        functools.partial(first_kernel, sizes, dims, layers, count),
        "first_direction",
        (meta,),
        (coeffs, residual, rows, dual, *received),
        [((fine_count, cases + tiles * half, LANES), BF16), full, half_full, (((count + 1) * terms * half, subs * half), BF16),
         ((count + 1, terms * HALF, LANES), BF16)],
        theirs,
    )
    own = lax.all_to_all(message, "fine", 0, 0, tiled=True)
    if layers == 1:
        others = [lax.ppermute(own, "coarse", [(0, 1), (1, 0)])]
    else:
        up = [(i, i + 1) for i in range(coarse_count - 1)]
        lower = lax.ppermute(applied[:, (PLANES + 1) * LANES :], "coarse", up)
        upper = lax.ppermute(applied[:, PLANES * LANES : (PLANES + 1) * LANES], "coarse", [(j, i) for i, j in up])
        others = [lax.all_gather(own, "coarse"), lower, upper]

    message, residual, multipliers, direction, applied = call(
        functools.partial(second_kernel, sizes, dims, layers, count),
        "second_direction",
        (meta,),
        (coeffs, residual, direction, applied, picks, factors, rows, dual, own, *others, *received),
        [((subs, cases + half, LANES), BF16), full, full, full, half_full],
        theirs + [pltpu.VMEM((subs, half, LANES), F32)],
    )
    arrived = swap_all(message)
    out = ((1, cases, width), F32)
    multipliers, residual = call(
        functools.partial(last_kernel, sizes),
        "finish",
        (meta,),
        (arrived, applied, residual, multipliers, direction),
        [out, out],
    )
    return multipliers, residual


def solution(mesh):
    rows = P(AXES, None, None)
    return jax.shard_map(
        body,
        mesh=mesh,
        in_specs=(rows, rows, rows, P(AXES, None, None, None), P(AXES, None), P(AXES, None), P(AXES, None)),
        out_specs=(rows, rows),
        check_vma=False,
    )
```

```python
import functools

import jax
import jax.numpy as jnp
from jax import lax
from jax.experimental import pallas as pl
from jax.experimental.pallas import tpu as pltpu
from jax.sharding import PartitionSpec as P

PLANES = 6
DISTANCES = (11, 5, 3, 7, 9, 1)
AXES = ("fine", "coarse")
LANES = 128
HALF = 64
BF16 = jnp.bfloat16
F32 = jnp.float32
SPARE = 32
GAMMA = 48
DELTA = 49


def lane_ids(rows):
    return lax.broadcasted_iota(jnp.int32, (rows, LANES), 1)


def dot(a, b):
    return lax.dot_general(a, b, (((1,), (0,)), ((), ())), preferred_element_type=F32)


def wanted_blocks(sizes, layers, meta_ref):
    slots = [slot_of(sizes, meta_ref[0, b]) for b in range(PLANES)]
    blocks = []
    for slot in range(PLANES):
        blocks.append(sum(jnp.where(slots[b] == slot, b, 0) for b in range(PLANES)))
    if layers == 1:
        return blocks + [jnp.where(lax.axis_index("coarse") == 0, PLANES + 1, PLANES)]
    return blocks + [PLANES, PLANES + 1]


def lanes_of(block):
    start = block * LANES
    return pl.ds(start if isinstance(start, int) else pl.multiple_of(start, LANES), LANES)


def facing_subs(sizes, partners_ref):
    fine_count, coarse_count = sizes
    fine = lax.axis_index("fine")
    coarse = lax.axis_index("coarse")
    me = fine * coarse_count + coarse
    subs = [partners_ref[0, b] * coarse_count + coarse for b in range(PLANES)]
    subs.append(jnp.where(coarse > 0, me - 1, me))
    subs.append(jnp.where(coarse < coarse_count - 1, me + 1, me))
    return subs


def slot_of(sizes, partner):
    fine_count = sizes[0]
    fine = lax.axis_index("fine")
    ahead = jnp.where(fine % 2 == 0, partner - fine, fine - partner)
    ahead = jnp.where(ahead < 0, ahead + fine_count, ahead)
    return sum(jnp.where(ahead == distance, slot, 0) for slot, distance in enumerate(DISTANCES))


def live_mask(counts_ref, block):
    return (lane_ids(1) < counts_ref[0, PLANES + block]).astype(F32)


def post_blocks(out_ref, targets, rows):
    cases = rows.shape[0]
    for block, target in enumerate(targets):
        out_ref[target, :cases, :] = rows[:, block * LANES : (block + 1) * LANES]


def fetch(pairs, sems):
    copies = [pltpu.make_async_copy(source, target, sems.at[i]) for i, (source, target) in enumerate(pairs)]
    for copy in copies:
        copy.start()
    return copies


def seat(part, rows, modes):
    gap = HALF - modes
    lane = lane_ids(rows) % HALF
    return (lane >= part * gap) & (lane < (part + 1) * gap), modes - part * gap


def board(hosts, guest, modes):
    seated = []
    for part, host in enumerate(hosts):
        mask, move = seat(part, guest.shape[0], modes)
        seated.append(host + pltpu.roll(jnp.where(mask, guest, 0.0), move, 1))
    return seated


def alight(hosts, modes):
    guest = jnp.zeros(hosts[0].shape, F32)
    for part, host in enumerate(hosts):
        mask, move = seat(part, guest.shape[0], modes)
        guest = jnp.where(mask, pltpu.roll(host, LANES - move, 1), guest)
    return guest


def pack_kernel(sizes, layers, partners_ref, counts_ref, pattern_ref, loads_ref, basis_ref, factors_hbm, *refs):
    rows_ref, outs = refs[0], refs[1:-7]
    partners_smem, counts_smem, pattern_smem, loads, basis, factors_ref, sems = refs[-7:]
    sources = (partners_ref, counts_ref, pattern_ref, loads_ref, basis_ref, factors_hbm)
    targets = (partners_smem, counts_smem, pattern_smem, loads, basis, factors_ref)
    for copy in fetch(list(zip(sources, targets)), sems):
        copy.wait()
    terms, modes = factors_ref.shape[1:3]
    cases = loads.shape[1]
    lane = lane_ids(8)
    row = lax.broadcasted_iota(jnp.int32, (8, LANES), 0)
    digits = jnp.zeros((8, LANES), F32)
    scalars = [partners_smem[0, b] for b in range(PLANES)]
    scalars += [counts_smem[0, b] for b in range(PLANES + 2)]
    for place, scalar in enumerate(scalars):
        digit = jnp.where(row == 0, scalar // 16, scalar % 16).astype(F32)
        digits = jnp.where(lane == place, digit, digits)
    rows_ref[:cases, :] = loads[0]
    rows_ref[cases : cases + modes, :] = basis[0]
    gap = jnp.zeros((modes, HALF - modes), F32)
    parts = []
    for term in range(terms):
        whole = factors_ref[0, term]
        high = whole.astype(BF16).astype(F32)
        parts.append(jnp.concatenate([high, gap, whole - high, gap], axis=1))
    factors = jnp.concatenate(board(parts[:-1], parts[-1], modes), axis=0).astype(BF16)
    ids = jnp.zeros((8, LANES), F32)
    for term in range(terms):
        sub = pattern_smem[0, term]
        ids = jnp.where(row == term, (sub // 16).astype(F32), ids)
        ids = jnp.where(row == terms + term, (sub % 16).astype(F32), ids)
    ids = ids.astype(BF16)
    places = layout_of(terms, modes)
    start = cases + modes
    depth = modes // 2
    rows_ref[start:, :] = jnp.zeros_like(rows_ref[start:, :])
    for group in range(2 * (terms - 1)):
        rows_ref[start : start + depth, group * LANES : (group + 1) * LANES] = factors[group * depth : (group + 1) * depth]
    rows_ref[start : start + 8, 6 * LANES : 7 * LANES] = ids
    rows_ref[start : start + 8, 7 * LANES :] = digits.astype(BF16)
    for out_ref, block in zip(outs, wanted_blocks(sizes, layers, partners_smem)):
        out_ref[places["factors"], :] = factors
        out_ref[places["ids"], :] = ids
        out_ref[places["loads"], :] = rows_ref[:cases, lanes_of(block)]
        out_ref[places["basis"], :] = rows_ref[cases:start, lanes_of(block)]


def layout_of(terms, modes):
    sizes = (("factors", (terms - 1) * modes), ("basis", modes), ("loads", 16), ("ids", 8))
    places, start = {}, 0
    for name, rows in sizes:
        places[name] = slice(start, start + rows)
        start += rows
    return places


def stage_kernel(start, dual_ref, rows_ref, dual_out, rows_out, meta_out, sems):
    copies = fetch([(dual_ref, dual_out), (rows_ref, rows_out)], sems)
    copies[1].wait()
    digits = rows_out[start : start + 8, 7 * LANES :].astype(F32)
    meta_out[...] = (digits[0:1] * 16.0 + digits[1:2]).astype(jnp.int32)
    copies[0].wait()


def basis_of(rows_ref, cases):
    return rows_ref[cases : rows_ref.shape[0] - SPARE, :]


def own_setup(dims, cases, rows_ref):
    terms, modes = dims
    start, depth = cases + modes, modes // 2
    groups = [
        rows_ref[start : start + depth, group * LANES : (group + 1) * LANES] for group in range(2 * (terms - 1))
    ]
    parts = [jnp.concatenate(groups[2 * term : 2 * term + 2], axis=0) for term in range(terms - 1)]
    return parts, rows_ref[start : start + 8, 6 * LANES : 7 * LANES]


def difference(counts_ref, mine, facing):
    result, ours, theirs = [], [], []
    for block, other in enumerate(facing):
        mask = live_mask(counts_ref, block)
        left = mine[:, block * LANES : (block + 1) * LANES].astype(F32) * mask
        right = other.astype(F32) * mask
        result.append(left - right)
        ours.append(left.astype(BF16))
        theirs.append(right.astype(BF16))
    return result, ours, theirs


def first_restrict_kernel(sizes, dims, layers, meta_ref, rows_ref, *refs):
    near_refs, (_, out_ref, message_ref, scratch_ref) = refs[: PLANES + layers], refs[PLANES + layers :]
    span = layout_of(*dims)["loads"]
    cases = out_ref.shape[0]
    for slot in range(PLANES):
        scratch_ref[slot] = near_refs[slot][span, :]
    facing = [scratch_ref[slot_of(sizes, meta_ref[0, b])] for b in range(PLANES)]
    facing += [near_refs[PLANES][span, :], near_refs[-1][span, :]]
    restrict(meta_ref, rows_ref[:cases, :], facing, basis_of(rows_ref, cases), out_ref, message_ref)


def twice(basis):
    gap = jnp.zeros((HALF - basis.shape[0], basis.shape[1]), BF16)
    return jnp.concatenate([basis, gap, basis, gap], axis=0)


def times_basis(rows, doubled):
    return lax.dot_general(rows, doubled, (((1,), (1,)), ((), ())), preferred_element_type=F32)


def fold(coefficients):
    half = coefficients.shape[0] // 2
    return jnp.where(lane_ids(half) < HALF, coefficients[:half], coefficients[half:])


def encode(sums):
    top = sums.astype(BF16).astype(F32)
    middle = (sums - top).astype(BF16).astype(F32)
    bottom = sums - top - middle
    return top + pltpu.roll(middle, 2, 1) + pltpu.roll(bottom, 4, 1)


def decode(totals):
    return totals + pltpu.roll(totals, LANES - 2, 1) + pltpu.roll(totals, LANES - 4, 1)


def restrict(meta_ref, mine, facing, basis, out_ref, message_ref):
    cases = mine.shape[0]
    result, ours, theirs = difference(meta_ref, mine, facing)
    for block, values in enumerate(result):
        out_ref[:, block * LANES : (block + 1) * LANES] = values
    both = jnp.concatenate([jnp.concatenate(ours, axis=1), jnp.concatenate(theirs, axis=1)], axis=0)
    coefficients = times_basis(both, twice(basis))
    message = fold(coefficients[:cases] - coefficients[cases:])
    message_ref[...] = jnp.broadcast_to(message[None], message_ref.shape)


def shares(sizes, dims, layers, meta_ref, applied_ref, near_refs, rows_ref, sums):
    cases = applied_ref.shape[0]
    span = layout_of(*dims)["basis"]
    masked = []
    for block in range(PLANES + 2):
        part = applied_ref[:, block * LANES : (block + 1) * LANES].astype(F32)
        masked.append((part * live_mask(meta_ref, block)).astype(BF16))
    own = fold(times_basis(jnp.concatenate(masked, axis=1), twice(basis_of(rows_ref, cases))))
    high = own.astype(BF16).astype(F32)
    tiles = []
    for near_ref, block in zip(near_refs, wanted_blocks(sizes, layers, meta_ref)):
        part = applied_ref[:, lanes_of(block)].astype(F32) * live_mask(meta_ref, block)
        tiles.append(fold(times_basis(part.astype(BF16), twice(near_ref[span, :]))))
    modes = dims[1]
    hosts = board(tiles[:3], own - high, modes) + board(tiles[3:PLANES], tiles[PLANES], modes)
    return jnp.concatenate([high + encode(sums)] + hosts + tiles[PLANES + 1 :], axis=0).astype(BF16)


def collect(sizes, dims, layers, cases, own_ref, others_ref, changes_ref):
    fine_count, coarse_count = sizes
    half = cases // 2
    coarse = lax.axis_index("coarse")

    def tile(layer, fine, index):
        rows = slice(cases + index * half, cases + (index + 1) * half)
        if layers == 1:
            source = own_ref if layer == 0 else others_ref
            return source[fine, rows, :].astype(F32)
        return others_ref[layer, fine, rows, :].astype(F32)

    def one(fine, totals):
        for layer in range(coarse_count):
            first = tile(layer, fine, 0)
            totals = totals + first
            value = first + alight([tile(layer, fine, 1 + slot) for slot in range(3)], dims[1])
            for slot in range(PLANES):
                distance = DISTANCES[slot]
                partner = jnp.where(fine % 2 == 0, fine + distance, fine - distance) if layers > 1 else (
                    fine + distance if fine % 2 == 0 else fine - distance
                )
                value = value - tile(layer, (partner + fine_count) % fine_count, 1 + slot)
            if layers == 1:
                value = value - alight([tile(1 - layer, fine, 4 + slot) for slot in range(3)], dims[1])
                place = fine * 2 + (coarse if layer == 0 else 1 - coarse)
            else:
                if layer > 0:
                    value = value - tile(layer - 1, fine, 1 + PLANES)
                if layer < coarse_count - 1:
                    value = value - alight([tile(layer + 1, fine, 4 + slot) for slot in range(3)], dims[1])
                place = fine * coarse_count + layer
            changes_ref[place] = value
        return totals

    totals = jnp.zeros((half, LANES), F32)
    if layers > 1:
        return decode(lax.fori_loop(0, fine_count, one, totals))
    for fine in range(fine_count):
        totals = one(fine, totals)
    return decode(totals)


def prepare(sizes, dims, cases, rows_ref, near_refs, picks_ref, factors_ref):
    terms, modes = dims
    places = layout_of(terms, modes)
    half = 8
    chunks = sizes[0] * sizes[1] * half // LANES
    lanes = lane_ids(half).astype(F32)
    step = lax.broadcasted_iota(jnp.int32, (half, LANES), 0).astype(F32)
    gap = jnp.zeros((HALF - modes, LANES), BF16)
    setups = [own_setup(dims, cases, rows_ref)]
    for near_ref in near_refs:
        parts = [near_ref[term * modes : (term + 1) * modes, :] for term in range(terms - 1)]
        setups.append((parts, near_ref[places["ids"], :]))
    for index, (packed, ids) in enumerate(setups):
        ids = ids.astype(F32)
        ids = (ids[:terms] * 16.0 + ids[terms : 2 * terms]) * float(half)
        picks = []
        for term in range(terms):
            target = ids[term : term + 1] + step
            picks.append(
                jnp.concatenate([(target == lanes + float(LANES * c)).astype(F32) for c in range(chunks)], axis=1)
            )
        rows = terms * half
        picks_ref[index * rows : (index + 1) * rows, :] = jnp.concatenate(picks, axis=0).astype(BF16)
        packed = packed + [alight([part.astype(F32) for part in packed], modes).astype(BF16)]
        for term, part in enumerate(packed):
            factors_ref[index, term * HALF : term * HALF + modes, :] = part
            factors_ref[index, term * HALF + modes : (term + 1) * HALF, :] = gap


def solve(coeffs, dims, picks_ref, factors_ref):
    terms, modes = dims
    half = 8
    high = coeffs.astype(BF16)
    low = (coeffs - high.astype(F32)).astype(BF16)
    picked = dot(picks_ref[...], jnp.concatenate([high, low], axis=1))
    left = lane_ids(half) < HALF
    solutions = []
    for index in range(factors_ref.shape[0]):
        sides = []
        for part in range(2):
            columns = []
            for pair in range(0, terms, 2):
                first, second = [
                    picked[(index * terms + term) * half : (index * terms + term + 1) * half, part * LANES : (part + 1) * LANES]
                    for term in (pair, pair + 1)
                ]
                top = jnp.where(left, first, pltpu.roll(second, HALF, 1))
                bottom = jnp.where(left, pltpu.roll(first, HALF, 1), second)
                columns.append(jnp.concatenate([top, bottom], axis=0))
            sides.append(jnp.concatenate(columns, axis=1))
        rows = jnp.concatenate(sides, axis=0).astype(BF16)
        product = dot(rows, factors_ref[index])
        product = product[: 2 * half] + product[2 * half :]
        product = product + pltpu.roll(product, HALF, 1)
        solutions.append(product[:, :modes].astype(BF16))
    return solutions


def advance(sizes, dims, meta_ref, coeffs, residual, near_refs, picks_ref, factors_ref, rows_ref, dual_ref, theirs_ref,
            direction_ref, applied_ref):
    span = layout_of(*dims)["basis"]
    solutions = solve(coeffs, dims, picks_ref, factors_ref)
    mine = dot(solutions[0], basis_of(rows_ref, residual.shape[0])).astype(BF16).astype(F32)
    for index, near_ref in enumerate(near_refs):
        theirs_ref[index] = dot(solutions[index + 1], near_ref[span, :]).astype(BF16).astype(F32)
    pieces = []
    for block in range(PLANES + 2):
        if block < PLANES:
            place = slot_of(sizes, meta_ref[0, block])
        else:
            place = min(block, len(near_refs) - 1)
        here = slice(block * LANES, (block + 1) * LANES)
        pieces.append(residual[:, here] + live_mask(meta_ref, block) * (mine[:, here] - theirs_ref[place]))
    direction = jnp.concatenate(pieces, axis=1)
    direction_ref[...] = direction
    applied = dot(direction.astype(BF16), dual_ref[0]).astype(BF16)
    applied_ref[...] = applied
    gamma = jnp.sum(residual * direction, axis=1, keepdims=True)
    delta = 2.0 * jnp.sum(direction * applied.astype(F32), axis=1, keepdims=True)
    half = gamma.shape[0] // 2
    lanes = lane_ids(half)
    sums = jnp.zeros((half, LANES), F32)
    for lane, values in ((GAMMA, gamma), (DELTA, delta)):
        sums = jnp.where(lanes == lane, values[:half], sums)
        sums = jnp.where(lanes == HALF + lane, values[half:], sums)
    return applied, sums


def first_kernel(sizes, dims, layers, count, meta_ref, coeffs_ref, residual_ref, rows_ref, dual_ref, *refs):
    near_refs = refs[:count]
    message_ref, direction_ref, applied_ref, picks_ref, factors_ref, theirs_ref = refs[count:]
    prepare(sizes, dims, residual_ref.shape[0], rows_ref, near_refs, picks_ref, factors_ref)
    applied, sums = advance(
        sizes, dims, meta_ref, coeffs_ref[...], residual_ref[...], near_refs, picks_ref, factors_ref, rows_ref, dual_ref,
        theirs_ref, direction_ref, applied_ref,
    )
    cases = applied.shape[0]
    tiles = shares(sizes, dims, layers, meta_ref, applied_ref, near_refs, rows_ref, sums)
    message_ref[:, :cases, :] = jnp.zeros((message_ref.shape[0], cases, LANES), BF16)
    message_ref[:, cases:, :] = jnp.broadcast_to(tiles[None], (message_ref.shape[0],) + tiles.shape)
    post_blocks(message_ref, [meta_ref[0, b] for b in range(PLANES)], applied)
    if layers == 1:
        block = wanted_blocks(sizes, layers, meta_ref)[-1]
        message_ref[lax.axis_index("fine"), :cases, :] = applied_ref[:, lanes_of(block)]


def steps_from(totals):
    low = totals[:, GAMMA : GAMMA + 1] / totals[:, DELTA : DELTA + 1]
    high = totals[:, HALF + GAMMA : HALF + GAMMA + 1] / totals[:, HALF + DELTA : HALF + DELTA + 1]
    return low, high


def second_kernel(sizes, dims, layers, count, meta_ref, coeffs_ref, residual_ref, before_ref, applied_before_ref,
                  picks_ref, factors_ref, rows_ref, dual_ref, own_ref, *refs):
    others_refs, refs = refs[: 1 if layers == 1 else 3], refs[1 if layers == 1 else 3 :]
    near_refs = refs[:count]
    message_ref, residual_out, multipliers_out, direction_ref, applied_ref, theirs_ref, changes_ref = refs[count:]
    cases = residual_ref.shape[0]
    half = cases // 2
    low, high = steps_from(collect(sizes, dims, layers, cases, own_ref, others_refs[0], changes_ref))
    step = jnp.concatenate([low, high], axis=0)
    packed_step = jnp.where(lane_ids(half) < HALF, low, high)
    coeffs = coeffs_ref[...] - (changes_ref[...] * packed_step[None]).reshape(coeffs_ref.shape)
    facing = [own_ref[meta_ref[0, b], :cases, :] for b in range(PLANES)]
    if layers == 1:
        facing += [others_refs[0][lax.axis_index("fine"), :cases, :]] * 2
    else:
        facing += [ref[...] for ref in others_refs[1:]]
    image, _, _ = difference(meta_ref, applied_before_ref[...], facing)
    residual = residual_ref[...] - step * jnp.concatenate(image, axis=1)
    residual_out[...] = residual
    multipliers_out[...] = step * before_ref[...]
    applied, sums = advance(
        sizes, dims, meta_ref, coeffs, residual, near_refs, picks_ref, factors_ref, rows_ref, dual_ref, theirs_ref,
        direction_ref, applied_ref,
    )
    message_ref[:, :cases, :] = jnp.zeros((message_ref.shape[0], cases, LANES), BF16)
    message_ref[:, cases:, :] = jnp.broadcast_to(encode(sums).astype(BF16)[None], (message_ref.shape[0], half, LANES))
    post_blocks(message_ref, facing_subs(sizes, meta_ref), applied)


def last_kernel(sizes, meta_ref, arrived_ref, applied_ref, residual_ref, multipliers_ref, direction_ref,
                multipliers_out, residual_out):
    cases = applied_ref.shape[0]
    totals = jnp.sum(arrived_ref[:, cases:, :].astype(F32), axis=0)
    step = jnp.concatenate(steps_from(decode(totals)), axis=0)
    facing = [arrived_ref[target, :cases, :] for target in facing_subs(sizes, meta_ref)]
    image, _, _ = difference(meta_ref, applied_ref[...], facing)
    fine = lax.axis_index("fine")
    for block in range(PLANES + 2):
        span = slice(block * LANES, (block + 1) * LANES)
        if block < PLANES:
            sign = jnp.where(fine < meta_ref[0, block], 1.0, -1.0).astype(F32)
        else:
            sign = -1.0 if block == PLANES else 1.0
        multipliers_out[0, :, span] = sign * (multipliers_ref[:, span] + step * direction_ref[:, span])
        residual_out[0, :, span] = sign * (residual_ref[:, span] - step * image[block])


SMEM = pl.BlockSpec(memory_space=pltpu.SMEM)
VMEM = pl.BlockSpec(memory_space=pltpu.VMEM)


HBM = pl.BlockSpec(memory_space=pltpu.HBM)
ANY = pl.BlockSpec(memory_space=pl.ANY)


def call(kernel, name, scalars, arrays, outs, scratch=(), far=(), after=(), vmem=40):
    return pl.pallas_call(
        kernel,
        name=name,
        out_shape=[jax.ShapeDtypeStruct(shape, dtype) for shape, dtype in outs],
        in_specs=[SMEM] * len(scalars) + [VMEM] * len(arrays) + [HBM] * len(far) + [ANY] * len(after),
        out_specs=[VMEM] * len(outs),
        scratch_shapes=list(scratch),
        compiler_params=pltpu.CompilerParams(vmem_limit_bytes=vmem * 1024 * 1024),
    )(*scalars, *arrays, *far, *after)


def body(load_cases, dual_ops, coarse_basis, factor_blocks, pattern, partners, row_counts):
    cases, width = load_cases.shape[1:]
    terms, modes = factor_blocks.shape[1:3]
    fine_count = lax.axis_size("fine")
    coarse_count = lax.axis_size("coarse")
    subs = fine_count * coarse_count
    sizes = (fine_count, coarse_count)
    dims = (terms, modes)
    half = cases // 2
    layers = 1 if coarse_count == 2 else 2

    def swap_all(message):
        return lax.all_to_all(message, AXES, 0, 0, tiled=True)

    def swap_slot(message, slot):
        distance = DISTANCES[slot]
        pairs = [(i, (i + distance if i % 2 == 0 else i - distance) % fine_count) for i in range(fine_count)]
        return lax.ppermute(message, "fine", pairs)

    def swap_blocks(messages):
        received = [swap_slot(messages[slot], slot) for slot in range(PLANES)]
        if layers == 1:
            return received + [lax.ppermute(messages[PLANES], "coarse", [(0, 1), (1, 0)])]
        up = [(i, i + 1) for i in range(coarse_count - 1)]
        lower = lax.ppermute(messages[PLANES + 1], "coarse", up)
        return received + [lower, lax.ppermute(messages[PLANES], "coarse", [(j, i) for i, j in up])]

    full = ((cases, width), F32)
    half_full = ((cases, width), BF16)
    coded = ((subs, half, LANES), F32)
    dma = pltpu.SemaphoreType.DMA

    inputs = (partners, row_counts, pattern, load_cases, coarse_basis, factor_blocks)
    spaces = (pltpu.SMEM,) * 3 + (pltpu.VMEM,) * 3
    rows, *packed = call(
        functools.partial(pack_kernel, sizes, layers),
        "pack_setup",
        (),
        (),
        [((cases + modes + SPARE, width), BF16)]
        + [((layout_of(terms, modes)["ids"].stop, LANES), BF16)] * (PLANES + layers),
        [space(array.shape, array.dtype) for space, array in zip(spaces, inputs)] + [dma((6,))],
        inputs,
        vmem=60,
    )
    received = swap_blocks(packed)
    dual, rows, meta = call(
        functools.partial(stage_kernel, cases + modes),
        "stage_operands",
        (),
        (),
        [(dual_ops.shape, BF16), (rows.shape, BF16), ((1, LANES), jnp.int32)],
        [dma((2,))],
        (dual_ops, rows),
    )
    count = len(received)
    theirs = [pltpu.VMEM((count, cases, LANES), F32)]

    residual, message = call(
        functools.partial(first_restrict_kernel, sizes, dims, layers),
        "restrict_residual",
        (meta,),
        (rows, *received),
        [full, coded],
        [pltpu.VMEM((PLANES, cases, LANES), BF16)],
        after=(dual,),
    )
    coeffs = swap_all(message).reshape(subs * half, LANES)

    tiles = PLANES + layers
    message, direction, applied, picks, factors = call(
        functools.partial(first_kernel, sizes, dims, layers, count),
        "first_direction",
        (meta,),
        (coeffs, residual, rows, dual, *received),
        [((fine_count, cases + tiles * half, LANES), BF16), full, half_full, (((count + 1) * terms * half, subs * half), BF16),
         ((count + 1, terms * HALF, LANES), BF16)],
        theirs,
    )
    own = lax.all_to_all(message, "fine", 0, 0, tiled=True)
    if layers == 1:
        others = [lax.ppermute(own, "coarse", [(0, 1), (1, 0)])]
    else:
        up = [(i, i + 1) for i in range(coarse_count - 1)]
        lower = lax.ppermute(applied[:, (PLANES + 1) * LANES :], "coarse", up)
        upper = lax.ppermute(applied[:, PLANES * LANES : (PLANES + 1) * LANES], "coarse", [(j, i) for i, j in up])
        others = [lax.all_gather(own, "coarse"), lower, upper]

    message, residual, multipliers, direction, applied = call(
        functools.partial(second_kernel, sizes, dims, layers, count),
        "second_direction",
        (meta,),
        (coeffs, residual, direction, applied, picks, factors, rows, dual, own, *others, *received),
        [((subs, cases + half, LANES), BF16), full, full, full, half_full],
        theirs + [pltpu.VMEM((subs, half, LANES), F32)],
    )
    arrived = swap_all(message)
    out = ((1, cases, width), F32)
    multipliers, residual = call(
        functools.partial(last_kernel, sizes),
        "finish",
        (meta,),
        (arrived, applied, residual, multipliers, direction),
        [out, out],
    )
    return multipliers, residual


def solution(mesh):
    rows = P(AXES, None, None)
    return jax.shard_map(
        body,
        mesh=mesh,
        in_specs=(rows, rows, rows, P(AXES, None, None, None), P(AXES, None), P(AXES, None), P(AXES, None)),
        out_specs=(rows, rows),
        check_vma=False,
    )
```
